32 devices in a mesh: dp: 2 (over x), ctx: 4 (over z), exp: 4 (over y, core).
Axes of the slice: x: 2, y: 2, z: 4, core: 2. Of those that a mesh axis runs over, the one named last changes fastest.
Arguments:
- tokens: bfloat16 [2, 4, 2048, 1536], P('dp', 'exp', 'ctx'), may hold values from -6 to 6
- cotangent: bfloat16 [2, 4, 2048, 1536], P('dp', 'exp', 'ctx'), may hold values from -6 to 6
- doc_starts: int32 [2, 4, 9], P('dp', 'exp'), may hold values from 0 to 2047, as said below
- routes: int32 [2, 4, 2048, 8], P('dp', 'exp', 'ctx'), may hold values from 0 to 15, all different within a row
- priority: int32 [2, 4, 4, 4096], P('dp', 'exp', 'ctx'), may hold values from 0 to 4095, each once within a row
- attend_master: float32 [1536, 2560], P(('dp', 'ctx', 'exp')), may hold values from -0.15625 to 0.15625
- attend_mean: float32 [1536, 2560], P(('dp', 'ctx', 'exp')), may hold values from -56 to 56
- attend_square: float32 [1536, 2560], P(('dp', 'ctx', 'exp')), may hold values from 409.6 to 1638.4
- outward_master: float32 [1536, 1536], P(None, ('dp', 'ctx', 'exp')), may hold values from -0.625 to 0.625
- outward_mean: float32 [1536, 1536], P(None, ('dp', 'ctx', 'exp')), may hold values from -14 to 14
- outward_square: float32 [1536, 1536], P(None, ('dp', 'ctx', 'exp')), may hold values from 24.576 to 98.304
- router_master: float32 [1536, 16], P(('dp', 'ctx', 'exp')), may hold values from -0.078125 to 0.078125
- router_mean: float32 [1536, 16], P(('dp', 'ctx', 'exp')), may hold values from -896 to 896
- router_square: float32 [1536, 16], P(('dp', 'ctx', 'exp')), may hold values from 98304 to 409600
- gains_master: float32 [2, 1536], P(None, ('dp', 'ctx', 'exp')), may hold values from 0.5 to 1.5
- gains_mean: float32 [2, 1536], P(None, ('dp', 'ctx', 'exp')), may hold values from -80 to 80
- gains_square: float32 [2, 1536], P(None, ('dp', 'ctx', 'exp')), may hold values from 655.36 to 2621.44
- expand_master: float32 [16, 1536, 1024], P('exp', ('dp', 'ctx')), may hold values from -0.15625 to 0.15625
- expand_mean: float32 [16, 1536, 1024], P('exp', ('dp', 'ctx')), may hold values from -40 to 40
- expand_square: float32 [16, 1536, 1024], P('exp', ('dp', 'ctx')), may hold values from 212.992 to 819.2
- shrink_master: float32 [16, 512, 1536], P('exp', ('dp', 'ctx')), may hold values from -1.5 to 1.5
- shrink_mean: float32 [16, 512, 1536], P('exp', ('dp', 'ctx')), may hold values from -4 to 4
- shrink_square: float32 [16, 512, 1536], P('exp', ('dp', 'ctx')), may hold values from 2.4576 to 9.8304
Outputs:
- output: bfloat16 [2, 4, 2048, 1536], P('dp', 'exp', 'ctx')
- input_grad: float32 [2, 4, 2048, 1536], P('dp', 'exp', 'ctx')
- attend_averaged: float32 [1536, 2560], P(('dp', 'ctx', 'exp'))
- attend_squares: float32 [1536, 2560], P(('dp', 'ctx', 'exp'))
- attend_updated: float32 [1536, 2560], P(('dp', 'ctx', 'exp'))
- attend_copy: bfloat16 [1536, 2560], P(('dp', 'ctx', 'exp'))
- outward_averaged: float32 [1536, 1536], P(None, ('dp', 'ctx', 'exp'))
- outward_squares: float32 [1536, 1536], P(None, ('dp', 'ctx', 'exp'))
- outward_updated: float32 [1536, 1536], P(None, ('dp', 'ctx', 'exp'))
- outward_copy: bfloat16 [1536, 1536], P(None, ('dp', 'ctx', 'exp'))
- router_averaged: float32 [1536, 16], P(('dp', 'ctx', 'exp'))
- router_squares: float32 [1536, 16], P(('dp', 'ctx', 'exp'))
- router_updated: float32 [1536, 16], P(('dp', 'ctx', 'exp'))
- router_copy: bfloat16 [1536, 16], P(('dp', 'ctx', 'exp'))
- gains_averaged: float32 [2, 1536], P(None, ('dp', 'ctx', 'exp'))
- gains_squares: float32 [2, 1536], P(None, ('dp', 'ctx', 'exp'))
- gains_updated: float32 [2, 1536], P(None, ('dp', 'ctx', 'exp'))
- gains_copy: bfloat16 [2, 1536], P(None, ('dp', 'ctx', 'exp'))
- expand_averaged: float32 [16, 1536, 1024], P('exp', ('dp', 'ctx'))
- expand_squares: float32 [16, 1536, 1024], P('exp', ('dp', 'ctx'))
- expand_updated: float32 [16, 1536, 1024], P('exp', ('dp', 'ctx'))
- expand_copy: bfloat16 [16, 1536, 1024], P('exp', ('dp', 'ctx'))
- shrink_averaged: float32 [16, 512, 1536], P('exp', ('dp', 'ctx'))
- shrink_squares: float32 [16, 512, 1536], P('exp', ('dp', 'ctx'))
- shrink_updated: float32 [16, 512, 1536], P('exp', ('dp', 'ctx'))
- shrink_copy: bfloat16 [16, 512, 1536], P('exp', ('dp', 'ctx'))
The draws below stay inside these ranges and needn't reach their ends.
Inputs may be any that keep to these rules, and one draw needn't show every extreme that they name: `doc_starts`: each stream's starts rise strictly from 0; one of its documents runs from rows of the first device along ctx to rows of the last. `priority`: each device's routed rows are ranked once each.
All inputs are finite; a program needn't handle non-finite values.
Results may differ from the reference program's by a relative error of at most 0.019.
Values may be sent and summed in bfloat16 or wider, within the bound.
A program may use at most 384 MiB of HBM per device.

```python
import math
import jax
import jax.numpy as jnp
from jax import lax

D = 1536
HEADS = 24
KVH = 8
HD = 64
FF = 512
TOP = 8
DOCS = 9
STEP = 10
DPG = 2
EXG = 4
CTXG = 4
EXPERTS = 16
STREAM = 2048
TOK_DEV = 512
CAP = 288
QKV = 2560
TOKENS = 16384


def draw_doc_starts(key, part):
    streams = DPG * EXG
    keys_list = jax.random.split(key, 4)
    head_len = jax.random.randint(keys_list[0], (streams, 1), TOK_DEV // 2, TOK_DEV)
    tail_len = jax.random.randint(keys_list[1], (streams, 1), TOK_DEV // 2, TOK_DEV)
    steps_index = jnp.arange(1, 4, dtype=jnp.int32)[None, :]
    head_step = head_len // 4
    tail_step = tail_len // 4
    front_starts = steps_index * head_step + jax.random.randint(keys_list[2], (streams, 3), 0, 1 << 20) % head_step
    back_starts = STREAM - tail_len + steps_index * tail_step + jax.random.randint(keys_list[3], (streams, 3), 0, 1 << 20) % tail_step
    zero_col = jnp.zeros((streams, 1), jnp.int32)
    starts = jnp.concatenate([zero_col, front_starts, head_len, STREAM - tail_len, back_starts], axis=1)
    return starts.reshape(DPG, EXG, DOCS).astype(jnp.int32)


def shard_levels(own_key, shape, shards, smallest, high):
    level = 1.0
    for position, shards_of in shards:
        heights = jax.random.uniform(jax.random.fold_in(jax.random.fold_in(own_key, 6), position), (shards_of,), jnp.float32, smallest / len(shards), high / len(shards))
        level = level * jnp.repeat(jnp.exp(heights), shape[position] // shards_of).reshape((-1,) + (1,) * (len(shape) - 1 - position))
    return level


def choose_distinct(stream_key, rows, number_of, top, lift):
    ranking = jax.random.permutation(jax.random.fold_in(stream_key, 1), number_of)
    pull = ranking
    for power in range(3):
        pull = pull * pull // number_of
    pull = pull * lift // number_of
    lots = jax.random.randint(jax.random.fold_in(stream_key, 2), (rows, number_of), 0, 4096) + pull
    fixed_rows = jax.random.permutation(jax.random.fold_in(stream_key, 3), rows)[jnp.arange(number_of) % rows]
    lots = jnp.where(jnp.arange(rows)[:, None] == fixed_rows[None, :], 1 << 14, lots)
    merit = lots * number_of + jnp.arange(number_of)
    return lax.top_k(merit.astype(jnp.int32), top)[1].astype(jnp.int32)


def normal_values(stream_key, extent, scale, reach, cuts=(), kind=jnp.bfloat16):
    entries = jax.random.normal(stream_key, extent, jnp.float32) * scale
    if len(cuts) > 0:
        entries = shard_levels(stream_key, extent, cuts, -0.22, 0.18) * entries
    return jnp.clip(entries, min=-reach, max=reach).astype(kind)


def setup_inputs(seed: int = 0) -> dict:
    streams_of = jax.random.split(jax.random.key(seed), 24)
    tokens = normal_values(streams_of[0], (DPG, EXG, STREAM, D), 1.0, 6.0, ((0, 2), (1, 4), (2, 4)))
    cotangent = normal_values(streams_of[1], (DPG, EXG, STREAM, D), 1.0, 6.0, ((0, 2), (1, 4), (2, 4)))
    doc_starts = draw_doc_starts(jax.random.fold_in(streams_of[23], 71), 0)
    routes = choose_distinct(streams_of[3], DPG * EXG * STREAM, EXPERTS, TOP, 4096).reshape((DPG, EXG, STREAM, TOP))
    priority = jax.vmap(lambda own: jax.random.permutation(own, TOK_DEV * TOP))(jax.random.split(streams_of[4], DPG * EXG * CTXG)).reshape((DPG, EXG, CTXG, TOK_DEV * TOP)).astype(jnp.int32)
    attend_master = normal_values(streams_of[5], (D, QKV), D ** -0.5, 0.15625, ((0, 32),), jnp.float32)
    attend_mean = normal_values(streams_of[6], (D, QKV), (0.075 * TOKENS ** 0.5), 56.0, ((0, 32),), jnp.float32)
    attend_square = jnp.clip(jnp.exp(math.log(1638.4) - 1.3862944 * jax.random.uniform(streams_of[7], (D, QKV), jnp.float32) ** shard_levels(streams_of[7], (D, QKV), ((0, 32),), -0.2, 0.2)), 409.6, 1638.4)
    outward_master = normal_values(streams_of[8], (HEADS * HD, D), (D // 16) ** -0.5, 0.625, ((1, 32),), jnp.float32)
    outward_mean = normal_values(streams_of[9], (HEADS * HD, D), (0.018 * TOKENS ** 0.5), 14.0, ((1, 32),), jnp.float32)
    outward_square = jnp.clip(jnp.exp(math.log(98.304) - 1.3862944 * jax.random.uniform(streams_of[10], (HEADS * HD, D), jnp.float32) ** shard_levels(streams_of[10], (HEADS * HD, D), ((1, 32),), -0.2, 0.2)), 24.576, 98.304)
    router_master = normal_values(streams_of[11], (D, EXPERTS), (4 * D) ** -0.5, 0.078125, ((0, 32),), jnp.float32)
    router_mean = normal_values(streams_of[12], (D, EXPERTS), (1.2 * TOKENS ** 0.5), 896.0, ((0, 32),), jnp.float32)
    router_square = jnp.clip(jnp.exp(math.log(409600.0) - 1.4271164 * jax.random.uniform(streams_of[13], (D, EXPERTS), jnp.float32) ** shard_levels(streams_of[13], (D, EXPERTS), ((0, 32),), -0.2, 0.2)), 98304.0, 409600.0)
    gains_master = jnp.clip(1.0 + 0.1 * jax.random.normal(streams_of[14], (2, D), jnp.float32), 0.5, 1.5)
    gains_mean = normal_values(streams_of[15], (2, D), (0.1 * TOKENS ** 0.5), 80.0, ((1, 32),), jnp.float32)
    gains_square = jnp.clip(jnp.exp(math.log(2621.44) - 1.3862944 * jax.random.uniform(streams_of[16], (2, D), jnp.float32) ** shard_levels(streams_of[16], (2, D), ((1, 32),), -0.2, 0.2)), 655.36, 2621.44)
    expand_master = normal_values(streams_of[17], (EXPERTS, D, 2 * FF), D ** -0.5, 0.15625, ((0, 4), (1, 8)), jnp.float32)
    expand_mean = normal_values(streams_of[18], (EXPERTS, D, 2 * FF), (0.05 * TOKENS ** 0.5), 40.0, ((0, 4), (1, 8)), jnp.float32)
    expand_square = jnp.clip(jnp.exp(math.log(819.2) - 1.34707364 * jax.random.uniform(streams_of[19], (EXPERTS, D, 2 * FF), jnp.float32) ** shard_levels(streams_of[19], (EXPERTS, D, 2 * FF), ((0, 4), (1, 8)), -0.2, 0.2)), 212.992, 819.2)
    shrink_master = normal_values(streams_of[20], (EXPERTS, FF, D), (FF // 32) ** -0.5, 1.5, ((0, 4), (1, 8)), jnp.float32)
    shrink_mean = normal_values(streams_of[21], (EXPERTS, FF, D), (0.0056 * TOKENS ** 0.5), 4.0, ((0, 4), (1, 8)), jnp.float32)
    shrink_square = jnp.clip(jnp.exp(math.log(9.8304) - 1.3862944 * jax.random.uniform(streams_of[22], (EXPERTS, FF, D), jnp.float32) ** shard_levels(streams_of[22], (EXPERTS, FF, D), ((0, 4), (1, 8)), -0.2, 0.2)), 2.4576, 9.8304)
    return {"tokens": tokens, "cotangent": cotangent, "doc_starts": doc_starts, "routes": routes, "priority": priority, "attend_master": attend_master, "attend_mean": attend_mean, "attend_square": attend_square, "outward_master": outward_master, "outward_mean": outward_mean, "outward_square": outward_square, "router_master": router_master, "router_mean": router_mean, "router_square": router_square, "gains_master": gains_master, "gains_mean": gains_mean, "gains_square": gains_square, "expand_master": expand_master, "expand_mean": expand_mean, "expand_square": expand_square, "shrink_master": shrink_master, "shrink_mean": shrink_mean, "shrink_square": shrink_square}


EPSILON = 1e-05
THETA = 10000.0
BETA_ONE = 0.9
BETA_TWO = 0.95
ADAM_EPSILON = 1e-08
DECAY = 0.1
NEGATIVE = -1e+30
HIGHEST = lax.Precision.HIGHEST

@jax.custom_vjp
def low(v):
    return lax.optimization_barrier(v.astype(jnp.bfloat16)).astype(jnp.float32)

@jax.custom_vjp
def low_back(v):
    return v

def low_keep(v):
    return (low(v), None)

def low_pass(kept, grad):
    return (grad,)

def back_keep(v):
    return (v, None)

def back_low(kept, grad):
    return (low(grad),)
low.defvjp(low_keep, low_pass)
low_back.defvjp(back_keep, back_low)

def rms_norm(values, gain_vec):
    return values * lax.rsqrt(lax.optimization_barrier(jnp.mean(values * values, axis=-1, keepdims=True)) + EPSILON) * gain_vec

def rotate_heads(values, positions):
    half_dim = values.shape[-1] // 2
    frequency = THETA ** (-jnp.arange(half_dim, dtype=jnp.float32) / half_dim)
    angles = positions.astype(jnp.float32)[:, None] * frequency[None, :]
    cosine = jnp.cos(angles)[:, None, :]
    sine_part = jnp.sin(angles)[:, None, :]
    lead_part = values[..., :half_dim]
    tail_part = values[..., half_dim:]
    return jnp.concatenate([lead_part * cosine - tail_part * sine_part, lead_part * sine_part + tail_part * cosine], axis=-1)

def attention(queries, keys, values, documents):
    block_rows = math.gcd(STREAM, 512)
    score_scale = HD ** (-0.5)
    positions = jnp.arange(STREAM, dtype=jnp.int32)

    def one_block(block_id):
        offset = block_id * block_rows
        query_blk = lax.dynamic_slice_in_dim(queries, offset, block_rows, 0)
        query_pos = offset + jnp.arange(block_rows, dtype=jnp.int32)
        query_doc = lax.dynamic_slice_in_dim(documents, offset, block_rows, 0)
        scores = low_back(jnp.einsum('qgrd,kgd->grqk', query_blk, keys, precision=HIGHEST) * score_scale)
        allowed = (positions[None, :] <= query_pos[:, None]) & (documents[None, :] == query_doc[:, None])
        masked = jnp.where(allowed, scores, NEGATIVE)
        row_max = lax.optimization_barrier(jnp.max(masked, axis=-1, keepdims=True))
        weights = jnp.where(allowed, jnp.exp(masked - row_max), 0.0)
        probs = low(weights / lax.optimization_barrier(jnp.sum(weights, axis=-1, keepdims=True)))
        return jnp.einsum('grqk,kgd->qgrd', probs, values, precision=HIGHEST)
    result = lax.map(jax.checkpoint(one_block), jnp.arange(STREAM // block_rows, dtype=jnp.int32))
    return result.reshape(queries.shape)

def slot_table(route_block, priority_row):
    flat_ids = route_block.reshape(-1)
    row_count = flat_ids.shape[0]
    ranked_rows = jnp.zeros((row_count,), jnp.int32).at[priority_row].set(jnp.arange(row_count, dtype=jnp.int32))
    ranked_ids = flat_ids[ranked_rows]
    matches = (ranked_ids[:, None] == jnp.arange(EXPERTS, dtype=jnp.int32)[None, :]).astype(jnp.int32)
    earlier = lax.optimization_barrier(jnp.sum((jnp.cumsum(matches, axis=0) - matches) * matches, axis=1))
    slot_rank = earlier[priority_row]
    return jnp.where(slot_rank < CAP, flat_ids * CAP + slot_rank, EXPERTS * CAP).astype(jnp.int32)

def forward(tokens_in, weights, documents, route_ids, targets):
    attend, outward, router, gains, expand, shrink = weights
    positions = jnp.arange(STREAM, dtype=jnp.int32)
    normed = low(rms_norm(tokens_in, gains[0]))
    project = low_back(jnp.dot(normed, attend, precision=HIGHEST))
    queries = project[:, :HEADS * HD].reshape(STREAM, HEADS, HD)
    keys = project[:, HEADS * HD:(HEADS + KVH) * HD].reshape(STREAM, KVH, HD)
    values = project[:, (HEADS + KVH) * HD:].reshape(STREAM, KVH, HD)
    queries = low(rotate_heads(queries, positions)).reshape(STREAM, KVH, HEADS // KVH, HD)
    keys = low(rotate_heads(keys, positions))
    values = low(values)
    mixed = attention(queries, keys, values, documents).reshape(STREAM, HEADS * HD)
    mixed = low(low_back(mixed))
    branch = low_back(jnp.dot(mixed, outward, precision=HIGHEST))
    middle = tokens_in + branch
    second = low(rms_norm(middle, gains[1]))
    logits = low_back(jnp.dot(second, router, precision=HIGHEST))
    choose = (route_ids[:, :, None] == jnp.arange(EXPERTS, dtype=jnp.int32)[None, None, :]).astype(jnp.float32)
    chosen = jnp.einsum('tke,te->tk', choose, logits, precision=HIGHEST)
    gates = jax.nn.softmax(chosen, axis=-1)
    blocks = second.reshape(CTXG, TOK_DEV, D)

    def dispatch(block_rows, target):
        spread = jnp.repeat(block_rows, TOP, axis=0)
        buffer = jnp.zeros((EXPERTS * CAP + 1, D), jnp.float32).at[target].add(spread)
        return buffer[:EXPERTS * CAP].reshape(EXPERTS, CAP, D)
    buffers = low_back(jax.vmap(dispatch)(blocks, targets))
    gate_up = low_back(jnp.einsum('becd,edf->becf', buffers, expand, precision=HIGHEST))
    hidden = low(jax.nn.silu(gate_up[..., :FF]) * gate_up[..., FF:])
    returned = low(low_back(jnp.einsum('becf,efd->becd', hidden, shrink, precision=HIGHEST)))

    def collect(result_block, target):
        flat = jnp.concatenate([result_block.reshape(EXPERTS * CAP, D), jnp.zeros((1, D), jnp.float32)], axis=0)
        return flat[target]
    picked = jax.vmap(collect)(returned, targets).reshape(STREAM, TOP, D)
    mixture = jnp.einsum('tk,tkd->td', gates, picked, precision=HIGHEST)
    return middle + mixture

def adam_update(master, first_mom, second_mom, grad, rate, decay):
    first_new = BETA_ONE * first_mom + (1.0 - BETA_ONE) * grad
    second_new = BETA_TWO * second_mom + (1.0 - BETA_TWO) * grad * grad
    first_hat = first_new / (1.0 - BETA_ONE ** STEP)
    second_hat = second_new / (1.0 - BETA_TWO ** STEP)
    master_new = master - rate * (first_hat / (jnp.sqrt(second_hat) + ADAM_EPSILON) + decay * master)
    return (first_new, second_new, master_new, master_new.astype(jnp.bfloat16))

def reference(tokens, cotangent, doc_starts, routes, priority, attend_master, attend_mean, attend_square, outward_master, outward_mean, outward_square, router_master, router_mean, router_square, gains_master, gains_mean, gains_square, expand_master, expand_mean, expand_square, shrink_master, shrink_mean, shrink_square):
    masters = (attend_master, outward_master, router_master, gains_master, expand_master, shrink_master)
    copies = tuple((weight.astype(jnp.bfloat16).astype(jnp.float32) for weight in masters))
    streams = DPG * EXG
    flat_tokens = tokens.reshape(streams, STREAM, D).astype(jnp.float32)
    flat_cot = cotangent.reshape(streams, STREAM, D).astype(jnp.float32)
    flat_starts = doc_starts.reshape(streams, DOCS)
    flat_routes = routes.reshape(streams, STREAM, TOP)
    flat_priority = priority.reshape(streams, CTXG, TOK_DEV * TOP)

    def one_stream(totals, inputs):
        stream_tokens, stream_cot, starts, route_ids, priority_rows = inputs
        positions = jnp.arange(STREAM, dtype=jnp.int32)
        documents = (lax.optimization_barrier(jnp.sum((starts[None, :] <= positions[:, None]).astype(jnp.int32), axis=1)) - 1).astype(jnp.int32)
        targets = jax.vmap(slot_table)(route_ids.reshape(CTXG, TOK_DEV, TOP), priority_rows)

        def apply_layer(values, weights):
            return forward(values, weights, documents, route_ids, targets)
        result, pullback = jax.vjp(apply_layer, stream_tokens, copies)
        grad_in, grad_weights = pullback(stream_cot)
        totals = tuple((left + right for left, right in zip(totals, grad_weights)))
        return (totals, (result.astype(jnp.bfloat16), grad_in))
    zero_grads = tuple((jnp.zeros_like(weight) for weight in copies))
    totals, (results, grads_in) = lax.scan(one_stream, zero_grads, (flat_tokens, flat_cot, flat_starts, flat_routes, flat_priority))
    output = results.reshape(DPG, EXG, STREAM, D)
    input_grad = grads_in.reshape(DPG, EXG, STREAM, D)
    attend_new = adam_update(attend_master, attend_mean, attend_square, totals[0], D ** (-0.5), DECAY)
    outward_new = adam_update(outward_master, outward_mean, outward_square, totals[1], 4.0 * D ** (-0.5), DECAY)
    router_new = adam_update(router_master, router_mean, router_square, totals[2], 0.5 * D ** (-0.5), DECAY)
    gains_new = adam_update(gains_master, gains_mean, gains_square, totals[3], 0.6, 0.0)
    expand_new = adam_update(expand_master, expand_mean, expand_square, totals[4], D ** (-0.5), DECAY)
    shrink_new = adam_update(shrink_master, shrink_mean, shrink_square, totals[5], (FF // 32) ** (-0.5), DECAY)
    return (output, input_grad, attend_new[0], attend_new[1], attend_new[2], attend_new[3], outward_new[0], outward_new[1], outward_new[2], outward_new[3], router_new[0], router_new[1], router_new[2], router_new[3], gains_new[0], gains_new[1], gains_new[2], gains_new[3], expand_new[0], expand_new[1], expand_new[2], expand_new[3], shrink_new[0], shrink_new[1], shrink_new[2], shrink_new[3])
```

```python
import functools
import math

import jax
import jax.numpy as jnp
from jax import lax
from jax.experimental import pallas as pl
from jax.experimental.pallas import tpu as pltpu
from jax.sharding import PartitionSpec as P

D = 1536
HEADS = 24
KVH = 8
HD = 64
FF = 512
STEP = 10
GROUP = HEADS // KVH
PAIRS = KVH // 2
LANES = 2 * HD
SCALE = HD**-0.5


EPSILON = 1e-05
THETA = 10000.0
BETA_ONE = 0.9
BETA_TWO = 0.95
ADAM_EPSILON = 1e-08
DECAY = 0.1
NEGATIVE = -1e30
BF16 = jnp.bfloat16
F32 = jnp.float32
NT = (((1,), (1,)), ((), ()))


def rms_forward(values, gain_vec):
    scale_row = lax.rsqrt(jnp.mean(values * values, axis=-1, keepdims=True) + EPSILON)
    unit_rows = values * scale_row
    return (unit_rows * gain_vec, unit_rows, scale_row)


def rms_backward(grad_rows, unit_rows, scale_row, gain_vec):
    inner = grad_rows * gain_vec
    grad_values = scale_row * (
        inner - unit_rows * jnp.mean(inner * unit_rows, axis=-1, keepdims=True)
    )
    return (grad_values, jnp.sum(grad_rows * unit_rows, axis=0))


def adam_update(master, first_mom, second_mom, grad, rate, decay):
    first_new = BETA_ONE * first_mom + (1.0 - BETA_ONE) * grad
    second_new = BETA_TWO * second_mom + (1.0 - BETA_TWO) * grad * grad
    first_hat = first_new / (1.0 - BETA_ONE**STEP)
    second_hat = second_new / (1.0 - BETA_TWO**STEP)
    master_new = master - rate * (
        first_hat / (jnp.sqrt(second_hat) + ADAM_EPSILON) + decay * master
    )
    return (first_new, second_new, master_new, master_new.astype(jnp.bfloat16))


def pair_heads(block, axis):
    shape = block.shape
    split = shape[:axis] + (PAIRS, 2, GROUP, HD) + shape[axis + 1 :]
    return jnp.swapaxes(block.reshape(split), axis + 1, axis + 2).reshape(shape)


def unpair_heads(block, axis):
    shape = block.shape
    split = shape[:axis] + (PAIRS, GROUP, 2, HD) + shape[axis + 1 :]
    return jnp.swapaxes(block.reshape(split), axis + 1, axis + 2).reshape(shape)


def turn_tables(positions):
    half = HD // 2
    frequency = THETA ** (-jnp.arange(half, dtype=F32) / half)
    angles = positions.astype(F32)[:, None] * frequency[None, :]
    cosine = jnp.cos(angles)
    sine = jnp.sin(angles)
    return (
        jnp.concatenate([cosine] * 4, axis=1),
        jnp.concatenate([-sine, sine, -sine, sine], axis=1),
    )


def swap_halves(block):
    half = HD // 2
    lane = lax.broadcasted_iota(jnp.int32, block.shape, 1)
    ahead = pltpu.roll(block, LANES - half, 1)
    behind = pltpu.roll(block, half, 1)
    return jnp.where(lane % HD < half, ahead, behind)


def project_kernel(x_ref, gain_ref, w_ref, cos_ref, sin_ref, q_ref, kv_ref, h_ref):
    step = pl.program_id(0)
    query_tiles = HEADS * HD // 256
    key_tiles = KVH * HD // 256

    @pl.when(step == 0)
    def _():
        rows = x_ref[...].astype(F32)
        scale_row = lax.rsqrt(jnp.mean(rows * rows, axis=-1, keepdims=True) + EPSILON)
        h_ref[...] = (rows * scale_row * gain_ref[...]).astype(BF16)

    acc = jnp.dot(h_ref[...], w_ref[...], preferred_element_type=F32)

    def turned(half):
        part = acc[:, half * LANES : (half + 1) * LANES]
        return part * cos_ref[...] + swap_halves(part) * sin_ref[...]

    @pl.when(step < query_tiles)
    def _():
        for half in range(2):
            q_ref[:, half * LANES : (half + 1) * LANES] = (turned(half) * SCALE).astype(BF16)

    @pl.when((step >= query_tiles) & (step < query_tiles + key_tiles))
    def _():
        for half in range(2):
            kv_ref[:, half * LANES : (half + 1) * LANES] = turned(half).astype(BF16)

    @pl.when(step >= query_tiles + key_tiles)
    def _():
        kv_ref[...] = acc.astype(BF16)


def project(x, gain, weights, cosine, sine):
    rows = x.shape[0]
    query_tiles = HEADS * HD // 256
    tiles = (HEADS + 2 * KVH) * HD // 256
    return pl.pallas_call(
        project_kernel,
        grid=(tiles,),
        in_specs=[
            pl.BlockSpec((rows, D), lambda j: (0, 0)),
            pl.BlockSpec((1, D), lambda j: (0, 0)),
            pl.BlockSpec((D, 256), lambda j: (0, j)),
            pl.BlockSpec((rows, LANES), lambda j: (0, 0)),
            pl.BlockSpec((rows, LANES), lambda j: (0, 0)),
        ],
        out_specs=[
            pl.BlockSpec((rows, 256), lambda j: (0, jnp.minimum(j, query_tiles - 1))),
            pl.BlockSpec((rows, 256), lambda j: (0, jnp.maximum(j - query_tiles, 0))),
            pl.BlockSpec((rows, D), lambda j: (0, 0)),
        ],
        out_shape=[
            jax.ShapeDtypeStruct((rows, HEADS * HD), BF16),
            jax.ShapeDtypeStruct((rows, 2 * KVH * HD), BF16),
            jax.ShapeDtypeStruct((rows, D), BF16),
        ],
        compiler_params=pltpu.CompilerParams(vmem_limit_bytes=40 * 1024 * 1024),
        cost_estimate=pl.CostEstimate(
            flops=2 * rows * D * tiles * 256, bytes_accessed=D * tiles * 512, transcendentals=0
        ),
    )(x, gain, weights, cosine, sine)


def masked_pair(block):
    lane = lax.broadcasted_iota(jnp.int32, block.shape, 1)
    zero = jnp.zeros_like(block)
    return jnp.concatenate(
        [jnp.where(lane < HD, block, zero), jnp.where(lane >= HD, block, zero)], axis=0
    )


def key_loops(bounds_ref, sub, step):
    low = bounds_ref[sub, 0]
    full_low = bounds_ref[sub, 1]
    full_high = bounds_ref[sub, 2]
    high = bounds_ref[sub, 3]
    lax.fori_loop(low, full_low, functools.partial(step, True), 0)
    lax.fori_loop(full_low, full_high, functools.partial(step, False), 0)
    lax.fori_loop(full_high, high, functools.partial(step, True), 0)


def allowed_keys(block_id, key_rows, columns, place_ref):
    key_pos = block_id * key_rows + lax.broadcasted_iota(jnp.int32, (key_rows, columns), 0)
    query_pos = jnp.concatenate([place_ref[0:1, :]] * 2, axis=1)
    first_pos = jnp.concatenate([place_ref[1:2, :]] * 2, axis=1)
    return (key_pos <= query_pos) & (key_pos >= first_pos)


def attend_kernel(
    bounds_ref, place_ref, q_ref, k_ref, v_ref, o_ref, ot_ref, lse_ref, qq, vt, top, total, acc
):
    sub = pl.program_id(1)
    query_rows = q_ref.shape[0]
    columns = 2 * query_rows
    key_rows = min(256, k_ref.shape[0])

    @pl.when(sub == 0)
    def _():
        vt[...] = v_ref[...].astype(F32).T.astype(BF16)

    for r in range(GROUP):
        qq[r] = masked_pair(q_ref[:, r * LANES : (r + 1) * LANES])
    top[...] = jnp.full(top.shape, NEGATIVE, F32)
    total[...] = jnp.zeros(total.shape, F32)
    acc[...] = jnp.zeros(acc.shape, F32)

    def step(masked, block_id, carry):
        start = pl.multiple_of(block_id * key_rows, key_rows)
        keys = k_ref[pl.ds(start, key_rows), :]
        turned = vt[:, pl.ds(start, key_rows)]
        if masked:
            allowed = allowed_keys(block_id, key_rows, columns, place_ref)
        for r in range(GROUP):
            scores = lax.dot_general(keys, qq[r], NT, preferred_element_type=F32)
            if masked:
                scores = jnp.where(allowed, scores, NEGATIVE)
            before = top[r]
            now = jnp.maximum(before, jnp.max(scores, axis=0, keepdims=True))
            shrinking = jnp.exp(before - now)
            terms = jnp.exp(scores - now)
            top[r] = now
            total[r] = total[r] * shrinking + jnp.sum(terms, axis=0, keepdims=True)
            acc[r] = acc[r] * shrinking + jnp.dot(
                turned, terms.astype(BF16), preferred_element_type=F32
            )
        return carry

    key_loops(bounds_ref, sub, step)
    for r in range(GROUP):
        mixed = acc[r] / total[r]
        lse = top[r] + jnp.log(total[r])
        for i in range(2):
            lse_ref[0, 2 * r + i : 2 * r + i + 1, :] = lse[
                :, i * query_rows : (i + 1) * query_rows
            ]
        both = jnp.concatenate([mixed[:HD, :query_rows], mixed[HD:, query_rows:]], axis=0)
        ot_ref[0, r] = both
        o_ref[:, r * LANES : (r + 1) * LANES] = both.T.astype(BF16)


def attend_forward(bounds, place, q, kv):
    rows = q.shape[0]
    stream = kv.shape[0]
    sub_rows = min(256, rows)
    subs = rows // sub_rows
    columns = 2 * sub_rows
    wide = GROUP * LANES
    return pl.pallas_call(
        attend_kernel,
        grid_spec=pltpu.PrefetchScalarGridSpec(
            num_scalar_prefetch=1,
            grid=(PAIRS, subs),
            in_specs=[
                pl.BlockSpec((2, sub_rows), lambda p, s, b: (0, s)),
                pl.BlockSpec((sub_rows, wide), lambda p, s, b: (s, p)),
                pl.BlockSpec((stream, LANES), lambda p, s, b: (0, p)),
                pl.BlockSpec((stream, LANES), lambda p, s, b: (0, PAIRS + p)),
            ],
            out_specs=[
                pl.BlockSpec((sub_rows, wide), lambda p, s, b: (s, p)),
                pl.BlockSpec((1, GROUP, LANES, sub_rows), lambda p, s, b: (p, 0, 0, s)),
                pl.BlockSpec((1, 2 * GROUP, sub_rows), lambda p, s, b: (p, 0, s)),
            ],
            scratch_shapes=[
                pltpu.VMEM((GROUP, columns, LANES), BF16),
                pltpu.VMEM((LANES, stream), BF16),
                pltpu.VMEM((GROUP, 1, columns), F32),
                pltpu.VMEM((GROUP, 1, columns), F32),
                pltpu.VMEM((GROUP, LANES, columns), F32),
            ],
        ),
        out_shape=[
            jax.ShapeDtypeStruct((rows, HEADS * HD), BF16),
            jax.ShapeDtypeStruct((PAIRS, GROUP, LANES, rows), F32),
            jax.ShapeDtypeStruct((PAIRS, 2 * GROUP, rows), F32),
        ],
        compiler_params=pltpu.CompilerParams(vmem_limit_bytes=40 * 1024 * 1024),
        cost_estimate=pl.CostEstimate(
            flops=16 * rows * stream * D, bytes_accessed=2 * stream * 1024, transcendentals=0
        ),
    )(bounds, place, q, kv, kv)


def attend_back_kernel(
    bounds_ref,
    place_ref,
    q_ref,
    do_ref,
    ot_ref,
    lse_ref,
    k_ref,
    v_ref,
    cos_ref,
    sin_ref,
    own_cos_ref,
    own_sin_ref,
    dq_ref,
    dk_ref,
    dv_ref,
    qq,
    dd,
    kt,
    stats,
    acc,
    dk,
    dv,
):
    sub = pl.program_id(1)
    query_rows = q_ref.shape[0]
    columns = 2 * query_rows
    key_rows = min(256, k_ref.shape[0])

    @pl.when(sub == 0)
    def _():
        kt[...] = k_ref[...].astype(F32).T.astype(BF16)
        dk[...] = jnp.zeros(dk.shape, F32)
        dv[...] = jnp.zeros(dv.shape, F32)

    for r in range(GROUP):
        lanes = slice(r * LANES, (r + 1) * LANES)
        qq[r] = masked_pair(q_ref[:, lanes])
        dd[r] = masked_pair(do_ref[:, lanes])
        product = do_ref[:, lanes].astype(F32).T * ot_ref[0, r]
        for i in range(2):
            own = slice(i * query_rows, (i + 1) * query_rows)
            stats[r, 0:1, own] = lse_ref[0, 2 * r + i : 2 * r + i + 1, :]
            stats[r, 1:2, own] = jnp.sum(product[i * HD : (i + 1) * HD], axis=0, keepdims=True)
    acc[...] = jnp.zeros(acc.shape, F32)

    def step(masked, block_id, carry):
        start = pl.multiple_of(block_id * key_rows, key_rows)
        keys = k_ref[pl.ds(start, key_rows), :]
        values = v_ref[pl.ds(start, key_rows), :]
        turned = kt[:, pl.ds(start, key_rows)]
        key_grad = dk[pl.ds(start, key_rows), :]
        value_grad = dv[pl.ds(start, key_rows), :]
        if masked:
            allowed = allowed_keys(block_id, key_rows, columns, place_ref)
        for r in range(GROUP):
            scores = lax.dot_general(keys, qq[r], NT, preferred_element_type=F32)
            probs = jnp.exp(scores - stats[r, 0:1, :])
            if masked:
                probs = jnp.where(allowed, probs, 0.0)
            value_grad += jnp.dot(probs.astype(BF16), dd[r], preferred_element_type=F32)
            prob_grad = lax.dot_general(values, dd[r], NT, preferred_element_type=F32)
            score_grad = (probs * (prob_grad - stats[r, 1:2, :])).astype(BF16)
            key_grad += jnp.dot(score_grad, qq[r], preferred_element_type=F32)
            acc[r] += jnp.dot(turned, score_grad, preferred_element_type=F32)
        dk[pl.ds(start, key_rows), :] = key_grad
        dv[pl.ds(start, key_rows), :] = value_grad
        return carry

    key_loops(bounds_ref, sub, step)
    for r in range(GROUP):
        both = jnp.concatenate([acc[r, :HD, :query_rows], acc[r, HD:, query_rows:]], axis=0)
        grad = both.T * SCALE
        grad = grad * own_cos_ref[...] - swap_halves(grad) * own_sin_ref[...]
        dq_ref[:, r * LANES : (r + 1) * LANES] = grad.astype(BF16)

    @pl.when(sub == pl.num_programs(1) - 1)
    def _():
        dk_ref[...] = (dk[...] * cos_ref[...] - swap_halves(dk[...]) * sin_ref[...]).astype(BF16)
        dv_ref[...] = dv[...].astype(BF16)


def attend_backward(bounds, place, q, do, ot, lse, kv, tables, own_tables):
    rows = q.shape[0]
    stream = kv.shape[0]
    sub_rows = min(256, rows)
    subs = rows // sub_rows
    columns = 2 * sub_rows
    wide = GROUP * LANES
    return pl.pallas_call(
        attend_back_kernel,
        grid_spec=pltpu.PrefetchScalarGridSpec(
            num_scalar_prefetch=1,
            grid=(PAIRS, subs),
            in_specs=[
                pl.BlockSpec((2, sub_rows), lambda p, s, b: (0, s)),
                pl.BlockSpec((sub_rows, wide), lambda p, s, b: (s, p)),
                pl.BlockSpec((sub_rows, wide), lambda p, s, b: (s, p)),
                pl.BlockSpec((1, GROUP, LANES, sub_rows), lambda p, s, b: (p, 0, 0, s)),
                pl.BlockSpec((1, 2 * GROUP, sub_rows), lambda p, s, b: (p, 0, s)),
                pl.BlockSpec((stream, LANES), lambda p, s, b: (0, p)),
                pl.BlockSpec((stream, LANES), lambda p, s, b: (0, PAIRS + p)),
                pl.BlockSpec((stream, LANES), lambda p, s, b: (0, 0)),
                pl.BlockSpec((stream, LANES), lambda p, s, b: (0, 0)),
                pl.BlockSpec((sub_rows, LANES), lambda p, s, b: (s, 0)),
                pl.BlockSpec((sub_rows, LANES), lambda p, s, b: (s, 0)),
            ],
            out_specs=[
                pl.BlockSpec((sub_rows, wide), lambda p, s, b: (s, p)),
                pl.BlockSpec((stream, LANES), lambda p, s, b: (0, p)),
                pl.BlockSpec((stream, LANES), lambda p, s, b: (0, p)),
            ],
            scratch_shapes=[
                pltpu.VMEM((GROUP, columns, LANES), BF16),
                pltpu.VMEM((GROUP, columns, LANES), BF16),
                pltpu.VMEM((LANES, stream), BF16),
                pltpu.VMEM((GROUP, 2, columns), F32),
                pltpu.VMEM((GROUP, LANES, columns), F32),
                pltpu.VMEM((stream, LANES), F32),
                pltpu.VMEM((stream, LANES), F32),
            ],
        ),
        out_shape=[
            jax.ShapeDtypeStruct((rows, HEADS * HD), BF16),
            jax.ShapeDtypeStruct((stream, KVH * HD), BF16),
            jax.ShapeDtypeStruct((stream, KVH * HD), BF16),
        ],
        compiler_params=pltpu.CompilerParams(vmem_limit_bytes=40 * 1024 * 1024),
        cost_estimate=pl.CostEstimate(
            flops=40 * rows * stream * D, bytes_accessed=4 * stream * 1024, transcendentals=0
        ),
    )(bounds, place, q, do, ot, lse, kv, kv, *tables, *own_tables)


def slot_codes(route_ids, priority_row, experts, capacity):
    rows, top_count = route_ids.shape
    ranks = priority_row.reshape(rows, top_count)
    routed = route_ids[:, :, None] == jnp.arange(experts, dtype=jnp.int32)[None, None, :]
    unused = rows * top_count
    rank = jnp.min(jnp.where(routed, ranks[:, :, None], unused), axis=1).T
    earlier = jnp.sum((rank[:, None, :] < rank[:, :, None]).astype(jnp.int32), axis=2)
    return jnp.where(rank < unused, jnp.minimum(earlier, capacity) + 1, 0).T


def swap_rows(block):
    return lax.all_gather(block, "exp", axis=0, tiled=False)


def body(
    tokens,
    cotangent,
    doc_starts,
    routes,
    priority,
    attend_master,
    attend_mean,
    attend_square,
    outward_master,
    outward_mean,
    outward_square,
    router_master,
    router_mean,
    router_square,
    gains_master,
    gains_mean,
    gains_square,
    expand_master,
    expand_mean,
    expand_square,
    shrink_master,
    shrink_mean,
    shrink_square,
):
    local_low = tokens[0, 0]
    local_rows = local_low.astype(F32)
    rows_dev, width = local_rows.shape
    ctx_count = lax.axis_size("ctx")
    ctx_place = lax.axis_index("ctx")
    exp_count = lax.axis_size("exp")
    exp_place = lax.axis_index("exp")
    stream_len = rows_dev * ctx_count
    experts = router_master.shape[1]
    local_experts = experts // exp_count
    top_count = routes.shape[-1]
    capacity = rows_dev * top_count * 9 // (8 * experts)
    every = ("dp", "ctx", "exp")
    query_end = HEADS * HD
    qkv = (HEADS + 2 * KVH) * HD
    shard = attend_master.shape[0]

    attend_own = jnp.concatenate(
        [pair_heads(attend_master[:, :query_end], 1), attend_master[:, query_end:]], axis=1
    )
    rest = LANES - experts - 2
    first_own = jnp.concatenate(
        [attend_own, router_master, gains_master.T, jnp.zeros((shard, rest), F32)], axis=1
    ).astype(BF16)
    first_w = lax.all_gather(first_own, every, axis=0, tiled=True)
    attend_w = first_w[:, :qkv]
    router_w = first_w[:, qkv : qkv + experts]
    gains_f = first_w[:, qkv + experts : qkv + experts + 2].T.astype(F32)
    outward_w = lax.all_gather(
        pair_heads(outward_master, 0).T.astype(BF16), every, axis=0, tiled=True
    )
    expand_w = lax.all_gather(expand_master.astype(BF16), ("dp", "ctx"), axis=1, tiled=True)
    shrink_w = lax.all_gather(shrink_master.astype(BF16), ("dp", "ctx"), axis=1, tiled=True)

    codes = slot_codes(routes[0, 0], priority[0, 0, 0], experts, capacity)
    known = jnp.concatenate(
        [
            cotangent[0, 0],
            (codes // 256).astype(BF16),
            (codes % 256).astype(BF16),
            jnp.zeros((rows_dev, LANES - 2 * experts), BF16),
        ],
        axis=1,
    )
    known = swap_rows(known)
    grad_out_all = known[:, :, :width]
    codes_all = 256 * known[:, :, width : width + experts].astype(jnp.int32) + known[
        :, :, width + experts : width + 2 * experts
    ].astype(jnp.int32)

    positions = ctx_place * rows_dev + jnp.arange(rows_dev, dtype=jnp.int32)
    all_positions = jnp.arange(stream_len, dtype=jnp.int32)
    starts = doc_starts[0, 0]
    first_pos = jnp.max(jnp.where(starts[None, :] <= positions[:, None], starts[None, :], 0), axis=1)
    place = jnp.stack([positions, first_pos], axis=0)
    sub_rows = min(256, rows_dev)
    key_rows = min(256, stream_len)
    sub_first = positions[::sub_rows]
    sub_last = positions[sub_rows - 1 :: sub_rows]
    low = first_pos[::sub_rows] // key_rows
    high = sub_last // key_rows + 1
    full_low = jnp.clip((first_pos[sub_rows - 1 :: sub_rows] + key_rows - 1) // key_rows, low, high)
    full_high = jnp.clip((sub_first + 1) // key_rows, full_low, high)
    bounds = jnp.stack([low, full_low, full_high, high], axis=1)
    tables = turn_tables(all_positions)
    own_tables = tuple(
        lax.dynamic_slice_in_dim(table, ctx_place * rows_dev, rows_dev, 0) for table in tables
    )
    queries, pairs, first_low = project(local_low, gains_f[0:1], first_w, *own_tables)
    pairs_all = lax.all_gather(pairs, "ctx", axis=0, tiled=True)
    mixed_low, mixed_turned, log_total = attend_forward(bounds, place, queries, pairs_all)
    branch = lax.dot_general(mixed_low, outward_w, NT, preferred_element_type=F32)
    middle = local_rows + branch
    second_norm, second_unit, second_scale = rms_forward(middle, gains_f[1])
    second_low = second_norm.astype(BF16)

    second_all = swap_rows(second_low)
    logits_all = jnp.einsum("ntd,de->nte", second_all, router_w, preferred_element_type=F32)
    gates_all = jax.nn.softmax(jnp.where(codes_all > 0, logits_all, NEGATIVE), axis=-1)
    gates_all = jnp.where(codes_all > 0, gates_all, 0.0)
    first_expert = exp_place * local_experts
    own_codes = lax.dynamic_slice_in_dim(codes_all, first_expert, local_experts, 2)
    own_gates = lax.dynamic_slice_in_dim(gates_all, first_expert, local_experts, 2)
    slots = jnp.arange(1, capacity + 1, dtype=jnp.int32)
    hot = jnp.swapaxes(own_codes, 1, 2)[:, :, None, :] == slots[None, None, :, None]
    hot_low = hot.astype(BF16)
    slot_gates = jnp.sum(
        jnp.where(hot, jnp.swapaxes(own_gates, 1, 2)[:, :, None, :], 0.0), axis=-1, keepdims=True
    )
    received = jnp.einsum("nist,ntd->nisd", hot_low, second_all, preferred_element_type=F32).astype(
        BF16
    )
    gate_up = jnp.einsum("nisd,idf->nisf", received, expand_w, preferred_element_type=F32)
    gate_part = gate_up[..., :FF]
    up_part = gate_up[..., FF:]
    hidden_low = (jax.nn.silu(gate_part) * up_part).astype(BF16)
    results = jnp.einsum("nisf,ifd->nisd", hidden_low, shrink_w, preferred_element_type=F32)
    results_low = (slot_gates * results).astype(BF16)
    mixture = jnp.einsum("nist,nisd->ntd", hot_low, results_low, preferred_element_type=F32)
    mixture = lax.psum_scatter(
        mixture.astype(BF16).reshape(exp_count * rows_dev, width),
        "exp",
        scatter_dimension=0,
        tiled=True,
    )
    output = (middle + mixture.astype(F32)).astype(BF16)

    grad_received = jnp.einsum("nist,ntd->nisd", hot_low, grad_out_all, preferred_element_type=F32)
    grad_slot_gates = jnp.sum(grad_received * results, axis=-1)
    grad_results = (slot_gates * grad_received).astype(BF16)
    grad_gates = jnp.einsum(
        "nist,nis->nti", hot.astype(F32), grad_slot_gates, precision=lax.Precision.HIGHEST
    )
    grad_gates = lax.all_to_all(grad_gates, "exp", split_axis=0, concat_axis=0, tiled=True)
    grad_gates = jnp.swapaxes(grad_gates, 0, 1).reshape(rows_dev, experts)
    grad_hidden = jnp.einsum("nisd,ifd->nisf", grad_results, shrink_w, preferred_element_type=F32)
    sigma = jax.nn.sigmoid(gate_part)
    grad_gate = grad_hidden * up_part * sigma * (1.0 + gate_part * (1.0 - sigma))
    grad_up = grad_hidden * gate_part * sigma
    grad_gate_up = jnp.concatenate([grad_gate, grad_up], axis=-1).astype(BF16)
    grad_rows = jnp.einsum(
        "nisf,idf->nisd", grad_gate_up, expand_w, preferred_element_type=F32
    ).astype(BF16)
    row_grads = jnp.einsum("nist,nisd->ntd", hot_low, grad_rows, preferred_element_type=F32)
    row_grads = lax.psum_scatter(
        row_grads.astype(BF16).reshape(exp_count * rows_dev, width),
        "exp",
        scatter_dimension=0,
        tiled=True,
    ).astype(F32)
    shrink_grad = jnp.einsum(
        "nisf,nisd->ifd", hidden_low, grad_results, preferred_element_type=F32
    ).astype(BF16)
    expand_grad = jnp.einsum(
        "nisd,nisf->idf", received, grad_gate_up, preferred_element_type=F32
    ).astype(BF16)
    shrink_sum = lax.psum_scatter(shrink_grad, ("dp", "ctx"), scatter_dimension=1, tiled=True)
    expand_sum = lax.psum_scatter(expand_grad, ("dp", "ctx"), scatter_dimension=1, tiled=True)

    gates = lax.dynamic_index_in_dim(gates_all, exp_place, 0, keepdims=False)
    mean_term = jnp.sum(gates * grad_gates, axis=-1, keepdims=True)
    grad_logits = (gates * (grad_gates - mean_term)).astype(BF16)
    router_grad = jnp.einsum("td,te->de", second_low, grad_logits, preferred_element_type=F32)
    grad_second = row_grads + jnp.einsum(
        "te,de->td", grad_logits, router_w, preferred_element_type=F32
    )
    grad_middle_norm, gain_two_grad = rms_backward(
        grad_second, second_unit, second_scale, gains_f[1]
    )
    grad_middle = cotangent[0, 0].astype(F32) + grad_middle_norm
    grad_branch = grad_middle.astype(BF16)

    grad_mixed = jnp.dot(grad_branch, outward_w, preferred_element_type=F32).astype(BF16)
    grad_query, grad_keys, grad_values = attend_backward(
        bounds,
        place,
        queries,
        grad_mixed,
        mixed_turned,
        log_total,
        pairs_all,
        tables,
        own_tables,
    )
    key_sum = lax.psum_scatter(
        jnp.concatenate([grad_keys, grad_values], axis=1), "ctx", scatter_dimension=0, tiled=True
    )
    outward_grad = jnp.einsum("td,tc->dc", grad_branch, mixed_low, preferred_element_type=F32)
    outward_sum = lax.psum_scatter(outward_grad.astype(BF16), every, scatter_dimension=0, tiled=True)
    grad_project = jnp.concatenate([grad_query, key_sum], axis=1)
    attend_grad = jnp.einsum("tc,tp->cp", first_low, grad_project, preferred_element_type=F32)
    grad_first = lax.dot_general(grad_project, attend_w, NT, preferred_element_type=F32)
    first_norm, first_unit, first_scale = rms_forward(local_rows, gains_f[0])
    grad_input_norm, gain_one_grad = rms_backward(grad_first, first_unit, first_scale, gains_f[0])
    input_grad = grad_middle + grad_input_norm
    first_grad = jnp.concatenate(
        [
            attend_grad.astype(BF16),
            router_grad.astype(BF16),
            jnp.stack([gain_one_grad, gain_two_grad], axis=1).astype(BF16),
            jnp.zeros((width, rest), BF16),
        ],
        axis=1,
    )
    first_sum = lax.psum_scatter(first_grad, every, scatter_dimension=0, tiled=True).astype(F32)
    attend_sum = jnp.concatenate(
        [unpair_heads(first_sum[:, :query_end], 1), first_sum[:, query_end:qkv]], axis=1
    )
    router_sum = first_sum[:, qkv : qkv + experts]
    gains_sum = first_sum[:, qkv + experts : qkv + experts + 2].T
    outward_sum = unpair_heads(outward_sum.astype(F32).T, 0)
    expand_sum = expand_sum.astype(F32)
    shrink_sum = shrink_sum.astype(F32)
    attend_new = adam_update(
        attend_master, attend_mean, attend_square, attend_sum, D ** (-0.5), DECAY
    )
    outward_new = adam_update(
        outward_master, outward_mean, outward_square, outward_sum, 4.0 * D ** (-0.5), DECAY
    )
    router_new = adam_update(
        router_master, router_mean, router_square, router_sum, 0.5 * D ** (-0.5), DECAY
    )
    gains_new = adam_update(gains_master, gains_mean, gains_square, gains_sum, 0.6, 0.0)
    expand_new = adam_update(
        expand_master, expand_mean, expand_square, expand_sum, D ** (-0.5), DECAY
    )
    shrink_new = adam_update(
        shrink_master, shrink_mean, shrink_square, shrink_sum, (FF // 32) ** (-0.5), DECAY
    )
    return (
        output[None, None],
        input_grad[None, None],
        attend_new[0],
        attend_new[1],
        attend_new[2],
        attend_new[3],
        outward_new[0],
        outward_new[1],
        outward_new[2],
        outward_new[3],
        router_new[0],
        router_new[1],
        router_new[2],
        router_new[3],
        gains_new[0],
        gains_new[1],
        gains_new[2],
        gains_new[3],
        expand_new[0],
        expand_new[1],
        expand_new[2],
        expand_new[3],
        shrink_new[0],
        shrink_new[1],
        shrink_new[2],
        shrink_new[3],
    )


def solution(mesh):
    in_specs = (
        P("dp", "exp", "ctx", None),
        P("dp", "exp", "ctx", None),
        P("dp", "exp", None),
        P("dp", "exp", "ctx", None),
        P("dp", "exp", "ctx", None),
        P(("dp", "ctx", "exp"), None),
        P(("dp", "ctx", "exp"), None),
        P(("dp", "ctx", "exp"), None),
        P(None, ("dp", "ctx", "exp")),
        P(None, ("dp", "ctx", "exp")),
        P(None, ("dp", "ctx", "exp")),
        P(("dp", "ctx", "exp"), None),
        P(("dp", "ctx", "exp"), None),
        P(("dp", "ctx", "exp"), None),
        P(None, ("dp", "ctx", "exp")),
        P(None, ("dp", "ctx", "exp")),
        P(None, ("dp", "ctx", "exp")),
        P("exp", ("dp", "ctx"), None),
        P("exp", ("dp", "ctx"), None),
        P("exp", ("dp", "ctx"), None),
        P("exp", ("dp", "ctx"), None),
        P("exp", ("dp", "ctx"), None),
        P("exp", ("dp", "ctx"), None),
    )
    out_specs = (
        P("dp", "exp", "ctx", None),
        P("dp", "exp", "ctx", None),
        P(("dp", "ctx", "exp"), None),
        P(("dp", "ctx", "exp"), None),
        P(("dp", "ctx", "exp"), None),
        P(("dp", "ctx", "exp"), None),
        P(None, ("dp", "ctx", "exp")),
        P(None, ("dp", "ctx", "exp")),
        P(None, ("dp", "ctx", "exp")),
        P(None, ("dp", "ctx", "exp")),
        P(("dp", "ctx", "exp"), None),
        P(("dp", "ctx", "exp"), None),
        P(("dp", "ctx", "exp"), None),
        P(("dp", "ctx", "exp"), None),
        P(None, ("dp", "ctx", "exp")),
        P(None, ("dp", "ctx", "exp")),
        P(None, ("dp", "ctx", "exp")),
        P(None, ("dp", "ctx", "exp")),
        P("exp", ("dp", "ctx"), None),
        P("exp", ("dp", "ctx"), None),
        P("exp", ("dp", "ctx"), None),
        P("exp", ("dp", "ctx"), None),
        P("exp", ("dp", "ctx"), None),
        P("exp", ("dp", "ctx"), None),
        P("exp", ("dp", "ctx"), None),
        P("exp", ("dp", "ctx"), None),
    )
    return jax.shard_map(body, mesh=mesh, in_specs=in_specs, out_specs=out_specs, check_vma=False)
```

```python
import functools
import math

import jax
import jax.numpy as jnp
from jax import lax
from jax.experimental import pallas as pl
from jax.experimental.pallas import tpu as pltpu
from jax.sharding import PartitionSpec as P

D = 1536
HEADS = 24
KVH = 8
HD = 64
FF = 512
STEP = 10
GROUP = HEADS // KVH
PAIRS = KVH // 2
LANES = 2 * HD
SCALE = HD**-0.5


EPSILON = 1e-05
THETA = 10000.0
BETA_ONE = 0.9
BETA_TWO = 0.95
ADAM_EPSILON = 1e-08
DECAY = 0.1
NEGATIVE = -1e30
BF16 = jnp.bfloat16
F32 = jnp.float32
NT = (((1,), (1,)), ((), ()))


def rms_forward(values, gain_vec):
    scale_row = lax.rsqrt(jnp.mean(values * values, axis=-1, keepdims=True) + EPSILON)
    unit_rows = values * scale_row
    return (unit_rows * gain_vec, unit_rows, scale_row)


def rms_backward(grad_rows, unit_rows, scale_row, gain_vec):
    inner = grad_rows * gain_vec
    grad_values = scale_row * (
        inner - unit_rows * jnp.mean(inner * unit_rows, axis=-1, keepdims=True)
    )
    return (grad_values, jnp.sum(grad_rows * unit_rows, axis=0))


def adam_update(master, first_mom, second_mom, grad, rate, decay):
    first_new = BETA_ONE * first_mom + (1.0 - BETA_ONE) * grad
    second_new = BETA_TWO * second_mom + (1.0 - BETA_TWO) * grad * grad
    first_hat = first_new / (1.0 - BETA_ONE**STEP)
    second_hat = second_new / (1.0 - BETA_TWO**STEP)
    master_new = master - rate * (
        first_hat / (jnp.sqrt(second_hat) + ADAM_EPSILON) + decay * master
    )
    return (first_new, second_new, master_new, master_new.astype(jnp.bfloat16))


def pair_heads(block, axis):
    shape = block.shape
    split = shape[:axis] + (PAIRS, 2, GROUP, HD) + shape[axis + 1 :]
    return jnp.swapaxes(block.reshape(split), axis + 1, axis + 2).reshape(shape)


def unpair_heads(block, axis):
    shape = block.shape
    split = shape[:axis] + (PAIRS, GROUP, 2, HD) + shape[axis + 1 :]
    return jnp.swapaxes(block.reshape(split), axis + 1, axis + 2).reshape(shape)


def turn_tables(positions):
    half = HD // 2
    frequency = THETA ** (-jnp.arange(half, dtype=F32) / half)
    angles = positions.astype(F32)[:, None] * frequency[None, :]
    cosine = jnp.cos(angles)
    sine = jnp.sin(angles)
    return (
        jnp.concatenate([cosine] * 4, axis=1),
        jnp.concatenate([-sine, sine, -sine, sine], axis=1),
    )


def swap_halves(block):
    half = HD // 2
    lane = lax.broadcasted_iota(jnp.int32, block.shape, 1)
    ahead = pltpu.roll(block, LANES - half, 1)
    behind = pltpu.roll(block, half, 1)
    return jnp.where(lane % HD < half, ahead, behind)


def project_kernel(x_ref, gain_ref, w_ref, cos_ref, sin_ref, q_ref, kv_ref, h_ref):
    step = pl.program_id(0)
    query_tiles = HEADS * HD // 256
    key_tiles = KVH * HD // 256

    @pl.when(step == 0)
    def _():
        rows = x_ref[...].astype(F32)
        scale_row = lax.rsqrt(jnp.mean(rows * rows, axis=-1, keepdims=True) + EPSILON)
        h_ref[...] = (rows * scale_row * gain_ref[...]).astype(BF16)

    acc = jnp.dot(h_ref[...], w_ref[...], preferred_element_type=F32)

    def turned(half):
        part = acc[:, half * LANES : (half + 1) * LANES]
        return part * cos_ref[...] + swap_halves(part) * sin_ref[...]

    @pl.when(step < query_tiles)
    def _():
        for half in range(2):
            q_ref[:, half * LANES : (half + 1) * LANES] = (turned(half) * SCALE).astype(BF16)

    @pl.when((step >= query_tiles) & (step < query_tiles + key_tiles))
    def _():
        for half in range(2):
            kv_ref[:, half * LANES : (half + 1) * LANES] = turned(half).astype(BF16)

    @pl.when(step >= query_tiles + key_tiles)
    def _():
        kv_ref[...] = acc.astype(BF16)


def project(x, gain, weights, cosine, sine):
    rows = x.shape[0]
    query_tiles = HEADS * HD // 256
    tiles = (HEADS + 2 * KVH) * HD // 256
    return pl.pallas_call(
        project_kernel,
        grid=(tiles,),
        in_specs=[
            pl.BlockSpec((rows, D), lambda j: (0, 0)),
            pl.BlockSpec((1, D), lambda j: (0, 0)),
            pl.BlockSpec((D, 256), lambda j: (0, j)),
            pl.BlockSpec((rows, LANES), lambda j: (0, 0)),
            pl.BlockSpec((rows, LANES), lambda j: (0, 0)),
        ],
        out_specs=[
            pl.BlockSpec((rows, 256), lambda j: (0, jnp.minimum(j, query_tiles - 1))),
            pl.BlockSpec((rows, 256), lambda j: (0, jnp.maximum(j - query_tiles, 0))),
            pl.BlockSpec((rows, D), lambda j: (0, 0)),
        ],
        out_shape=[
            jax.ShapeDtypeStruct((rows, HEADS * HD), BF16),
            jax.ShapeDtypeStruct((rows, 2 * KVH * HD), BF16),
            jax.ShapeDtypeStruct((rows, D), BF16),
        ],
        compiler_params=pltpu.CompilerParams(vmem_limit_bytes=40 * 1024 * 1024),
        cost_estimate=pl.CostEstimate(
            flops=2 * rows * D * tiles * 256, bytes_accessed=D * tiles * 512, transcendentals=0
        ),
    )(x, gain, weights, cosine, sine)


def masked_pair(block):
    lane = lax.broadcasted_iota(jnp.int32, block.shape, 1)
    zero = jnp.zeros_like(block)
    return jnp.concatenate(
        [jnp.where(lane < HD, block, zero), jnp.where(lane >= HD, block, zero)], axis=0
    )


def key_loops(bounds_ref, sub, step):
    low = bounds_ref[sub, 0]
    full_low = bounds_ref[sub, 1]
    full_high = bounds_ref[sub, 2]
    high = bounds_ref[sub, 3]
    lax.fori_loop(low, full_low, functools.partial(step, True), 0)
    lax.fori_loop(full_low, full_high, functools.partial(step, False), 0)
    lax.fori_loop(full_high, high, functools.partial(step, True), 0)


def allowed_keys(block_id, key_rows, columns, place_ref):
    key_pos = block_id * key_rows + lax.broadcasted_iota(jnp.int32, (key_rows, columns), 0)
    query_pos = jnp.concatenate([place_ref[0:1, :]] * 2, axis=1)
    first_pos = jnp.concatenate([place_ref[1:2, :]] * 2, axis=1)
    return (key_pos <= query_pos) & (key_pos >= first_pos)


def lay_keys(owner_ref, pieces, k_ref, v_ref):
    for index, (key_piece, value_piece) in enumerate(pieces):
        rows = key_piece.shape[0]
        owner = owner_ref[index]

        @pl.when(owner >= 0)
        def _():
            start = pl.multiple_of(owner * rows, rows)
            k_ref[pl.ds(start, rows), :] = key_piece[...]
            v_ref[pl.ds(start, rows), :] = value_piece[...]


def attend_kernel(bounds_ref, owner_ref, place_ref, q_ref, *refs):
    count = owner_ref.shape[0]
    pieces = [(refs[2 * i], refs[2 * i + 1]) for i in range(count)]
    o_ref, ot_ref, lse_ref, k_ref, v_ref, qq, vt, top, total, acc = refs[2 * count :]
    sub = pl.program_id(1)
    query_rows = q_ref.shape[0]
    columns = 2 * query_rows
    key_rows = min(256, k_ref.shape[0])

    @pl.when(sub == 0)
    def _():
        lay_keys(owner_ref, pieces, k_ref, v_ref)
        vt[...] = v_ref[...].astype(F32).T.astype(BF16)

    for r in range(GROUP):
        qq[r] = masked_pair(q_ref[:, r * LANES : (r + 1) * LANES])
    top[...] = jnp.full(top.shape, NEGATIVE, F32)
    total[...] = jnp.zeros(total.shape, F32)
    acc[...] = jnp.zeros(acc.shape, F32)

    def step(masked, block_id, carry):
        start = pl.multiple_of(block_id * key_rows, key_rows)
        keys = k_ref[pl.ds(start, key_rows), :]
        turned = vt[:, pl.ds(start, key_rows)]
        if masked:
            allowed = allowed_keys(block_id, key_rows, columns, place_ref)
        for r in range(GROUP):
            scores = lax.dot_general(keys, qq[r], NT, preferred_element_type=F32)
            if masked:
                scores = jnp.where(allowed, scores, NEGATIVE)
            before = top[r]
            now = jnp.maximum(before, jnp.max(scores, axis=0, keepdims=True))
            shrinking = jnp.exp(before - now)
            terms = jnp.exp(scores - now)
            top[r] = now
            total[r] = total[r] * shrinking + jnp.sum(terms, axis=0, keepdims=True)
            acc[r] = acc[r] * shrinking + jnp.dot(
                turned, terms.astype(BF16), preferred_element_type=F32
            )
        return carry

    key_loops(bounds_ref, sub, step)
    for r in range(GROUP):
        mixed = acc[r] / total[r]
        lse = top[r] + jnp.log(total[r])
        for i in range(2):
            lse_ref[0, 2 * r + i : 2 * r + i + 1, :] = lse[
                :, i * query_rows : (i + 1) * query_rows
            ]
        both = jnp.concatenate([mixed[:HD, :query_rows], mixed[HD:, query_rows:]], axis=0)
        ot_ref[0, r] = both
        o_ref[:, r * LANES : (r + 1) * LANES] = both.T.astype(BF16)


def piece_specs(pieces):
    specs = []
    operands = []
    for piece in pieces:
        rows = piece.shape[0]
        specs.append(pl.BlockSpec((rows, LANES), lambda p, s, *_: (0, p)))
        specs.append(pl.BlockSpec((rows, LANES), lambda p, s, *_: (0, PAIRS + p)))
        operands += [piece, piece]
    return (specs, operands)


def attend_forward(bounds, owners, place, q, pieces):
    rows = q.shape[0]
    stream = rows * len(pieces)
    specs, operands = piece_specs(pieces)
    sub_rows = min(256, rows)
    subs = rows // sub_rows
    columns = 2 * sub_rows
    wide = GROUP * LANES
    return pl.pallas_call(
        attend_kernel,
        grid_spec=pltpu.PrefetchScalarGridSpec(
            num_scalar_prefetch=2,
            grid=(PAIRS, subs),
            in_specs=[
                pl.BlockSpec((2, sub_rows), lambda p, s, *_: (0, s)),
                pl.BlockSpec((sub_rows, wide), lambda p, s, *_: (s, p)),
                *specs,
            ],
            out_specs=[
                pl.BlockSpec((sub_rows, wide), lambda p, s, *_: (s, p)),
                pl.BlockSpec((1, GROUP, LANES, sub_rows), lambda p, s, *_: (p, 0, 0, s)),
                pl.BlockSpec((1, 2 * GROUP, sub_rows), lambda p, s, *_: (p, 0, s)),
            ],
            scratch_shapes=[
                pltpu.VMEM((stream, LANES), BF16),
                pltpu.VMEM((stream, LANES), BF16),
                pltpu.VMEM((GROUP, columns, LANES), BF16),
                pltpu.VMEM((LANES, stream), BF16),
                pltpu.VMEM((GROUP, 1, columns), F32),
                pltpu.VMEM((GROUP, 1, columns), F32),
                pltpu.VMEM((GROUP, LANES, columns), F32),
            ],
        ),
        out_shape=[
            jax.ShapeDtypeStruct((rows, HEADS * HD), BF16),
            jax.ShapeDtypeStruct((PAIRS, GROUP, LANES, rows), F32),
            jax.ShapeDtypeStruct((PAIRS, 2 * GROUP, rows), F32),
        ],
        compiler_params=pltpu.CompilerParams(vmem_limit_bytes=40 * 1024 * 1024),
        cost_estimate=pl.CostEstimate(
            flops=16 * rows * stream * D, bytes_accessed=2 * stream * 1024, transcendentals=0
        ),
    )(bounds, owners, place, q, *operands)


def attend_back_kernel(
    bounds_ref,
    owner_ref,
    place_ref,
    q_ref,
    do_ref,
    ot_ref,
    lse_ref,
    cos_ref,
    sin_ref,
    own_cos_ref,
    own_sin_ref,
    *refs,
):
    count = owner_ref.shape[0]
    pieces = [(refs[2 * i], refs[2 * i + 1]) for i in range(count)]
    dq_ref, dk_ref, dv_ref, k_ref, v_ref, qq, dd, kt, stats, acc, dk, dv = refs[2 * count :]
    sub = pl.program_id(1)
    query_rows = q_ref.shape[0]
    columns = 2 * query_rows
    key_rows = min(256, k_ref.shape[0])

    @pl.when(sub == 0)
    def _():
        lay_keys(owner_ref, pieces, k_ref, v_ref)
        kt[...] = k_ref[...].astype(F32).T.astype(BF16)
        dk[...] = jnp.zeros(dk.shape, F32)
        dv[...] = jnp.zeros(dv.shape, F32)

    for r in range(GROUP):
        lanes = slice(r * LANES, (r + 1) * LANES)
        qq[r] = masked_pair(q_ref[:, lanes])
        dd[r] = masked_pair(do_ref[:, lanes])
        product = do_ref[:, lanes].astype(F32).T * ot_ref[0, r]
        for i in range(2):
            own = slice(i * query_rows, (i + 1) * query_rows)
            stats[r, 0:1, own] = lse_ref[0, 2 * r + i : 2 * r + i + 1, :]
            stats[r, 1:2, own] = jnp.sum(product[i * HD : (i + 1) * HD], axis=0, keepdims=True)
    acc[...] = jnp.zeros(acc.shape, F32)

    def step(masked, block_id, carry):
        start = pl.multiple_of(block_id * key_rows, key_rows)
        keys = k_ref[pl.ds(start, key_rows), :]
        values = v_ref[pl.ds(start, key_rows), :]
        turned = kt[:, pl.ds(start, key_rows)]
        key_grad = dk[pl.ds(start, key_rows), :]
        value_grad = dv[pl.ds(start, key_rows), :]
        if masked:
            allowed = allowed_keys(block_id, key_rows, columns, place_ref)
        for r in range(GROUP):
            scores = lax.dot_general(keys, qq[r], NT, preferred_element_type=F32)
            probs = jnp.exp(scores - stats[r, 0:1, :])
            if masked:
                probs = jnp.where(allowed, probs, 0.0)
            value_grad += jnp.dot(probs.astype(BF16), dd[r], preferred_element_type=F32)
            prob_grad = lax.dot_general(values, dd[r], NT, preferred_element_type=F32)
            score_grad = (probs * (prob_grad - stats[r, 1:2, :])).astype(BF16)
            key_grad += jnp.dot(score_grad, qq[r], preferred_element_type=F32)
            acc[r] += jnp.dot(turned, score_grad, preferred_element_type=F32)
        dk[pl.ds(start, key_rows), :] = key_grad
        dv[pl.ds(start, key_rows), :] = value_grad
        return carry

    key_loops(bounds_ref, sub, step)
    for r in range(GROUP):
        both = jnp.concatenate([acc[r, :HD, :query_rows], acc[r, HD:, query_rows:]], axis=0)
        grad = both.T * SCALE
        grad = grad * own_cos_ref[...] - swap_halves(grad) * own_sin_ref[...]
        dq_ref[:, r * LANES : (r + 1) * LANES] = grad.astype(BF16)

    @pl.when(sub == pl.num_programs(1) - 1)
    def _():
        dk_ref[...] = (dk[...] * cos_ref[...] - swap_halves(dk[...]) * sin_ref[...]).astype(BF16)
        dv_ref[...] = dv[...].astype(BF16)


def attend_backward(bounds, owners, place, q, do, ot, lse, pieces, tables, own_tables):
    rows = q.shape[0]
    stream = rows * len(pieces)
    specs, operands = piece_specs(pieces)
    sub_rows = min(256, rows)
    subs = rows // sub_rows
    columns = 2 * sub_rows
    wide = GROUP * LANES
    return pl.pallas_call(
        attend_back_kernel,
        grid_spec=pltpu.PrefetchScalarGridSpec(
            num_scalar_prefetch=2,
            grid=(PAIRS, subs),
            in_specs=[
                pl.BlockSpec((2, sub_rows), lambda p, s, *_: (0, s)),
                pl.BlockSpec((sub_rows, wide), lambda p, s, *_: (s, p)),
                pl.BlockSpec((sub_rows, wide), lambda p, s, *_: (s, p)),
                pl.BlockSpec((1, GROUP, LANES, sub_rows), lambda p, s, *_: (p, 0, 0, s)),
                pl.BlockSpec((1, 2 * GROUP, sub_rows), lambda p, s, *_: (p, 0, s)),
                pl.BlockSpec((stream, LANES), lambda p, s, *_: (0, 0)),
                pl.BlockSpec((stream, LANES), lambda p, s, *_: (0, 0)),
                pl.BlockSpec((sub_rows, LANES), lambda p, s, *_: (s, 0)),
                pl.BlockSpec((sub_rows, LANES), lambda p, s, *_: (s, 0)),
                *specs,
            ],
            out_specs=[
                pl.BlockSpec((sub_rows, wide), lambda p, s, *_: (s, p)),
                pl.BlockSpec((stream, LANES), lambda p, s, *_: (0, p)),
                pl.BlockSpec((stream, LANES), lambda p, s, *_: (0, p)),
            ],
            scratch_shapes=[
                pltpu.VMEM((stream, LANES), BF16),
                pltpu.VMEM((stream, LANES), BF16),
                pltpu.VMEM((GROUP, columns, LANES), BF16),
                pltpu.VMEM((GROUP, columns, LANES), BF16),
                pltpu.VMEM((LANES, stream), BF16),
                pltpu.VMEM((GROUP, 2, columns), F32),
                pltpu.VMEM((GROUP, LANES, columns), F32),
                pltpu.VMEM((stream, LANES), F32),
                pltpu.VMEM((stream, LANES), F32),
            ],
        ),
        out_shape=[
            jax.ShapeDtypeStruct((rows, HEADS * HD), BF16),
            jax.ShapeDtypeStruct((stream, KVH * HD), BF16),
            jax.ShapeDtypeStruct((stream, KVH * HD), BF16),
        ],
        compiler_params=pltpu.CompilerParams(vmem_limit_bytes=40 * 1024 * 1024),
        cost_estimate=pl.CostEstimate(
            flops=40 * rows * stream * D, bytes_accessed=4 * stream * 1024, transcendentals=0
        ),
    )(bounds, owners, place, q, do, ot, lse, *tables, *own_tables, *operands)


def slot_codes(route_ids, priority_row, experts, capacity):
    rows, top_count = route_ids.shape
    ranks = priority_row.reshape(rows, top_count)
    routed = route_ids[:, :, None] == jnp.arange(experts, dtype=jnp.int32)[None, None, :]
    unused = rows * top_count
    rank = jnp.min(jnp.where(routed, ranks[:, :, None], unused), axis=1).T
    earlier = jnp.sum((rank[:, None, :] < rank[:, :, None]).astype(jnp.int32), axis=2)
    return jnp.where(rank < unused, jnp.where(earlier < capacity, 2, 1), 0).T


def pack_experts(expand, shrink):
    parts = [expand[:, :, :FF], expand[:, :, FF:]]
    parts += [shrink[:, :, j * FF : (j + 1) * FF] for j in range(D // FF)]
    return jnp.concatenate(parts, axis=1)


def after(value, *others):
    return lax.optimization_barrier((value, *others))[0]


def split_devices():
    return (lax.axis_size("dp"), lax.axis_size("ctx"), lax.axis_size("exp")) == (2, 4, 4)


def greet(partners):
    barrier = pltpu.get_barrier_semaphore()
    for partner in partners:
        pl.semaphore_signal(
            barrier, inc=1, device_id=partner, device_id_type=pl.DeviceIdType.MESH
        )
    pl.semaphore_wait(barrier, len(partners))


def neighbours():
    x = lax.axis_index("dp")
    z = lax.axis_index("ctx")
    spot = lax.axis_index("exp")
    y = spot // 2
    core = spot % 2
    other_core = {"exp": 2 * y + 1 - core}
    other_x = {"dp": 1 - x}
    other_y = {"exp": 2 * (1 - y) + core}
    along = [{"ctx": lax.rem(z + d, 4)} for d in range(1, 4)]
    return (x, y, z, core, other_core, other_x, other_y, along)


def send_to(source, target, sems, number, device):
    copy = pltpu.make_async_remote_copy(
        src_ref=source,
        dst_ref=target,
        send_sem=sems[0].at[number],
        recv_sem=sems[1].at[number],
        device_id=device,
        device_id_type=pl.DeviceIdType.MESH,
    )
    copy.start()
    return copy


def dense_gather_kernel(first_ref, second_ref, all_first, all_second, local_sem, *sems):
    x, y, z, core, other_core, other_x, other_y, along = neighbours()
    greet([other_core, other_x, other_y] + along)
    spread = [
        (
            send_to(first_ref, all_first.at[x, z, y, core], sems, 2 * d, along[d]),
            send_to(second_ref, all_second.at[x, z, y, core], sems, 2 * d + 1, along[d]),
        )
        for d in range(3)
    ]
    local = [
        pltpu.make_async_copy(first_ref, all_first.at[x, z, y, core], local_sem.at[0]),
        pltpu.make_async_copy(second_ref, all_second.at[x, z, y, core], local_sem.at[1]),
    ]
    for copy in local:
        copy.start()
    steps = [[], [], []]

    def send_near(index):
        if index == 0:
            for copy in local:
                copy.wait()
        else:
            for copy in spread[index - 1]:
                copy.wait_recv()
        spot = lax.rem(z - index + 4, 4)
        base = 6 + 6 * index
        block = all_first.at[x, spot, y, core]
        other = all_second.at[x, spot, y, core]
        steps[0].append(
            (
                send_to(block, block, sems, base, other_y),
                send_to(other, other, sems, base + 1, other_x),
            )
        )

    def send_far(index):
        for copy in steps[0][index]:
            copy.wait_recv()
        spot = lax.rem(z - index + 4, 4)
        base = 6 + 6 * index
        block = all_first.at[x, spot, :, core]
        other = all_second.at[:, spot, y, core]
        steps[1].append(
            (
                send_to(block, block, sems, base + 2, other_x),
                send_to(other, other, sems, base + 3, other_y),
            )
        )

    def send_core(index):
        for copy in steps[1][index]:
            copy.wait_recv()
        spot = lax.rem(z - index + 4, 4)
        base = 6 + 6 * index
        block = all_first.at[:, spot, :, core]
        other = all_second.at[:, spot, :, core]
        steps[2].append(
            (
                send_to(block, block, sems, base + 4, other_core),
                send_to(other, other, sems, base + 5, other_core),
            )
        )

    send_near(0)
    send_far(0)
    send_near(1)
    send_core(0)
    send_far(1)
    send_near(2)
    send_core(1)
    send_far(2)
    send_near(3)
    send_core(2)
    send_far(3)
    send_core(3)
    for pair in steps[2]:
        for copy in pair:
            copy.wait_recv()
    for pair in spread + steps[0] + steps[1] + steps[2]:
        for copy in pair:
            copy.wait_send()


def dense_gather(first, second):
    if not split_devices():
        every = ("dp", "ctx", "exp")
        return tuple(
            lax.all_gather(part, every, axis=0, tiled=True) for part in (first, second)
        )
    shapes = [(2, 4, 2, 2) + part.shape for part in (first, second)]
    gathered = pl.pallas_call(
        dense_gather_kernel,
        in_specs=[pl.BlockSpec(memory_space=pl.ANY)] * 2,
        out_specs=[pl.BlockSpec(memory_space=pl.ANY)] * 2,
        out_shape=[jax.ShapeDtypeStruct(shape, BF16) for shape in shapes],
        scratch_shapes=[
            pltpu.SemaphoreType.DMA((2,)),
            pltpu.SemaphoreType.DMA((30,)),
            pltpu.SemaphoreType.DMA((30,)),
        ],
        compiler_params=pltpu.CompilerParams(collective_id=2, has_side_effects=True),
        cost_estimate=pl.CostEstimate(
            flops=0, bytes_accessed=64 * (first.size + second.size), transcendentals=0
        ),
    )(first, second)
    return tuple(part.reshape(-1, part.shape[-1]) for part in gathered)


def dense_sum_kernel(starts, *refs):
    count = len(starts)
    parts = refs[:count]
    (
        out_ref,
        own,
        got_core,
        got_x,
        got_y,
        late_x,
        late_y,
        got_z,
        load_sem,
        send_sem,
        recv_sem,
    ) = refs[count:]
    x, y, z, core, other_core, other_x, other_y, along = neighbours()
    half = got_x.shape[-1]
    greet([other_core, other_x, other_y] + along)
    sems = (send_sem, recv_sem)
    first = []
    loads = []
    for index in range(count):
        columns = slice(starts[index], starts[index] + parts[index].shape[-1])
        first.append(
            send_to(
                parts[index].at[:, :, :, 1 - core],
                got_core.at[:, :, :, :, columns],
                sems,
                7 + index,
                other_core,
            )
        )
        loads.append(
            pltpu.make_async_copy(
                parts[index].at[:, :, :, core], own.at[:, :, :, :, columns], load_sem.at[index]
            )
        )
    for copy in loads:
        copy.start()
    for copy in loads + first:
        copy.wait()

    def add_core(index, carry):
        i = index // 8
        j = (index // 2) % 4
        k = index % 2
        own[i, j, k] = (own[i, j, k].astype(F32) + got_core[i, j, k].astype(F32)).astype(BF16)
        return carry

    lax.fori_loop(0, 16, add_core, 0)
    by_x = send_to(own.at[1 - x, :, :, :, :half], got_x, sems, 0, other_x)
    by_y = send_to(own.at[:, :, 1 - y, :, half:], got_y, sems, 1, other_y)
    by_x.wait()

    def add_x(index, carry):
        j = index // 2
        k = index % 2
        own[x, j, k, :, :half] = (
            own[x, j, k, :, :half].astype(F32) + got_x[j, k].astype(F32)
        ).astype(BF16)
        return carry

    lax.fori_loop(0, 8, add_x, 0)
    next_y = send_to(own.at[x, :, 1 - y, :, :half], late_y, sems, 2, other_y)
    by_y.wait()

    def add_y(index, carry):
        i = index // 4
        j = index % 4
        own[i, j, y, :, half:] = (
            own[i, j, y, :, half:].astype(F32) + got_y[i, j].astype(F32)
        ).astype(BF16)
        return carry

    lax.fori_loop(0, 8, add_y, 0)
    next_x = send_to(own.at[1 - x, :, y, :, half:], late_x, sems, 3, other_x)
    next_y.wait()
    next_x.wait()

    def add_late(j, carry):
        own[x, j, y, :, :half] = (
            own[x, j, y, :, :half].astype(F32) + late_y[j].astype(F32)
        ).astype(BF16)
        own[x, j, y, :, half:] = (
            own[x, j, y, :, half:].astype(F32) + late_x[j].astype(F32)
        ).astype(BF16)
        return carry

    lax.fori_loop(0, 4, add_late, 0)
    last = [
        send_to(own.at[x, lax.rem(z + d + 1, 4), y], got_z.at[d], sems, 4 + d, along[d])
        for d in range(3)
    ]
    for copy in last:
        copy.wait()
    total = own[x, z, y].astype(F32)
    for d in range(3):
        total += got_z[d].astype(F32)
    out_ref[...] = total


def dense_sum(*parts):
    if not split_devices():
        every = ("dp", "ctx", "exp")
        sums = [lax.psum_scatter(part, every, scatter_dimension=0, tiled=True) for part in parts]
        return jnp.concatenate(sums, axis=1).astype(F32)
    rows = parts[0].shape[0] // 32
    starts = []
    columns = 0
    for part in parts:
        starts.append(columns)
        columns += part.shape[1]
    half = columns // 2 // LANES * LANES
    rest = columns - half
    return pl.pallas_call(
        functools.partial(dense_sum_kernel, tuple(starts)),
        in_specs=[pl.BlockSpec(memory_space=pl.ANY)] * len(parts),
        out_specs=pl.BlockSpec(memory_space=pltpu.VMEM),
        out_shape=jax.ShapeDtypeStruct((rows, columns), F32),
        scratch_shapes=[
            pltpu.VMEM((2, 4, 2, rows, columns), BF16),
            pltpu.VMEM((2, 4, 2, rows, columns), BF16),
            pltpu.VMEM((4, 2, rows, half), BF16),
            pltpu.VMEM((2, 4, rows, rest), BF16),
            pltpu.VMEM((4, rows, rest), BF16),
            pltpu.VMEM((4, rows, half), BF16),
            pltpu.VMEM((3, rows, columns), BF16),
            pltpu.SemaphoreType.DMA((len(parts),)),
            pltpu.SemaphoreType.DMA((7 + len(parts),)),
            pltpu.SemaphoreType.DMA((7 + len(parts),)),
        ],
        compiler_params=pltpu.CompilerParams(
            collective_id=1, has_side_effects=True, vmem_limit_bytes=48 * 1024 * 1024
        ),
        cost_estimate=pl.CostEstimate(
            flops=0, bytes_accessed=64 * 1536 * columns, transcendentals=0
        ),
    )(*[part.reshape(2, 4, 2, 2, rows, part.shape[1]) for part in parts])


def scatter_keys(grads, rows):
    count = lax.axis_size("ctx")
    place = lax.axis_index("ctx")

    def own(spot):
        return lax.dynamic_slice_in_dim(grads, jnp.maximum(spot, 0) * rows, rows, 0).astype(F32)

    got = jnp.zeros((rows, grads.shape[1]), F32)
    for step in range(1, count):
        send = (own(place - count + step) + got).astype(BF16)
        got = lax.ppermute(
            send, "ctx", [(i, i - 1) for i in range(count - step, count)]
        ).astype(F32)
    return own(place) + got


def experts_kernel(has_before, first_ref, h_ref, do_ref, code_ref, router_ref, weights, *refs):
    if has_before:
        back_before, mix_before = refs[:2]
        refs = refs[2:]
    refs = refs[len(refs) - 7 :]
    gh_ref, dgu_ref, back_ref, mix_ref, table, back_acc, mix_acc = refs
    expert = pl.program_id(0)
    chunk = pl.program_id(1)
    tokens = h_ref.shape[0]
    owners = weights.shape[0]
    rows = D // owners
    thin = FF // owners
    own = pl.ds(pl.multiple_of(chunk * tokens, tokens), tokens)
    lane = lax.broadcasted_iota(jnp.int32, (tokens, LANES), 1)
    codes = code_ref[...].astype(F32)

    @pl.when(expert == 0)
    def _():
        logits = jnp.dot(h_ref[...], router_ref[...], preferred_element_type=F32)
        routed = codes > 0.5
        top = jnp.max(jnp.where(routed, logits, NEGATIVE), axis=1, keepdims=True)
        terms = jnp.where(routed, jnp.exp(jnp.where(routed, logits - top, 0.0)), 0.0)
        shares = terms / jnp.sum(terms, axis=1, keepdims=True)
        table[own, :] = jnp.where(codes > 1.5, shares, 0.0)
        back_acc[own, :] = jnp.zeros((tokens, D), F32)
        mix_acc[own, :] = jnp.zeros((tokens, D), F32)

    mine = lane == first_ref[0] + expert
    kept = jnp.sum(jnp.where(mine, codes, 0.0), axis=1, keepdims=True) > 1.5
    gate = jnp.sum(jnp.where(mine, table[own, :], 0.0), axis=1, keepdims=True)
    gate_w = weights[:, 0, :rows].reshape(D, FF)
    up_w = weights[:, 0, rows : 2 * rows].reshape(D, FF)
    thirds = [
        weights[:, 0, 2 * rows + j * thin : 2 * rows + (j + 1) * thin].reshape(FF, FF)
        for j in range(D // FF)
    ]
    hidden_rows = h_ref[...]
    gated = jnp.dot(hidden_rows, gate_w, preferred_element_type=F32)
    upper = jnp.dot(hidden_rows, up_w, preferred_element_type=F32)
    grad_hidden = jnp.zeros((tokens, FF), F32)
    for j in range(D // FF):
        grad_hidden += lax.dot_general(
            do_ref[:, j * FF : (j + 1) * FF], thirds[j], NT, preferred_element_type=F32
        )
    sigma = 1.0 / (1.0 + jnp.exp(-gated))
    silu = gated * sigma
    hidden = silu * upper
    gated_hidden = (gate * hidden).astype(BF16)
    grad_gate = jnp.sum(grad_hidden * hidden, axis=1, keepdims=True)
    spot = lane == first_ref[0] + expert + LANES // 2
    table[own, :] += jnp.where(spot, jnp.where(kept, grad_gate, 0.0), 0.0)
    grad_hidden = gate * grad_hidden
    dg = (grad_hidden * upper * (sigma * (1.0 + gated * (1.0 - sigma)))).astype(BF16)
    du = (grad_hidden * silu).astype(BF16)
    gh_ref[...] = gated_hidden
    dgu_ref[:, :FF] = dg
    dgu_ref[:, FF:] = du
    for j in range(D // FF):
        cols = slice(j * FF, (j + 1) * FF)
        mix_acc[own, cols] += jnp.dot(gated_hidden, thirds[j], preferred_element_type=F32)
        back_acc[own, cols] += lax.dot_general(
            dg, gate_w[cols], NT, preferred_element_type=F32
        ) + lax.dot_general(du, up_w[cols], NT, preferred_element_type=F32)

    @pl.when(expert == pl.num_programs(0) - 1)
    def _():
        total = jnp.where(lane < LANES // 2, pltpu.roll(table[own, :], LANES // 2, 1), 0.0)
        coarse = total.astype(BF16)
        fine = total - coarse.astype(F32)
        grad_gates = coarse.astype(F32) + pltpu.roll(fine, LANES // 2, 1)
        if has_before:
            mix_ref[...] = (mix_acc[own, :] + mix_before[...].astype(F32)).astype(BF16)
            back_ref[:, :D] = (back_acc[own, :] + back_before[:, :D].astype(F32)).astype(BF16)
            back_ref[:, D:] = (grad_gates + back_before[:, D:].astype(F32)).astype(BF16)
        else:
            mix_ref[...] = mix_acc[own, :].astype(BF16)
            back_ref[:, :D] = back_acc[own, :].astype(BF16)
            back_ref[:, D:] = grad_gates.astype(BF16)


def run_experts(first, part, parts, second, known, first_w, weights, block, before, kept):
    tokens = second.shape[0]
    chunk = tokens // 2
    owners, experts, depth, _ = weights.shape
    last = experts - 1
    once = pl.Buffered(1)

    def final(e, c, *_):
        return (jnp.where(e == last, c, 0), 0)

    in_specs = [
        pl.BlockSpec((chunk, D), lambda e, c, *_: (c, 0)),
        pl.BlockSpec((chunk, D), lambda e, c, *_: (c, 0)),
        pl.BlockSpec((chunk, LANES), lambda e, c, *_: (c, D // LANES)),
        pl.BlockSpec((D, LANES), lambda e, c, *_: (0, block), pipeline_mode=once),
    ]
    in_specs.append(pl.BlockSpec((owners, 1, depth, FF), lambda e, c, *_: (0, e, 0, 0)))
    operands = [first, second, known, known, first_w, weights]
    if before:
        in_specs += [
            pl.BlockSpec((chunk, D + LANES), final, pipeline_mode=once),
            pl.BlockSpec((chunk, D), final, pipeline_mode=once),
        ]
        operands += list(before)
    aliases = {}
    if kept:
        in_specs += [pl.BlockSpec(memory_space=pl.ANY)] * 2
        aliases = {len(operands): 0, len(operands) + 1: 1}
        operands += list(kept)
    return pl.pallas_call(
        functools.partial(experts_kernel, bool(before)),
        grid_spec=pltpu.PrefetchScalarGridSpec(
            num_scalar_prefetch=1,
            grid=(experts, 2),
            in_specs=in_specs,
            out_specs=[
                pl.BlockSpec((chunk, FF), lambda e, c, *_: (2 * part + c, e)),
                pl.BlockSpec((chunk, 2 * FF), lambda e, c, *_: (2 * part + c, e)),
                pl.BlockSpec((chunk, D + LANES), final),
                pl.BlockSpec((chunk, D), final),
            ],
            scratch_shapes=[
                pltpu.VMEM((tokens, LANES), F32),
                pltpu.VMEM((tokens, D), F32),
                pltpu.VMEM((tokens, D), F32),
            ],
        ),
        out_shape=[
            jax.ShapeDtypeStruct((parts * tokens, experts * FF), BF16),
            jax.ShapeDtypeStruct((parts * tokens, experts * 2 * FF), BF16),
            jax.ShapeDtypeStruct((tokens, D + LANES), BF16),
            jax.ShapeDtypeStruct((tokens, D), BF16),
        ],
        input_output_aliases=aliases,
        compiler_params=pltpu.CompilerParams(vmem_limit_bytes=58 * 1024 * 1024),
        cost_estimate=pl.CostEstimate(
            flops=18 * tokens * D * FF * experts,
            bytes_accessed=tokens * D * 16,
            transcendentals=0,
        ),
    )(*operands)


def swap_core(block):
    return lax.ppermute(block, "exp", [(i, i ^ 1) for i in range(lax.axis_size("exp"))])


def swap_far(block):
    return lax.ppermute(block, "exp", [(i, i ^ 2) for i in range(lax.axis_size("exp"))])


def body(
    tokens,
    cotangent,
    doc_starts,
    routes,
    priority,
    attend_master,
    attend_mean,
    attend_square,
    outward_master,
    outward_mean,
    outward_square,
    router_master,
    router_mean,
    router_square,
    gains_master,
    gains_mean,
    gains_square,
    expand_master,
    expand_mean,
    expand_square,
    shrink_master,
    shrink_mean,
    shrink_square,
):
    local_low = tokens[0, 0]
    local_rows = local_low.astype(F32)
    rows_dev, width = local_rows.shape
    ctx_count = lax.axis_size("ctx")
    ctx_place = lax.axis_index("ctx")
    exp_count = lax.axis_size("exp")
    exp_place = lax.axis_index("exp")
    stream_len = rows_dev * ctx_count
    experts = router_master.shape[1]
    local_experts = experts // exp_count
    top_count = routes.shape[-1]
    capacity = rows_dev * top_count * 9 // (8 * experts)
    query_end = HEADS * HD
    qkv = (HEADS + 2 * KVH) * HD
    shard = attend_master.shape[0]

    attend_own = jnp.concatenate(
        [pair_heads(attend_master[:, :query_end], 1), attend_master[:, query_end:]], axis=1
    )
    rest = LANES - experts - 2
    first_own = jnp.concatenate(
        [attend_own, router_master, gains_master.T, jnp.zeros((shard, rest), F32)], axis=1
    ).astype(BF16)
    half = local_experts // 2
    packed = [
        pack_experts(
            expand_master[i : i + half].astype(BF16), shrink_master[i : i + half].astype(BF16)
        )
        for i in (0, half)
    ]
    front = lax.all_gather(packed[0], ("dp", "ctx"), axis=0, tiled=False)
    rear = lax.all_gather(packed[1], ("dp", "ctx"), axis=0, tiled=False)
    first_w, outward_w = dense_gather(first_own, pair_heads(outward_master, 0).T.astype(BF16))
    attend_w = first_w[:, :qkv]
    router_w = first_w[:, qkv : qkv + experts]
    gains_f = first_w[:, qkv + experts : qkv + experts + 2].T.astype(F32)

    codes = slot_codes(routes[0, 0], priority[0, 0, 0], experts, capacity)
    known = jnp.concatenate(
        [cotangent[0, 0], codes.astype(BF16), jnp.zeros((rows_dev, LANES - experts), BF16)], axis=1
    )
    known_core = swap_core(known)
    known_far = swap_far(known)
    known_last = swap_core(known_far)
    known_near = jnp.concatenate([known, known_core], axis=0)
    known_far = jnp.concatenate([known_far, known_last], axis=0)

    positions = ctx_place * rows_dev + jnp.arange(rows_dev, dtype=jnp.int32)
    all_positions = jnp.arange(stream_len, dtype=jnp.int32)
    starts = doc_starts[0, 0]
    first_pos = jnp.max(jnp.where(starts[None, :] <= positions[:, None], starts[None, :], 0), axis=1)
    place = jnp.stack([positions, first_pos], axis=0)
    sub_rows = min(256, rows_dev)
    key_rows = min(256, stream_len)
    sub_first = positions[::sub_rows]
    sub_last = positions[sub_rows - 1 :: sub_rows]
    low = first_pos[::sub_rows] // key_rows
    high = sub_last // key_rows + 1
    full_low = jnp.clip((first_pos[sub_rows - 1 :: sub_rows] + key_rows - 1) // key_rows, low, high)
    full_high = jnp.clip((sub_first + 1) // key_rows, full_low, high)
    bounds = jnp.stack([low, full_low, full_high, high], axis=1)
    tables = turn_tables(all_positions)
    own_tables = tuple(
        lax.dynamic_slice_in_dim(table, ctx_place * rows_dev, rows_dev, 0) for table in tables
    )
    queries, pairs, first_low = project(local_low, gains_f[0:1], first_w, *own_tables)
    key_pieces = [pairs]
    for step in range(ctx_count - 1):
        key_pieces.append(
            lax.ppermute(key_pieces[-1], "ctx", [(i, i + 1) for i in range(step, ctx_count - 1)])
        )
    key_owners = ctx_place - jnp.arange(ctx_count, dtype=jnp.int32)
    mixed_low, mixed_turned, log_total = attend_forward(
        bounds, key_owners, place, queries, key_pieces
    )
    branch = lax.dot_general(mixed_low, outward_w, NT, preferred_element_type=F32)
    middle = local_rows + branch
    second_norm, second_unit, second_scale = rms_forward(middle, gains_f[1])
    second_low = second_norm.astype(BF16)

    first_expert = jnp.reshape(exp_place * local_experts, (1,)).astype(jnp.int32)
    second_core = swap_core(second_low)
    second_far = swap_far(second_low)
    second_near = jnp.concatenate([second_low, second_core], axis=0)
    router_block = qkv // LANES

    def group(index, part, second, known, weights, before, kept):
        first = first_expert + index * half
        return run_experts(
            first, part, 2, second, known, first_w, weights, router_block, before, kept
        )

    def weight_grads(hidden, grad):
        contract = (((0,), (0,)), ((), ()))
        wide = lax.dot_general(second_all, grad, contract, preferred_element_type=F32)
        thin = lax.dot_general(hidden, grad_out_all, contract, preferred_element_type=F32)
        return (wide.astype(BF16), thin.astype(BF16).reshape(half, FF, width))

    def scatter(wide, thin):
        inner = ("dp", "ctx")
        wide = lax.psum_scatter(wide, inner, scatter_dimension=0, tiled=True)
        thin = lax.psum_scatter(thin, inner, scatter_dimension=1, tiled=True)
        wide = jnp.swapaxes(wide.reshape(-1, half, 2 * FF), 0, 1)
        return (wide.astype(F32), thin.astype(F32))

    *kept, back_near, mix_near = group(0, 0, second_near, known_near, front, (), ())
    second_last = swap_core(second_far)
    second_far = jnp.concatenate([second_far, second_last], axis=0)
    second_far = after(second_far, back_near)
    second_all = jnp.concatenate([second_near, second_far], axis=0)
    grad_out_all = jnp.concatenate([known_near[:, :width], known_far[:, :width]], axis=0)
    hidden, grad, back_far, mix_far = group(0, 1, second_far, known_far, front, (), kept)
    front_grads = weight_grads(hidden, grad)
    front_sums = scatter(*front_grads)
    second_far = after(second_far, *front_grads)
    *kept, back_far, mix_far = group(
        1, 1, second_far, known_far, rear, (back_far, mix_far), ()
    )
    across = back_far[:rows_dev].astype(F32) + swap_core(back_far[rows_dev:]).astype(F32)
    across = swap_far(across.astype(BF16))
    second_near = after(second_near, back_far)
    hidden, grad, back_near, mix_near = group(
        1, 0, second_near, known_near, rear, (back_near, mix_near), kept
    )
    row_grads = (
        back_near[:rows_dev].astype(F32)
        + swap_core(back_near[rows_dev:]).astype(F32)
        + across.astype(F32)
    )
    grad_gates = (
        row_grads[:, width : width + experts]
        + row_grads[:, width + LANES // 2 : width + LANES // 2 + experts]
    )
    rear_grads = weight_grads(hidden, after(grad, back_near))
    rear_sums = scatter(*rear_grads)
    mix_near, mix_far, row_grads = lax.optimization_barrier((mix_near, mix_far, row_grads))
    mix_core = swap_core(mix_near[rows_dev:])
    mixture = mix_far[:rows_dev].astype(F32) + swap_core(mix_far[rows_dev:]).astype(F32)
    mixture = swap_far(mixture.astype(BF16))
    row_grads = row_grads[:, :width]

    logits = jnp.dot(second_low, router_w, preferred_element_type=F32)
    gates = jax.nn.softmax(jnp.where(codes > 0, logits, NEGATIVE), axis=-1)
    gates = jnp.where(codes > 0, gates, 0.0)
    mean_term = jnp.sum(gates * grad_gates, axis=-1, keepdims=True)
    grad_logits = (gates * (grad_gates - mean_term)).astype(BF16)
    router_grad = jnp.einsum("td,te->de", second_low, grad_logits, preferred_element_type=F32)
    grad_second = row_grads + jnp.einsum(
        "te,de->td", grad_logits, router_w, preferred_element_type=F32
    )
    grad_middle_norm, gain_two_grad = rms_backward(
        grad_second, second_unit, second_scale, gains_f[1]
    )
    grad_middle = cotangent[0, 0].astype(F32) + grad_middle_norm
    grad_branch = grad_middle.astype(BF16)

    grad_mixed = jnp.dot(grad_branch, outward_w, preferred_element_type=F32).astype(BF16)
    grad_query, grad_keys, grad_values = attend_backward(
        bounds,
        key_owners,
        place,
        queries,
        grad_mixed,
        mixed_turned,
        log_total,
        key_pieces,
        tables,
        own_tables,
    )
    grad_pairs = jnp.concatenate([grad_keys, grad_values], axis=1)
    key_sum = scatter_keys(grad_pairs, rows_dev).astype(BF16)
    mixture, mix_core = lax.optimization_barrier((mixture, mix_core, key_sum))[:2]
    mixture = mixture.astype(F32) + mix_core.astype(F32) + mix_near[:rows_dev].astype(F32)
    output = (middle + mixture).astype(BF16)
    outward_grad = jnp.einsum("td,tc->dc", grad_branch, mixed_low, preferred_element_type=F32)
    grad_project = jnp.concatenate([grad_query, key_sum], axis=1)
    attend_grad = jnp.einsum("tc,tp->cp", first_low, grad_project, preferred_element_type=F32)
    grad_first = lax.dot_general(grad_project, attend_w, NT, preferred_element_type=F32)
    first_norm, first_unit, first_scale = rms_forward(local_rows, gains_f[0])
    grad_input_norm, gain_one_grad = rms_backward(grad_first, first_unit, first_scale, gains_f[0])
    input_grad = grad_middle + grad_input_norm
    thin_grad = jnp.concatenate(
        [
            router_grad.astype(BF16),
            jnp.stack([gain_one_grad, gain_two_grad], axis=1).astype(BF16),
            jnp.zeros((width, rest), BF16),
        ],
        axis=1,
    )
    first_sum = dense_sum(attend_grad.astype(BF16), thin_grad, outward_grad.astype(BF16))
    outward_sum = first_sum[:, qkv + LANES :]
    attend_sum = jnp.concatenate(
        [unpair_heads(first_sum[:, :query_end], 1), first_sum[:, query_end:qkv]], axis=1
    )
    router_sum = first_sum[:, qkv : qkv + experts]
    gains_sum = first_sum[:, qkv + experts : qkv + experts + 2].T
    outward_sum = unpair_heads(outward_sum.T, 0)
    expand_sum, shrink_sum = (
        jnp.concatenate(parts, axis=0)
        for parts in zip(front_sums, rear_sums)
    )
    attend_new = adam_update(
        attend_master, attend_mean, attend_square, attend_sum, D ** (-0.5), DECAY
    )
    outward_new = adam_update(
        outward_master, outward_mean, outward_square, outward_sum, 4.0 * D ** (-0.5), DECAY
    )
    router_new = adam_update(
        router_master, router_mean, router_square, router_sum, 0.5 * D ** (-0.5), DECAY
    )
    gains_new = adam_update(gains_master, gains_mean, gains_square, gains_sum, 0.6, 0.0)
    expand_new = adam_update(
        expand_master, expand_mean, expand_square, expand_sum, D ** (-0.5), DECAY
    )
    shrink_new = adam_update(
        shrink_master, shrink_mean, shrink_square, shrink_sum, (FF // 32) ** (-0.5), DECAY
    )
    return (
        output[None, None],
        input_grad[None, None],
        attend_new[0],
        attend_new[1],
        attend_new[2],
        attend_new[3],
        outward_new[0],
        outward_new[1],
        outward_new[2],
        outward_new[3],
        router_new[0],
        router_new[1],
        router_new[2],
        router_new[3],
        gains_new[0],
        gains_new[1],
        gains_new[2],
        gains_new[3],
        expand_new[0],
        expand_new[1],
        expand_new[2],
        expand_new[3],
        shrink_new[0],
        shrink_new[1],
        shrink_new[2],
        shrink_new[3],
    )


def solution(mesh):
    in_specs = (
        P("dp", "exp", "ctx", None),
        P("dp", "exp", "ctx", None),
        P("dp", "exp", None),
        P("dp", "exp", "ctx", None),
        P("dp", "exp", "ctx", None),
        P(("dp", "ctx", "exp"), None),
        P(("dp", "ctx", "exp"), None),
        P(("dp", "ctx", "exp"), None),
        P(None, ("dp", "ctx", "exp")),
        P(None, ("dp", "ctx", "exp")),
        P(None, ("dp", "ctx", "exp")),
        P(("dp", "ctx", "exp"), None),
        P(("dp", "ctx", "exp"), None),
        P(("dp", "ctx", "exp"), None),
        P(None, ("dp", "ctx", "exp")),
        P(None, ("dp", "ctx", "exp")),
        P(None, ("dp", "ctx", "exp")),
        P("exp", ("dp", "ctx"), None),
        P("exp", ("dp", "ctx"), None),
        P("exp", ("dp", "ctx"), None),
        P("exp", ("dp", "ctx"), None),
        P("exp", ("dp", "ctx"), None),
        P("exp", ("dp", "ctx"), None),
    )
    out_specs = (
        P("dp", "exp", "ctx", None),
        P("dp", "exp", "ctx", None),
        P(("dp", "ctx", "exp"), None),
        P(("dp", "ctx", "exp"), None),
        P(("dp", "ctx", "exp"), None),
        P(("dp", "ctx", "exp"), None),
        P(None, ("dp", "ctx", "exp")),
        P(None, ("dp", "ctx", "exp")),
        P(None, ("dp", "ctx", "exp")),
        P(None, ("dp", "ctx", "exp")),
        P(("dp", "ctx", "exp"), None),
        P(("dp", "ctx", "exp"), None),
        P(("dp", "ctx", "exp"), None),
        P(("dp", "ctx", "exp"), None),
        P(None, ("dp", "ctx", "exp")),
        P(None, ("dp", "ctx", "exp")),
        P(None, ("dp", "ctx", "exp")),
        P(None, ("dp", "ctx", "exp")),
        P("exp", ("dp", "ctx"), None),
        P("exp", ("dp", "ctx"), None),
        P("exp", ("dp", "ctx"), None),
        P("exp", ("dp", "ctx"), None),
        P("exp", ("dp", "ctx"), None),
        P("exp", ("dp", "ctx"), None),
        P("exp", ("dp", "ctx"), None),
        P("exp", ("dp", "ctx"), None),
    )
    return jax.shard_map(body, mesh=mesh, in_specs=in_specs, out_specs=out_specs, check_vma=False)
```

```python
import functools
import math

import jax
import jax.numpy as jnp
from jax import lax
from jax.experimental import pallas as pl
from jax.experimental.pallas import tpu as pltpu
from jax.sharding import PartitionSpec as P

D = 1536
HEADS = 24
KVH = 8
HD = 64
FF = 512
STEP = 10
GROUP = HEADS // KVH
PAIRS = KVH // 2
LANES = 2 * HD
SCALE = HD**-0.5


EPSILON = 1e-05
THETA = 10000.0
BETA_ONE = 0.9
BETA_TWO = 0.95
ADAM_EPSILON = 1e-08
DECAY = 0.1
NEGATIVE = -1e30
BF16 = jnp.bfloat16
F32 = jnp.float32
NT = (((1,), (1,)), ((), ()))


def rms_forward(values, gain_vec):
    scale_row = lax.rsqrt(jnp.mean(values * values, axis=-1, keepdims=True) + EPSILON)
    unit_rows = values * scale_row
    return (unit_rows * gain_vec, unit_rows, scale_row)


def rms_backward(grad_rows, unit_rows, scale_row, gain_vec):
    inner = grad_rows * gain_vec
    grad_values = scale_row * (
        inner - unit_rows * jnp.mean(inner * unit_rows, axis=-1, keepdims=True)
    )
    return (grad_values, jnp.sum(grad_rows * unit_rows, axis=0))


def adam_update(master, first_mom, second_mom, grad, rate, decay):
    first_new = BETA_ONE * first_mom + (1.0 - BETA_ONE) * grad
    second_new = BETA_TWO * second_mom + (1.0 - BETA_TWO) * grad * grad
    first_hat = first_new / (1.0 - BETA_ONE**STEP)
    second_hat = second_new / (1.0 - BETA_TWO**STEP)
    master_new = master - rate * (
        first_hat / (jnp.sqrt(second_hat) + ADAM_EPSILON) + decay * master
    )
    return (first_new, second_new, master_new, master_new.astype(jnp.bfloat16))


def pair_heads(block, axis):
    shape = block.shape
    split = shape[:axis] + (PAIRS, 2, GROUP, HD) + shape[axis + 1 :]
    return jnp.swapaxes(block.reshape(split), axis + 1, axis + 2).reshape(shape)


def unpair_heads(block, axis):
    shape = block.shape
    split = shape[:axis] + (PAIRS, GROUP, 2, HD) + shape[axis + 1 :]
    return jnp.swapaxes(block.reshape(split), axis + 1, axis + 2).reshape(shape)


def turn_tables(positions):
    half = HD // 2
    frequency = THETA ** (-jnp.arange(half, dtype=F32) / half)
    angles = positions.astype(F32)[:, None] * frequency[None, :]
    cosine = jnp.cos(angles)
    sine = jnp.sin(angles)
    return (
        jnp.concatenate([cosine] * 4, axis=1),
        jnp.concatenate([-sine, sine, -sine, sine], axis=1),
    )


def swap_halves(block):
    half = HD // 2
    lane = lax.broadcasted_iota(jnp.int32, block.shape, 1)
    ahead = pltpu.roll(block, LANES - half, 1)
    behind = pltpu.roll(block, half, 1)
    return jnp.where(lane % HD < half, ahead, behind)


def project_kernel(x_ref, gain_ref, w_ref, cos_ref, sin_ref, q_ref, kv_ref, h_ref):
    step = pl.program_id(0)
    query_tiles = HEADS * HD // 256
    key_tiles = KVH * HD // 256

    @pl.when(step == 0)
    def _():
        rows = x_ref[...].astype(F32)
        scale_row = lax.rsqrt(jnp.mean(rows * rows, axis=-1, keepdims=True) + EPSILON)
        h_ref[...] = (rows * scale_row * gain_ref[...]).astype(BF16)

    acc = jnp.dot(h_ref[...], w_ref[...], preferred_element_type=F32)

    def turned(half):
        part = acc[:, half * LANES : (half + 1) * LANES]
        return part * cos_ref[...] + swap_halves(part) * sin_ref[...]

    @pl.when(step < query_tiles)
    def _():
        for half in range(2):
            q_ref[:, half * LANES : (half + 1) * LANES] = (turned(half) * SCALE).astype(BF16)

    @pl.when((step >= query_tiles) & (step < query_tiles + key_tiles))
    def _():
        for half in range(2):
            kv_ref[:, half * LANES : (half + 1) * LANES] = turned(half).astype(BF16)

    @pl.when(step >= query_tiles + key_tiles)
    def _():
        kv_ref[...] = acc.astype(BF16)


def project(x, gain, weights, cosine, sine):
    rows = x.shape[0]
    query_tiles = HEADS * HD // 256
    tiles = (HEADS + 2 * KVH) * HD // 256
    return pl.pallas_call(
        project_kernel,
        grid=(tiles,),
        in_specs=[
            pl.BlockSpec((rows, D), lambda j: (0, 0)),
            pl.BlockSpec((1, D), lambda j: (0, 0)),
            pl.BlockSpec((D, 256), lambda j: (0, j)),
            pl.BlockSpec((rows, LANES), lambda j: (0, 0)),
            pl.BlockSpec((rows, LANES), lambda j: (0, 0)),
        ],
        out_specs=[
            pl.BlockSpec((rows, 256), lambda j: (0, jnp.minimum(j, query_tiles - 1))),
            pl.BlockSpec((rows, 256), lambda j: (0, jnp.maximum(j - query_tiles, 0))),
            pl.BlockSpec((rows, D), lambda j: (0, 0)),
        ],
        out_shape=[
            jax.ShapeDtypeStruct((rows, HEADS * HD), BF16),
            jax.ShapeDtypeStruct((rows, 2 * KVH * HD), BF16),
            jax.ShapeDtypeStruct((rows, D), BF16),
        ],
        compiler_params=pltpu.CompilerParams(vmem_limit_bytes=40 * 1024 * 1024),
        cost_estimate=pl.CostEstimate(
            flops=2 * rows * D * tiles * 256, bytes_accessed=D * tiles * 512, transcendentals=0
        ),
    )(x, gain, weights, cosine, sine)


def masked_pair(block):
    lane = lax.broadcasted_iota(jnp.int32, block.shape, 1)
    zero = jnp.zeros_like(block)
    return jnp.concatenate(
        [jnp.where(lane < HD, block, zero), jnp.where(lane >= HD, block, zero)], axis=0
    )


def chunk_flags(place, owner, sub_rows):
    rows = place.shape[1]
    start = owner * rows
    end = start + rows - 1
    first = place[:, ::sub_rows]
    last = place[:, sub_rows - 1 :: sub_rows]
    seen = (owner >= 0) & (start <= last[0]) & (end >= first[1])
    whole = (last[1] <= start) & (end <= first[0])
    return jnp.where(seen, jnp.where(whole, 2, 1), 0).astype(jnp.int32)


def allowed_keys(owner, key_rows, columns, place_ref):
    key_pos = owner * key_rows + lax.broadcasted_iota(jnp.int32, (key_rows, columns), 0)
    query_pos = jnp.concatenate([place_ref[0:1, :]] * 2, axis=1)
    first_pos = jnp.concatenate([place_ref[1:2, :]] * 2, axis=1)
    return (key_pos <= query_pos) & (key_pos >= first_pos)


def halves(index, rows):
    return slice(index * rows, (index + 1) * rows)


def attend_kernel(first, final, flag_ref, owner_ref, place_ref, q_ref, k_ref, v_ref, *refs):
    sub = pl.program_id(1)
    rows = q_ref.shape[0]
    key_rows = k_ref.shape[0]
    columns = 2 * rows
    if first:
        before = None
    else:
        before, refs = refs[:3], refs[3:]
    outs, (top, total, acc) = refs[:3], refs[3:]
    for r in range(GROUP):
        if first:
            top[r] = jnp.full((1, columns), NEGATIVE, F32)
            total[r] = jnp.zeros((1, columns), F32)
            acc[r] = jnp.zeros((LANES, columns), F32)
        else:
            acc[r] = jnp.zeros((LANES, columns), F32)
            for i in range(2):
                cols = halves(i, rows)
                head = slice(2 * r + i, 2 * r + i + 1)
                top[r, :, cols] = before[0][0, head, :]
                total[r, :, cols] = before[1][0, head, :]
                acc[r, halves(i, HD), cols] = before[2][0, r, halves(i, HD), :]

    def update(masked):
        keys = k_ref[...]
        turned = v_ref[...].astype(F32).T.astype(BF16)
        if masked:
            allowed = allowed_keys(owner_ref[0], key_rows, columns, place_ref)
        for r in range(GROUP):
            queries = masked_pair(q_ref[:, r * LANES : (r + 1) * LANES])
            scores = lax.dot_general(keys, queries, NT, preferred_element_type=F32)
            if masked:
                scores = jnp.where(allowed, scores, NEGATIVE)
            old = top[r]
            now = jnp.maximum(old, jnp.max(scores, axis=0, keepdims=True))
            shrinking = jnp.exp(old - now)
            terms = jnp.exp(scores - now)
            top[r] = now
            total[r] = total[r] * shrinking + jnp.sum(terms, axis=0, keepdims=True)
            acc[r] = acc[r] * shrinking + jnp.dot(
                turned, terms.astype(BF16), preferred_element_type=F32
            )

    @pl.when(flag_ref[sub] == 1)
    def _():
        update(True)

    @pl.when(flag_ref[sub] == 2)
    def _():
        update(False)

    for r in range(GROUP):
        mixed = acc[r] / total[r] if final else acc[r]
        both = jnp.concatenate([mixed[:HD, :rows], mixed[HD:, rows:]], axis=0)
        if final:
            lse = top[r] + jnp.log(total[r])
        for i in range(2):
            head = slice(2 * r + i, 2 * r + i + 1)
            if final:
                outs[1][0, head, :] = lse[:, halves(i, rows)]
            else:
                outs[0][0, head, :] = top[r, :, halves(i, rows)]
                outs[1][0, head, :] = total[r, :, halves(i, rows)]
        outs[2][0, r] = both
        if final:
            outs[0][:, r * LANES : (r + 1) * LANES] = both.T.astype(BF16)


def head_specs(rows, sub_rows):
    line = pl.BlockSpec((1, 2 * GROUP, sub_rows), lambda p, s, *_: (p, 0, s))
    turned = pl.BlockSpec((1, GROUP, LANES, sub_rows), lambda p, s, *_: (p, 0, 0, s))
    wide = pl.BlockSpec((sub_rows, GROUP * LANES), lambda p, s, *_: (s, p))
    line_shape = jax.ShapeDtypeStruct((PAIRS, 2 * GROUP, rows), F32)
    turned_shape = jax.ShapeDtypeStruct((PAIRS, GROUP, LANES, rows), F32)
    wide_shape = jax.ShapeDtypeStruct((rows, HEADS * HD), BF16)
    return (line, turned, wide, line_shape, turned_shape, wide_shape)


def attend_forward(place, owner, q, piece, before, final):
    rows = q.shape[0]
    sub_rows = min(256, rows)
    columns = 2 * sub_rows
    line, turned, wide, line_shape, turned_shape, wide_shape = head_specs(rows, sub_rows)
    return pl.pallas_call(
        functools.partial(attend_kernel, not before, final),
        grid_spec=pltpu.PrefetchScalarGridSpec(
            num_scalar_prefetch=2,
            grid=(PAIRS, rows // sub_rows),
            in_specs=[
                pl.BlockSpec((2, sub_rows), lambda p, s, *_: (0, s)),
                wide,
                pl.BlockSpec((rows, LANES), lambda p, s, *_: (0, p)),
                pl.BlockSpec((rows, LANES), lambda p, s, *_: (0, PAIRS + p)),
                *([line, line, turned] if before else []),
            ],
            out_specs=[wide, line, turned] if final else [line, line, turned],
            scratch_shapes=[
                pltpu.VMEM((GROUP, 1, columns), F32),
                pltpu.VMEM((GROUP, 1, columns), F32),
                pltpu.VMEM((GROUP, LANES, columns), F32),
            ],
        ),
        out_shape=[wide_shape if final else line_shape, line_shape, turned_shape],
        compiler_params=pltpu.CompilerParams(vmem_limit_bytes=40 * 1024 * 1024),
        cost_estimate=pl.CostEstimate(
            flops=40 * rows * rows * D, bytes_accessed=8 * rows * D, transcendentals=0
        ),
    )(chunk_flags(place, owner, sub_rows), owner[None], place, q, piece, piece, *before)


def delta_kernel(do_ref, ot_ref, delta_ref):
    for r in range(GROUP):
        product = do_ref[:, r * LANES : (r + 1) * LANES].astype(F32).T * ot_ref[0, r]
        for i in range(2):
            delta_ref[0, 2 * r + i : 2 * r + i + 1, :] = jnp.sum(
                product[halves(i, HD)], axis=0, keepdims=True
            )


def row_deltas(do, ot):
    rows = do.shape[0]
    line, turned, wide, line_shape, _, _ = head_specs(rows, rows)
    return pl.pallas_call(
        delta_kernel,
        grid=(PAIRS, 1),
        in_specs=[wide, turned],
        out_specs=line,
        out_shape=line_shape,
        cost_estimate=pl.CostEstimate(
            flops=2 * rows * D, bytes_accessed=6 * rows * D, transcendentals=0
        ),
    )(do, ot)


def attend_back_kernel(
    first,
    final,
    flag_ref,
    owner_ref,
    place_ref,
    q_ref,
    do_ref,
    lse_ref,
    delta_ref,
    k_ref,
    v_ref,
    cos_ref,
    sin_ref,
    own_cos_ref,
    own_sin_ref,
    *refs,
):
    sub = pl.program_id(1)
    rows = q_ref.shape[0]
    key_rows = k_ref.shape[0]
    columns = 2 * rows
    if not first:
        before = refs[0]
    grad_ref, pair_ref, acc, dk, dv = refs[len(refs) - 5 :]

    @pl.when(sub == 0)
    def _():
        dk[...] = jnp.zeros(dk.shape, F32)
        dv[...] = jnp.zeros(dv.shape, F32)

    acc[...] = jnp.zeros(acc.shape, F32)
    if not first:
        for r in range(GROUP):
            for i in range(2):
                acc[r, halves(i, HD), halves(i, rows)] = before[0, r, halves(i, HD), :]

    def update(masked):
        keys = k_ref[...]
        values = v_ref[...]
        turned = keys.astype(F32).T.astype(BF16)
        key_grad = dk[...]
        value_grad = dv[...]
        if masked:
            allowed = allowed_keys(owner_ref[0], key_rows, columns, place_ref)
        for r in range(GROUP):
            lanes = slice(r * LANES, (r + 1) * LANES)
            queries = masked_pair(q_ref[:, lanes])
            grads = masked_pair(do_ref[:, lanes])
            heads = [slice(2 * r + i, 2 * r + i + 1) for i in range(2)]
            lse = jnp.concatenate([lse_ref[0, head, :] for head in heads], axis=1)
            delta = jnp.concatenate([delta_ref[0, head, :] for head in heads], axis=1)
            scores = lax.dot_general(keys, queries, NT, preferred_element_type=F32)
            probs = jnp.exp(scores - lse)
            if masked:
                probs = jnp.where(allowed, probs, 0.0)
            value_grad += jnp.dot(probs.astype(BF16), grads, preferred_element_type=F32)
            prob_grad = lax.dot_general(values, grads, NT, preferred_element_type=F32)
            score_grad = (probs * (prob_grad - delta)).astype(BF16)
            key_grad += jnp.dot(score_grad, queries, preferred_element_type=F32)
            acc[r] += jnp.dot(turned, score_grad, preferred_element_type=F32)
        dk[...] = key_grad
        dv[...] = value_grad

    @pl.when(flag_ref[sub] == 1)
    def _():
        update(True)

    @pl.when(flag_ref[sub] == 2)
    def _():
        update(False)

    for r in range(GROUP):
        both = jnp.concatenate([acc[r, :HD, :rows], acc[r, HD:, rows:]], axis=0)
        if final:
            grad = both.T * SCALE
            grad = grad * own_cos_ref[...] - swap_halves(grad) * own_sin_ref[...]
            grad_ref[:, r * LANES : (r + 1) * LANES] = grad.astype(BF16)
        else:
            grad_ref[0, r] = both

    @pl.when(sub == pl.num_programs(1) - 1)
    def _():
        pair_ref[0] = (dk[...] * cos_ref[...] - swap_halves(dk[...]) * sin_ref[...]).astype(BF16)
        pair_ref[1] = dv[...].astype(BF16)


def attend_backward(
    place, owner, q, do, lse, delta, piece, tables, own_tables, before, final, tie
):
    rows = q.shape[0]
    sub_rows = min(256, rows)
    columns = 2 * sub_rows
    line, turned, wide, _, turned_shape, wide_shape = head_specs(rows, sub_rows)
    far = pl.BlockSpec((rows, LANES), lambda p, s, flags, own: (jnp.maximum(own[0], 0), 0))
    near = pl.BlockSpec((sub_rows, LANES), lambda p, s, *_: (s, 0))
    return pl.pallas_call(
        functools.partial(attend_back_kernel, not before, final),
        grid_spec=pltpu.PrefetchScalarGridSpec(
            num_scalar_prefetch=2,
            grid=(PAIRS, rows // sub_rows),
            in_specs=[
                pl.BlockSpec((2, sub_rows), lambda p, s, *_: (0, s)),
                wide,
                wide,
                line,
                line,
                pl.BlockSpec((rows, LANES), lambda p, s, *_: (0, p)),
                pl.BlockSpec((rows, LANES), lambda p, s, *_: (0, PAIRS + p)),
                far,
                far,
                near,
                near,
                *([turned] if before else []),
                *([pl.BlockSpec(memory_space=pl.ANY)] * len(tie)),
            ],
            out_specs=[
                wide if final else turned,
                pl.BlockSpec((2, rows, LANES), lambda p, s, *_: (0, 0, p)),
            ],
            scratch_shapes=[
                pltpu.VMEM((GROUP, LANES, columns), F32),
                pltpu.VMEM((rows, LANES), F32),
                pltpu.VMEM((rows, LANES), F32),
            ],
        ),
        out_shape=[
            wide_shape if final else turned_shape,
            jax.ShapeDtypeStruct((2, rows, KVH * HD), BF16),
        ],
        compiler_params=pltpu.CompilerParams(vmem_limit_bytes=40 * 1024 * 1024),
        cost_estimate=pl.CostEstimate(
            flops=60 * rows * rows * D, bytes_accessed=8 * rows * D, transcendentals=0
        ),
    )(
        chunk_flags(place, owner, sub_rows),
        owner[None],
        place,
        q,
        do,
        lse,
        delta,
        piece,
        piece,
        *tables,
        *own_tables,
        *before,
        *tie,
    )


def slot_codes(route_ids, priority_row, experts, capacity):
    rows, top_count = route_ids.shape
    ranks = priority_row.reshape(rows, top_count)
    routed = route_ids[:, :, None] == jnp.arange(experts, dtype=jnp.int32)[None, None, :]
    unused = rows * top_count
    rank = jnp.min(jnp.where(routed, ranks[:, :, None], unused), axis=1).T
    earlier = jnp.sum((rank[:, None, :] < rank[:, :, None]).astype(jnp.int32), axis=2)
    return jnp.where(rank < unused, jnp.where(earlier < capacity, 2, 1), 0).T


def pack_experts(expand, shrink):
    parts = [expand[:, :, :FF], expand[:, :, FF:]]
    parts += [shrink[:, :, j * FF : (j + 1) * FF] for j in range(D // FF)]
    return jnp.concatenate(parts, axis=1)


def after(value, *others):
    return lax.optimization_barrier((value, *others))[0]


def split_devices():
    return (lax.axis_size("dp"), lax.axis_size("ctx"), lax.axis_size("exp")) == (2, 4, 4)


def greet(partners):
    barrier = pltpu.get_barrier_semaphore()
    for partner in partners:
        pl.semaphore_signal(
            barrier, inc=1, device_id=partner, device_id_type=pl.DeviceIdType.MESH
        )
    pl.semaphore_wait(barrier, len(partners))


def neighbours():
    x = lax.axis_index("dp")
    z = lax.axis_index("ctx")
    spot = lax.axis_index("exp")
    y = spot // 2
    core = spot % 2
    other_core = {"exp": 2 * y + 1 - core}
    other_x = {"dp": 1 - x}
    other_y = {"exp": 2 * (1 - y) + core}
    along = [{"ctx": lax.rem(z + d, 4)} for d in range(1, 4)]
    return (x, y, z, core, other_core, other_x, other_y, along)


def send_to(source, target, sems, number, device):
    copy = pltpu.make_async_remote_copy(
        src_ref=source,
        dst_ref=target,
        send_sem=sems[0].at[number],
        recv_sem=sems[1].at[number],
        device_id=device,
        device_id_type=pl.DeviceIdType.MESH,
    )
    copy.start()
    return copy


def dense_gather_kernel(first_ref, second_ref, all_first, all_second, local_sem, *sems):
    x, y, z, core, other_core, other_x, other_y, along = neighbours()
    greet([other_core, other_x, other_y] + along)
    spread = [
        (
            send_to(first_ref, all_first.at[x, z, y, core], sems, 2 * d, along[d]),
            send_to(second_ref, all_second.at[x, z, y, core], sems, 2 * d + 1, along[d]),
        )
        for d in range(3)
    ]
    local = [
        pltpu.make_async_copy(first_ref, all_first.at[x, z, y, core], local_sem.at[0]),
        pltpu.make_async_copy(second_ref, all_second.at[x, z, y, core], local_sem.at[1]),
    ]
    for copy in local:
        copy.start()
    steps = [[], [], []]

    def send_near(index):
        if index == 0:
            for copy in local:
                copy.wait()
        else:
            for copy in spread[index - 1]:
                copy.wait_recv()
        spot = lax.rem(z - index + 4, 4)
        base = 6 + 6 * index
        block = all_first.at[x, spot, y, core]
        other = all_second.at[x, spot, y, core]
        steps[0].append(
            (
                send_to(block, block, sems, base, other_y),
                send_to(other, other, sems, base + 1, other_x),
            )
        )

    def send_far(index):
        for copy in steps[0][index]:
            copy.wait_recv()
        spot = lax.rem(z - index + 4, 4)
        base = 6 + 6 * index
        block = all_first.at[x, spot, :, core]
        other = all_second.at[:, spot, y, core]
        steps[1].append(
            (
                send_to(block, block, sems, base + 2, other_x),
                send_to(other, other, sems, base + 3, other_y),
            )
        )

    def send_core(index):
        for copy in steps[1][index]:
            copy.wait_recv()
        spot = lax.rem(z - index + 4, 4)
        base = 6 + 6 * index
        block = all_first.at[:, spot, :, core]
        other = all_second.at[:, spot, :, core]
        steps[2].append(
            (
                send_to(block, block, sems, base + 4, other_core),
                send_to(other, other, sems, base + 5, other_core),
            )
        )

    send_near(0)
    send_far(0)
    send_near(1)
    send_core(0)
    send_far(1)
    send_near(2)
    send_core(1)
    send_far(2)
    send_near(3)
    send_core(2)
    send_far(3)
    send_core(3)
    for pair in steps[2]:
        for copy in pair:
            copy.wait_recv()
    for pair in spread + steps[0] + steps[1] + steps[2]:
        for copy in pair:
            copy.wait_send()


def dense_gather(first, second):
    if not split_devices():
        every = ("dp", "ctx", "exp")
        return tuple(
            lax.all_gather(part, every, axis=0, tiled=True) for part in (first, second)
        )
    shapes = [(2, 4, 2, 2) + part.shape for part in (first, second)]
    gathered = pl.pallas_call(
        dense_gather_kernel,
        in_specs=[pl.BlockSpec(memory_space=pl.ANY)] * 2,
        out_specs=[pl.BlockSpec(memory_space=pl.ANY)] * 2,
        out_shape=[jax.ShapeDtypeStruct(shape, BF16) for shape in shapes],
        scratch_shapes=[
            pltpu.SemaphoreType.DMA((2,)),
            pltpu.SemaphoreType.DMA((30,)),
            pltpu.SemaphoreType.DMA((30,)),
        ],
        compiler_params=pltpu.CompilerParams(collective_id=2, has_side_effects=True),
        cost_estimate=pl.CostEstimate(
            flops=0, bytes_accessed=64 * (first.size + second.size), transcendentals=0
        ),
    )(first, second)
    return tuple(part.reshape(-1, part.shape[-1]) for part in gathered)


def dense_sum_kernel(starts, *refs):
    count = len(starts)
    parts = refs[:count]
    (
        out_ref,
        own,
        got_core,
        got_x,
        got_y,
        late_x,
        late_y,
        got_z,
        load_sem,
        send_sem,
        recv_sem,
    ) = refs[count:]
    x, y, z, core, other_core, other_x, other_y, along = neighbours()
    half = got_x.shape[-1]
    greet([other_core, other_x, other_y] + along)
    sems = (send_sem, recv_sem)
    first = []
    loads = []
    for index in range(count):
        columns = slice(starts[index], starts[index] + parts[index].shape[-1])
        first.append(
            send_to(
                parts[index].at[:, :, :, 1 - core],
                got_core.at[:, :, :, :, columns],
                sems,
                7 + index,
                other_core,
            )
        )
        loads.append(
            pltpu.make_async_copy(
                parts[index].at[:, :, :, core], own.at[:, :, :, :, columns], load_sem.at[index]
            )
        )
    for copy in loads:
        copy.start()
    for copy in loads + first:
        copy.wait()

    def add_core(index, carry):
        i = index // 8
        j = (index // 2) % 4
        k = index % 2
        own[i, j, k] = (own[i, j, k].astype(F32) + got_core[i, j, k].astype(F32)).astype(BF16)
        return carry

    lax.fori_loop(0, 16, add_core, 0)
    by_x = send_to(own.at[1 - x, :, :, :, :half], got_x, sems, 0, other_x)
    by_y = send_to(own.at[:, :, 1 - y, :, half:], got_y, sems, 1, other_y)
    by_x.wait()

    def add_x(index, carry):
        j = index // 2
        k = index % 2
        own[x, j, k, :, :half] = (
            own[x, j, k, :, :half].astype(F32) + got_x[j, k].astype(F32)
        ).astype(BF16)
        return carry

    lax.fori_loop(0, 8, add_x, 0)
    next_y = send_to(own.at[x, :, 1 - y, :, :half], late_y, sems, 2, other_y)
    by_y.wait()

    def add_y(index, carry):
        i = index // 4
        j = index % 4
        own[i, j, y, :, half:] = (
            own[i, j, y, :, half:].astype(F32) + got_y[i, j].astype(F32)
        ).astype(BF16)
        return carry

    lax.fori_loop(0, 8, add_y, 0)
    next_x = send_to(own.at[1 - x, :, y, :, half:], late_x, sems, 3, other_x)
    next_y.wait()
    next_x.wait()

    def add_late(j, carry):
        own[x, j, y, :, :half] = (
            own[x, j, y, :, :half].astype(F32) + late_y[j].astype(F32)
        ).astype(BF16)
        own[x, j, y, :, half:] = (
            own[x, j, y, :, half:].astype(F32) + late_x[j].astype(F32)
        ).astype(BF16)
        return carry

    lax.fori_loop(0, 4, add_late, 0)
    last = [
        send_to(own.at[x, lax.rem(z + d + 1, 4), y], got_z.at[d], sems, 4 + d, along[d])
        for d in range(3)
    ]
    for copy in last:
        copy.wait()
    total = own[x, z, y].astype(F32)
    for d in range(3):
        total += got_z[d].astype(F32)
    out_ref[...] = total


def dense_sum(*parts):
    if not split_devices():
        every = ("dp", "ctx", "exp")
        sums = [lax.psum_scatter(part, every, scatter_dimension=0, tiled=True) for part in parts]
        return jnp.concatenate(sums, axis=1).astype(F32)
    rows = parts[0].shape[0] // 32
    starts = []
    columns = 0
    for part in parts:
        starts.append(columns)
        columns += part.shape[1]
    half = columns // 2 // LANES * LANES
    rest = columns - half
    return pl.pallas_call(
        functools.partial(dense_sum_kernel, tuple(starts)),
        in_specs=[pl.BlockSpec(memory_space=pl.ANY)] * len(parts),
        out_specs=pl.BlockSpec(memory_space=pltpu.VMEM),
        out_shape=jax.ShapeDtypeStruct((rows, columns), F32),
        scratch_shapes=[
            pltpu.VMEM((2, 4, 2, rows, columns), BF16),
            pltpu.VMEM((2, 4, 2, rows, columns), BF16),
            pltpu.VMEM((4, 2, rows, half), BF16),
            pltpu.VMEM((2, 4, rows, rest), BF16),
            pltpu.VMEM((4, rows, rest), BF16),
            pltpu.VMEM((4, rows, half), BF16),
            pltpu.VMEM((3, rows, columns), BF16),
            pltpu.SemaphoreType.DMA((len(parts),)),
            pltpu.SemaphoreType.DMA((7 + len(parts),)),
            pltpu.SemaphoreType.DMA((7 + len(parts),)),
        ],
        compiler_params=pltpu.CompilerParams(
            collective_id=1, has_side_effects=True, vmem_limit_bytes=48 * 1024 * 1024
        ),
        cost_estimate=pl.CostEstimate(
            flops=0, bytes_accessed=64 * 1536 * columns, transcendentals=0
        ),
    )(*[part.reshape(2, 4, 2, 2, rows, part.shape[1]) for part in parts])


def experts_kernel(has_before, first_ref, h_ref, do_ref, code_ref, router_ref, weights, *refs):
    if has_before:
        back_before, tail_before, mix_before = refs[:3]
        refs = refs[3:]
    refs = refs[len(refs) - 7 :]
    gh_ref, dgu_ref, back_ref, mix_ref, table, back_acc, mix_acc = refs
    expert = pl.program_id(0)
    chunk = pl.program_id(1)
    tokens = h_ref.shape[0]
    owners = weights.shape[0]
    rows = D // owners
    thin = FF // owners
    own = pl.ds(pl.multiple_of(chunk * tokens, tokens), tokens)
    lane = lax.broadcasted_iota(jnp.int32, (tokens, LANES), 1)
    codes = code_ref[...].astype(F32)

    @pl.when(expert == 0)
    def _():
        logits = jnp.dot(h_ref[...], router_ref[...], preferred_element_type=F32)
        routed = codes > 0.5
        top = jnp.max(jnp.where(routed, logits, NEGATIVE), axis=1, keepdims=True)
        terms = jnp.where(routed, jnp.exp(jnp.where(routed, logits - top, 0.0)), 0.0)
        shares = terms / jnp.sum(terms, axis=1, keepdims=True)
        table[own, :] = jnp.where(codes > 1.5, shares, 0.0)
        if has_before:
            back_acc[own, :] = back_before[...].astype(F32)
            mix_acc[own, :] = mix_before[...].astype(F32)
        else:
            back_acc[own, :] = jnp.zeros((tokens, D), F32)
            mix_acc[own, :] = jnp.zeros((tokens, D), F32)

    mine = lane == first_ref[0] + expert
    kept = jnp.sum(jnp.where(mine, codes, 0.0), axis=1, keepdims=True) > 1.5
    gate = jnp.sum(jnp.where(mine, table[own, :], 0.0), axis=1, keepdims=True)
    gate_w = weights[:, 0, :rows].reshape(D, FF)
    up_w = weights[:, 0, rows : 2 * rows].reshape(D, FF)
    thirds = [
        weights[:, 0, 2 * rows + j * thin : 2 * rows + (j + 1) * thin].reshape(FF, FF)
        for j in range(D // FF)
    ]
    hidden_rows = h_ref[...]
    gated = jnp.dot(hidden_rows, gate_w, preferred_element_type=F32)
    upper = jnp.dot(hidden_rows, up_w, preferred_element_type=F32)
    grad_hidden = jnp.zeros((tokens, FF), F32)
    for j in range(D // FF):
        grad_hidden += lax.dot_general(
            do_ref[:, j * FF : (j + 1) * FF], thirds[j], NT, preferred_element_type=F32
        )
    sigma = 1.0 / (1.0 + jnp.exp(-gated))
    silu = gated * sigma
    hidden = silu * upper
    gated_hidden = (gate * hidden).astype(BF16)
    grad_gate = jnp.sum(grad_hidden * hidden, axis=1, keepdims=True)
    spot = lane == first_ref[0] + expert + LANES // 2
    table[own, :] += jnp.where(spot, jnp.where(kept, grad_gate, 0.0), 0.0)
    grad_hidden = gate * grad_hidden
    dg = (grad_hidden * upper * (sigma * (1.0 + gated * (1.0 - sigma)))).astype(BF16)
    du = (grad_hidden * silu).astype(BF16)
    gh_ref[...] = gated_hidden
    dgu_ref[:, :FF] = dg
    dgu_ref[:, FF:] = du
    for j in range(D // FF):
        cols = slice(j * FF, (j + 1) * FF)
        mix_acc[own, cols] += jnp.dot(gated_hidden, thirds[j], preferred_element_type=F32)
        back_acc[own, cols] += lax.dot_general(
            dg, gate_w[cols], NT, preferred_element_type=F32
        ) + lax.dot_general(du, up_w[cols], NT, preferred_element_type=F32)

    @pl.when(expert == pl.num_programs(0) - 1)
    def _():
        total = jnp.where(lane < LANES // 2, pltpu.roll(table[own, :], LANES // 2, 1), 0.0)
        coarse = total.astype(BF16)
        fine = total - coarse.astype(F32)
        grad_gates = coarse.astype(F32) + pltpu.roll(fine, LANES // 2, 1)
        if has_before:
            grad_gates += tail_before[...].astype(F32)
        mix_ref[...] = mix_acc[own, :].astype(BF16)
        back_ref[:, :D] = back_acc[own, :].astype(BF16)
        back_ref[:, D:] = grad_gates.astype(BF16)


def run_experts(first, part, parts, second, known, first_w, weights, block, before, kept, tie):
    tokens = second.shape[0]
    chunk = tokens // 2
    owners, experts, depth, _ = weights.shape
    last = experts - 1
    once = pl.Buffered(1)

    def final(e, c, *_):
        return (jnp.where(e == last, c, 0), 0)

    def initial(e, c, *_):
        return (jnp.where(e == 0, c, 1), 0)

    in_specs = [
        pl.BlockSpec((chunk, D), lambda e, c, *_: (c, 0)),
        pl.BlockSpec((chunk, D), lambda e, c, *_: (c, 0)),
        pl.BlockSpec((chunk, LANES), lambda e, c, *_: (c, D // LANES)),
        pl.BlockSpec((D, LANES), lambda e, c, *_: (0, block), pipeline_mode=once),
    ]
    in_specs.append(pl.BlockSpec((owners, 1, depth, FF), lambda e, c, *_: (0, e, 0, 0)))
    operands = [first, second, known, known, first_w, weights]
    if before:
        in_specs += [
            pl.BlockSpec((chunk, D), initial),
            pl.BlockSpec((chunk, LANES), lambda e, c, *_: (c, D // LANES)),
            pl.BlockSpec((chunk, D), initial),
        ]
        operands += [before[0], before[0], before[1]]
    in_specs += [pl.BlockSpec(memory_space=pl.ANY)] * len(tie)
    operands += list(tie)
    aliases = {}
    if kept:
        in_specs += [pl.BlockSpec(memory_space=pl.ANY)] * 2
        aliases = {len(operands): 0, len(operands) + 1: 1}
        operands += list(kept)
    return pl.pallas_call(
        functools.partial(experts_kernel, bool(before)),
        grid_spec=pltpu.PrefetchScalarGridSpec(
            num_scalar_prefetch=1,
            grid=(experts, 2),
            in_specs=in_specs,
            out_specs=[
                pl.BlockSpec((chunk, FF), lambda e, c, *_: (2 * part + c, e)),
                pl.BlockSpec((chunk, 2 * FF), lambda e, c, *_: (2 * part + c, e)),
                pl.BlockSpec((chunk, D + LANES), final),
                pl.BlockSpec((chunk, D), final),
            ],
            scratch_shapes=[
                pltpu.VMEM((tokens, LANES), F32),
                pltpu.VMEM((tokens, D), F32),
                pltpu.VMEM((tokens, D), F32),
            ],
        ),
        out_shape=[
            jax.ShapeDtypeStruct((parts * tokens, experts * FF), BF16),
            jax.ShapeDtypeStruct((parts * tokens, experts * 2 * FF), BF16),
            jax.ShapeDtypeStruct((tokens, D + LANES), BF16),
            jax.ShapeDtypeStruct((tokens, D), BF16),
        ],
        input_output_aliases=aliases,
        compiler_params=pltpu.CompilerParams(vmem_limit_bytes=58 * 1024 * 1024),
        cost_estimate=pl.CostEstimate(
            flops=18 * tokens * D * FF * experts,
            bytes_accessed=tokens * D * 16,
            transcendentals=0,
        ),
    )(*operands)


def swap_core(block):
    return lax.ppermute(block, "exp", [(i, i ^ 1) for i in range(lax.axis_size("exp"))])


def swap_far(block):
    return lax.ppermute(block, "exp", [(i, i ^ 2) for i in range(lax.axis_size("exp"))])


def body(
    tokens,
    cotangent,
    doc_starts,
    routes,
    priority,
    attend_master,
    attend_mean,
    attend_square,
    outward_master,
    outward_mean,
    outward_square,
    router_master,
    router_mean,
    router_square,
    gains_master,
    gains_mean,
    gains_square,
    expand_master,
    expand_mean,
    expand_square,
    shrink_master,
    shrink_mean,
    shrink_square,
):
    local_low = tokens[0, 0]
    local_rows = local_low.astype(F32)
    rows_dev, width = local_rows.shape
    ctx_count = lax.axis_size("ctx")
    ctx_place = lax.axis_index("ctx")
    exp_count = lax.axis_size("exp")
    exp_place = lax.axis_index("exp")
    stream_len = rows_dev * ctx_count
    experts = router_master.shape[1]
    local_experts = experts // exp_count
    top_count = routes.shape[-1]
    capacity = rows_dev * top_count * 9 // (8 * experts)
    query_end = HEADS * HD
    qkv = (HEADS + 2 * KVH) * HD
    shard = attend_master.shape[0]

    attend_own = jnp.concatenate(
        [pair_heads(attend_master[:, :query_end], 1), attend_master[:, query_end:]], axis=1
    )
    rest = LANES - experts - 2
    first_own = jnp.concatenate(
        [attend_own, router_master, gains_master.T, jnp.zeros((shard, rest), F32)], axis=1
    ).astype(BF16)
    half = local_experts // 2
    packed = [
        pack_experts(
            expand_master[i : i + half].astype(BF16), shrink_master[i : i + half].astype(BF16)
        )
        for i in (0, half)
    ]
    front = lax.all_gather(packed[0], ("dp", "ctx"), axis=0, tiled=False)
    first_w, outward_w = dense_gather(first_own, pair_heads(outward_master, 0).T.astype(BF16))
    attend_w = first_w[:, :qkv]
    router_w = first_w[:, qkv : qkv + experts]
    gains_f = first_w[:, qkv + experts : qkv + experts + 2].T.astype(F32)

    codes = slot_codes(routes[0, 0], priority[0, 0, 0], experts, capacity)
    known = jnp.concatenate(
        [cotangent[0, 0], codes.astype(BF16), jnp.zeros((rows_dev, LANES - experts), BF16)], axis=1
    )
    known = after(known, first_w)
    known_core = swap_core(known)
    known_far = swap_far(known)
    known_last = swap_core(known_far)
    known_near = jnp.concatenate([known, known_core], axis=0)
    known_far = jnp.concatenate([known_far, known_last], axis=0)
    grad_out_all = jnp.concatenate([known_near[:, :width], known_far[:, :width]], axis=0)

    positions = ctx_place * rows_dev + jnp.arange(rows_dev, dtype=jnp.int32)
    all_positions = jnp.arange(stream_len, dtype=jnp.int32)
    starts = doc_starts[0, 0]
    first_pos = jnp.max(jnp.where(starts[None, :] <= positions[:, None], starts[None, :], 0), axis=1)
    place = jnp.stack([positions, first_pos], axis=0)
    tables = turn_tables(all_positions)
    own_tables = tuple(
        lax.dynamic_slice_in_dim(table, ctx_place * rows_dev, rows_dev, 0) for table in tables
    )
    queries, pairs, first_low = project(local_low, gains_f[0:1], first_w, *own_tables)
    key_pieces = [pairs]
    for step in range(ctx_count - 1):
        key_pieces.append(
            lax.ppermute(key_pieces[-1], "ctx", [(i, i + 1) for i in range(step, ctx_count - 1)])
        )
    rear = lax.all_gather(after(packed[1], key_pieces[-1]), ("dp", "ctx"), axis=0, tiled=False)
    state = ()
    for step in range(ctx_count):
        state = attend_forward(
            place, ctx_place - step, queries, key_pieces[step], state, step == ctx_count - 1
        )
        if step == ctx_count - 2:
            *state, known_near, known_far, grad_out_all = lax.optimization_barrier(
                (*state, known_near, known_far, grad_out_all)
            )
    mixed_low, log_total, mixed_turned = state
    branch = lax.dot_general(mixed_low, outward_w, NT, preferred_element_type=F32)
    middle = local_rows + branch
    second_norm, second_unit, second_scale = rms_forward(middle, gains_f[1])
    second_low = second_norm.astype(BF16)

    first_expert = jnp.reshape(exp_place * local_experts, (1,)).astype(jnp.int32)
    second_core = swap_core(second_low)
    second_far = swap_far(second_low)
    second_near = jnp.concatenate([second_low, second_core], axis=0)
    router_block = qkv // LANES

    def group(index, part, second, known, weights, before, kept, *tie):
        first = first_expert + index * half
        return run_experts(
            first, part, 2, second, known, first_w, weights, router_block, before, kept, tie
        )

    contract = (((0,), (0,)), ((), ()))

    def wide_grad_of(grad, *others):
        grad = after(grad, *others)
        wide = lax.dot_general(second_all, grad, contract, preferred_element_type=F32)
        return wide.astype(BF16)

    def thin_grad_of(hidden, *others):
        hidden = after(hidden, *others)
        thin = lax.dot_general(hidden, grad_out_all, contract, preferred_element_type=F32)
        return thin.astype(BF16).reshape(half, FF, width)

    owners = lax.axis_size("dp") * ctx_count

    def owner_rows(wide, thin):
        thin = jnp.swapaxes(thin.reshape(half, owners, FF // owners, width), 0, 1)
        thin = thin.reshape(owners, width // owners, half * FF)
        both = jnp.concatenate([wide.reshape(owners, width // owners, -1), thin], axis=2)
        return both.reshape(width, -1)

    def scatter(both):
        return lax.psum_scatter(both, ("dp", "ctx"), scatter_dimension=0, tiled=True)

    def own_grads(total):
        wide = total[:, : half * 2 * FF].reshape(-1, half, 2 * FF)
        thin = total[:, half * 2 * FF :].reshape(half, FF // owners, width)
        return (jnp.swapaxes(wide, 0, 1).astype(F32), thin.astype(F32))

    *kept, back_near, mix_near = group(0, 0, second_near, known_near, front, (), ())
    second_far = after(second_far, back_near)
    second_last = swap_core(second_far)
    second_far = jnp.concatenate([second_far, second_last], axis=0)
    second_all = jnp.concatenate([second_near, second_far], axis=0)
    hidden, grad, back_far, mix_far = group(0, 1, second_far, known_far, front, (), kept)
    front_grads = (wide_grad_of(grad, back_far), thin_grad_of(hidden, back_far))
    front_rows = owner_rows(*front_grads)
    front_sum = scatter(front_rows)
    *kept, back_far, mix_far = group(
        1, 1, second_far, known_far, rear, (back_far, mix_far), (), front_rows
    )
    across = back_far[:rows_dev].astype(F32) + swap_core(back_far[rows_dev:]).astype(F32)
    across = across.astype(BF16)
    second_near = after(second_near, across)
    across = swap_far(across)
    hidden, grad, back_near, mix_near = group(
        1, 0, second_near, known_near, rear, (back_near, mix_near), kept
    )
    back_near, across = lax.optimization_barrier((back_near, across))
    row_grads = (
        back_near[:rows_dev].astype(F32)
        + swap_core(back_near[rows_dev:]).astype(F32)
        + across.astype(F32)
    )
    grad_gates = (
        row_grads[:, width : width + experts]
        + row_grads[:, width + LANES // 2 : width + LANES // 2 + experts]
    )
    mix_near, mix_far, row_grads = lax.optimization_barrier((mix_near, mix_far, row_grads))
    mix_core = swap_core(mix_near[rows_dev:])
    mixture = mix_far[:rows_dev].astype(F32) + swap_core(mix_far[rows_dev:]).astype(F32)
    mixture = swap_far(mixture.astype(BF16))
    row_grads = row_grads[:, :width]

    logits = jnp.dot(second_low, router_w, preferred_element_type=F32)
    gates = jax.nn.softmax(jnp.where(codes > 0, logits, NEGATIVE), axis=-1)
    gates = jnp.where(codes > 0, gates, 0.0)
    mean_term = jnp.sum(gates * grad_gates, axis=-1, keepdims=True)
    grad_logits = (gates * (grad_gates - mean_term)).astype(BF16)
    router_grad = jnp.einsum("td,te->de", second_low, grad_logits, preferred_element_type=F32)
    grad_second = row_grads + jnp.einsum(
        "te,de->td", grad_logits, router_w, preferred_element_type=F32
    )
    grad_middle_norm, gain_two_grad = rms_backward(
        grad_second, second_unit, second_scale, gains_f[1]
    )
    grad_middle = cotangent[0, 0].astype(F32) + grad_middle_norm
    grad_branch = grad_middle.astype(BF16)

    grad_mixed = jnp.dot(grad_branch, outward_w, preferred_element_type=F32).astype(BF16)
    deltas = row_deltas(grad_mixed, mixed_turned)
    grad_query = ()
    got = None
    for step in range(1, ctx_count + 1):
        back = ctx_count - step
        *grad_query, grad_pairs = attend_backward(
            place,
            ctx_place - back,
            queries,
            grad_mixed,
            log_total,
            deltas,
            key_pieces[back],
            tables,
            own_tables,
            grad_query,
            back == 0,
            (front_sum,) if step == 3 else (),
        )
        key_sum = grad_pairs.astype(F32)
        if step > 1:
            key_sum += got.astype(F32)
        key_sum = key_sum.astype(BF16)
        if back > 0:
            pairs_back = [(i, i - 1) for i in range(back, ctx_count)]
            got = lax.ppermute(key_sum, "ctx", pairs_back)
        if step == 1:
            thin = thin_grad_of(hidden, grad_pairs)
        if step == 2:
            wide = wide_grad_of(grad, grad_pairs)
    (grad_query,) = grad_query
    rear_sum = scatter(owner_rows(wide, thin))
    mixture, mix_core = lax.optimization_barrier((mixture, mix_core, key_sum))[:2]
    mixture = mixture.astype(F32) + mix_core.astype(F32) + mix_near[:rows_dev].astype(F32)
    output = (middle + mixture).astype(BF16)
    outward_grad = jnp.einsum("td,tc->dc", grad_branch, mixed_low, preferred_element_type=F32)
    grad_project = jnp.concatenate([grad_query, key_sum[0], key_sum[1]], axis=1)
    attend_grad = jnp.einsum("tc,tp->cp", first_low, grad_project, preferred_element_type=F32)
    grad_first = lax.dot_general(grad_project, attend_w, NT, preferred_element_type=F32)
    first_norm, first_unit, first_scale = rms_forward(local_rows, gains_f[0])
    grad_input_norm, gain_one_grad = rms_backward(grad_first, first_unit, first_scale, gains_f[0])
    input_grad = grad_middle + grad_input_norm
    thin_grad = jnp.concatenate(
        [
            router_grad.astype(BF16),
            jnp.stack([gain_one_grad, gain_two_grad], axis=1).astype(BF16),
            jnp.zeros((width, rest), BF16),
        ],
        axis=1,
    )
    first_sum = dense_sum(attend_grad.astype(BF16), thin_grad, outward_grad.astype(BF16))
    outward_sum = first_sum[:, qkv + LANES :]
    attend_sum = jnp.concatenate(
        [unpair_heads(first_sum[:, :query_end], 1), first_sum[:, query_end:qkv]], axis=1
    )
    router_sum = first_sum[:, qkv : qkv + experts]
    gains_sum = first_sum[:, qkv + experts : qkv + experts + 2].T
    outward_sum = unpair_heads(outward_sum.T, 0)
    front_sum, rear_sum, first_sum = lax.optimization_barrier((front_sum, rear_sum, first_sum))
    expand_sum, shrink_sum = (
        jnp.concatenate(parts, axis=0) for parts in zip(own_grads(front_sum), own_grads(rear_sum))
    )
    attend_new = adam_update(
        attend_master, attend_mean, attend_square, attend_sum, D ** (-0.5), DECAY
    )
    outward_new = adam_update(
        outward_master, outward_mean, outward_square, outward_sum, 4.0 * D ** (-0.5), DECAY
    )
    router_new = adam_update(
        router_master, router_mean, router_square, router_sum, 0.5 * D ** (-0.5), DECAY
    )
    gains_new = adam_update(gains_master, gains_mean, gains_square, gains_sum, 0.6, 0.0)
    expand_new = adam_update(
        expand_master, expand_mean, expand_square, expand_sum, D ** (-0.5), DECAY
    )
    shrink_new = adam_update(
        shrink_master, shrink_mean, shrink_square, shrink_sum, (FF // 32) ** (-0.5), DECAY
    )
    return (
        output[None, None],
        input_grad[None, None],
        attend_new[0],
        attend_new[1],
        attend_new[2],
        attend_new[3],
        outward_new[0],
        outward_new[1],
        outward_new[2],
        outward_new[3],
        router_new[0],
        router_new[1],
        router_new[2],
        router_new[3],
        gains_new[0],
        gains_new[1],
        gains_new[2],
        gains_new[3],
        expand_new[0],
        expand_new[1],
        expand_new[2],
        expand_new[3],
        shrink_new[0],
        shrink_new[1],
        shrink_new[2],
        shrink_new[3],
    )


def solution(mesh):
    in_specs = (
        P("dp", "exp", "ctx", None),
        P("dp", "exp", "ctx", None),
        P("dp", "exp", None),
        P("dp", "exp", "ctx", None),
        P("dp", "exp", "ctx", None),
        P(("dp", "ctx", "exp"), None),
        P(("dp", "ctx", "exp"), None),
        P(("dp", "ctx", "exp"), None),
        P(None, ("dp", "ctx", "exp")),
        P(None, ("dp", "ctx", "exp")),
        P(None, ("dp", "ctx", "exp")),
        P(("dp", "ctx", "exp"), None),
        P(("dp", "ctx", "exp"), None),
        P(("dp", "ctx", "exp"), None),
        P(None, ("dp", "ctx", "exp")),
        P(None, ("dp", "ctx", "exp")),
        P(None, ("dp", "ctx", "exp")),
        P("exp", ("dp", "ctx"), None),
        P("exp", ("dp", "ctx"), None),
        P("exp", ("dp", "ctx"), None),
        P("exp", ("dp", "ctx"), None),
        P("exp", ("dp", "ctx"), None),
        P("exp", ("dp", "ctx"), None),
    )
    out_specs = (
        P("dp", "exp", "ctx", None),
        P("dp", "exp", "ctx", None),
        P(("dp", "ctx", "exp"), None),
        P(("dp", "ctx", "exp"), None),
        P(("dp", "ctx", "exp"), None),
        P(("dp", "ctx", "exp"), None),
        P(None, ("dp", "ctx", "exp")),
        P(None, ("dp", "ctx", "exp")),
        P(None, ("dp", "ctx", "exp")),
        P(None, ("dp", "ctx", "exp")),
        P(("dp", "ctx", "exp"), None),
        P(("dp", "ctx", "exp"), None),
        P(("dp", "ctx", "exp"), None),
        P(("dp", "ctx", "exp"), None),
        P(None, ("dp", "ctx", "exp")),
        P(None, ("dp", "ctx", "exp")),
        P(None, ("dp", "ctx", "exp")),
        P(None, ("dp", "ctx", "exp")),
        P("exp", ("dp", "ctx"), None),
        P("exp", ("dp", "ctx"), None),
        P("exp", ("dp", "ctx"), None),
        P("exp", ("dp", "ctx"), None),
        P("exp", ("dp", "ctx"), None),
        P("exp", ("dp", "ctx"), None),
        P("exp", ("dp", "ctx"), None),
        P("exp", ("dp", "ctx"), None),
    )
    return jax.shard_map(body, mesh=mesh, in_specs=in_specs, out_specs=out_specs, check_vma=False)
```

```python
import functools
import math

import jax
import jax.numpy as jnp
from jax import lax
from jax.experimental import pallas as pl
from jax.experimental.pallas import tpu as pltpu
from jax.sharding import PartitionSpec as P

D = 1536
HEADS = 24
KVH = 8
HD = 64
FF = 512
STEP = 10
GROUP = HEADS // KVH
PAIRS = KVH // 2
LANES = 2 * HD
SCALE = HD**-0.5


EPSILON = 1e-05
THETA = 10000.0
BETA_ONE = 0.9
BETA_TWO = 0.95
ADAM_EPSILON = 1e-08
DECAY = 0.1
NEGATIVE = -1e30
BF16 = jnp.bfloat16
F32 = jnp.float32
NT = (((1,), (1,)), ((), ()))


def rms_forward(values, gain_vec):
    scale_row = lax.rsqrt(jnp.mean(values * values, axis=-1, keepdims=True) + EPSILON)
    unit_rows = values * scale_row
    return (unit_rows * gain_vec, unit_rows, scale_row)


def rms_backward(grad_rows, unit_rows, scale_row, gain_vec):
    inner = grad_rows * gain_vec
    grad_values = scale_row * (
        inner - unit_rows * jnp.mean(inner * unit_rows, axis=-1, keepdims=True)
    )
    return (grad_values, jnp.sum(grad_rows * unit_rows, axis=0))


def adam_update(master, first_mom, second_mom, grad, rate, decay):
    first_new = BETA_ONE * first_mom + (1.0 - BETA_ONE) * grad
    second_new = BETA_TWO * second_mom + (1.0 - BETA_TWO) * grad * grad
    first_hat = first_new / (1.0 - BETA_ONE**STEP)
    second_hat = second_new / (1.0 - BETA_TWO**STEP)
    master_new = master - rate * (
        first_hat / (jnp.sqrt(second_hat) + ADAM_EPSILON) + decay * master
    )
    return (first_new, second_new, master_new, master_new.astype(jnp.bfloat16))


def adam_kernel(rate, decay, master_ref, mean_ref, square_ref, grad_ref, *refs):
    outs = refs[len(refs) - 4 :]
    grad = grad_ref[...].reshape(master_ref.shape).astype(F32)
    news = adam_update(master_ref[...], mean_ref[...], square_ref[...], grad, rate, decay)
    for out, new in zip(outs, news):
        out[...] = new


def dense_adam_kernel(experts, rates, sum_ref, *refs):
    groups = [refs[3 * i : 3 * i + 3] for i in range(4)]
    results = [refs[12 + 4 * i : 16 + 4 * i] for i in range(4)]
    rows = sum_ref.shape[0]
    lane = lax.broadcasted_iota(jnp.int32, (rows, LANES), 1)
    qkv = (HEADS + 2 * KVH) * HD

    def update(index, cut, grad):
        rate, decay = rates[index]
        news = adam_update(*(ref[cut] for ref in groups[index]), grad, rate, decay)
        for out, new in zip(results[index], news):
            out[cut] = new

    def columns(start):
        return (slice(None), slice(start, start + LANES))

    def place(head):
        group, member = head // GROUP, head % GROUP
        return (GROUP * (group // 2) + member, group % 2)

    for index, begin in ((0, 0), (1, qkv + LANES)):
        for pair in range(HEADS // 2):
            parts = []
            for side in range(2):
                spot, part = place(2 * pair + side)
                block = sum_ref[columns(begin + spot * LANES)]
                parts.append(block if part == side else pltpu.roll(block, HD, 1))
            update(index, columns(pair * LANES), jnp.where(lane < HD, parts[0], parts[1]))
    for start in range(HEADS * HD, qkv, LANES):
        update(0, columns(start), sum_ref[columns(start)])
    thin = sum_ref[columns(qkv)]
    whole = (slice(None), slice(None))
    update(2, whole, thin[:, :experts])
    update(3, whole, thin.T[experts : experts + 2])


def dense_adam(total, arrays, rates):
    shapes = []
    for master, _, _ in arrays:
        shapes += [jax.ShapeDtypeStruct(master.shape, F32)] * 3
        shapes.append(jax.ShapeDtypeStruct(master.shape, BF16))
    outs = pl.pallas_call(
        functools.partial(dense_adam_kernel, arrays[2][0].shape[1], rates),
        in_specs=[pl.BlockSpec(memory_space=pltpu.VMEM)] * 13,
        out_specs=[pl.BlockSpec(memory_space=pltpu.VMEM)] * 16,
        out_shape=shapes,
        compiler_params=pltpu.CompilerParams(vmem_limit_bytes=48 * 1024 * 1024),
        cost_estimate=pl.CostEstimate(
            flops=20 * total.size, bytes_accessed=40 * total.size, transcendentals=0
        ),
    )(total, *(array for group in arrays for array in group))
    return [outs[4 * i : 4 * i + 4] for i in range(4)]


def adam_group(arrays, grad, grad_spec, first, tiles, rate, decay, kept):
    shape = arrays[0].shape
    rows = shape[1] // tiles
    own = pl.BlockSpec((1, rows, shape[2]), lambda i, j: (first + i, j, 0))
    count = shape[0] // 2
    whole = [pl.BlockSpec(memory_space=pl.ANY)] * len(kept)
    return pl.pallas_call(
        functools.partial(adam_kernel, rate, decay),
        grid=(count, tiles),
        in_specs=[own, own, own, grad_spec, *whole],
        out_specs=[own] * 4,
        out_shape=[jax.ShapeDtypeStruct(shape, F32)] * 3 + [jax.ShapeDtypeStruct(shape, BF16)],
        input_output_aliases={4 + i: i for i in range(len(kept))},
        compiler_params=pltpu.CompilerParams(vmem_limit_bytes=40 * 1024 * 1024),
        cost_estimate=pl.CostEstimate(
            flops=10 * arrays[0].size, bytes_accessed=14 * arrays[0].size, transcendentals=0
        ),
    )(*arrays, grad, *kept)


def pair_heads(block, axis):
    shape = block.shape
    split = shape[:axis] + (PAIRS, 2, GROUP, HD) + shape[axis + 1 :]
    return jnp.swapaxes(block.reshape(split), axis + 1, axis + 2).reshape(shape)


def unpair_heads(block, axis):
    shape = block.shape
    split = shape[:axis] + (PAIRS, GROUP, 2, HD) + shape[axis + 1 :]
    return jnp.swapaxes(block.reshape(split), axis + 1, axis + 2).reshape(shape)


def turn_tables(positions):
    half = HD // 2
    frequency = THETA ** (-jnp.arange(half, dtype=F32) / half)
    angles = positions.astype(F32)[:, None] * frequency[None, :]
    cosine = jnp.cos(angles)
    sine = jnp.sin(angles)
    return (
        jnp.concatenate([cosine] * 4, axis=1),
        jnp.concatenate([-sine, sine, -sine, sine], axis=1),
    )


def swap_halves(block):
    half = HD // 2
    lane = lax.broadcasted_iota(jnp.int32, block.shape, 1)
    ahead = pltpu.roll(block, LANES - half, 1)
    behind = pltpu.roll(block, half, 1)
    return jnp.where(lane % HD < half, ahead, behind)


def project_kernel(x_ref, gain_ref, w_ref, cos_ref, sin_ref, q_ref, kv_ref, h_ref):
    step = pl.program_id(0)
    query_tiles = HEADS * HD // 256
    key_tiles = KVH * HD // 256

    @pl.when(step == 0)
    def _():
        rows = x_ref[...].astype(F32)
        scale_row = lax.rsqrt(jnp.mean(rows * rows, axis=-1, keepdims=True) + EPSILON)
        h_ref[...] = (rows * scale_row * gain_ref[...]).astype(BF16)

    acc = jnp.dot(h_ref[...], w_ref[...], preferred_element_type=F32)

    def turned(half):
        part = acc[:, half * LANES : (half + 1) * LANES]
        return part * cos_ref[...] + swap_halves(part) * sin_ref[...]

    @pl.when(step < query_tiles)
    def _():
        for half in range(2):
            q_ref[:, half * LANES : (half + 1) * LANES] = (turned(half) * SCALE).astype(BF16)

    @pl.when((step >= query_tiles) & (step < query_tiles + key_tiles))
    def _():
        for half in range(2):
            kv_ref[:, half * LANES : (half + 1) * LANES] = turned(half).astype(BF16)

    @pl.when(step >= query_tiles + key_tiles)
    def _():
        kv_ref[...] = acc.astype(BF16)


def project(x, gain, weights, cosine, sine):
    rows = x.shape[0]
    query_tiles = HEADS * HD // 256
    tiles = (HEADS + 2 * KVH) * HD // 256
    return pl.pallas_call(
        project_kernel,
        grid=(tiles,),
        in_specs=[
            pl.BlockSpec((rows, D), lambda j: (0, 0)),
            pl.BlockSpec((1, D), lambda j: (0, 0)),
            pl.BlockSpec((D, 256), lambda j: (0, j)),
            pl.BlockSpec((rows, LANES), lambda j: (0, 0)),
            pl.BlockSpec((rows, LANES), lambda j: (0, 0)),
        ],
        out_specs=[
            pl.BlockSpec((rows, 256), lambda j: (0, jnp.minimum(j, query_tiles - 1))),
            pl.BlockSpec((rows, 256), lambda j: (0, jnp.maximum(j - query_tiles, 0))),
            pl.BlockSpec((rows, D), lambda j: (0, 0)),
        ],
        out_shape=[
            jax.ShapeDtypeStruct((rows, HEADS * HD), BF16),
            jax.ShapeDtypeStruct((rows, 2 * KVH * HD), BF16),
            jax.ShapeDtypeStruct((rows, D), BF16),
        ],
        compiler_params=pltpu.CompilerParams(vmem_limit_bytes=40 * 1024 * 1024),
        cost_estimate=pl.CostEstimate(
            flops=2 * rows * D * tiles * 256, bytes_accessed=D * tiles * 512, transcendentals=0
        ),
    )(x, gain, weights, cosine, sine)


def masked_pair(block):
    lane = lax.broadcasted_iota(jnp.int32, block.shape, 1)
    zero = jnp.zeros_like(block)
    return jnp.concatenate(
        [jnp.where(lane < HD, block, zero), jnp.where(lane >= HD, block, zero)], axis=0
    )


def chunk_flags(place, owner, sub_rows):
    rows = place.shape[1]
    start = owner * rows
    end = start + rows - 1
    first = place[:, ::sub_rows]
    last = place[:, sub_rows - 1 :: sub_rows]
    seen = (owner >= 0) & (start <= last[0]) & (end >= first[1])
    whole = (last[1] <= start) & (end <= first[0])
    return jnp.where(seen, jnp.where(whole, 2, 1), 0).astype(jnp.int32)


def allowed_keys(owner, key_rows, columns, place_ref):
    key_pos = owner * key_rows + lax.broadcasted_iota(jnp.int32, (key_rows, columns), 0)
    query_pos = jnp.concatenate([place_ref[0:1, :]] * 2, axis=1)
    first_pos = jnp.concatenate([place_ref[1:2, :]] * 2, axis=1)
    return (key_pos <= query_pos) & (key_pos >= first_pos)


def halves(index, rows):
    return slice(index * rows, (index + 1) * rows)


def attend_kernel(first, final, flag_ref, owner_ref, place_ref, q_ref, k_ref, v_ref, *refs):
    sub = pl.program_id(1)
    rows = q_ref.shape[0]
    key_rows = k_ref.shape[0]
    columns = 2 * rows
    if first:
        before = None
    else:
        before, refs = refs[:3], refs[3:]
    outs, (top, total, acc) = refs[:3], refs[3:]
    for r in range(GROUP):
        if first:
            top[r] = jnp.full((1, columns), NEGATIVE, F32)
            total[r] = jnp.zeros((1, columns), F32)
            acc[r] = jnp.zeros((LANES, columns), F32)
        else:
            acc[r] = jnp.zeros((LANES, columns), F32)
            for i in range(2):
                cols = halves(i, rows)
                head = slice(2 * r + i, 2 * r + i + 1)
                top[r, :, cols] = before[0][0, head, :]
                total[r, :, cols] = before[1][0, head, :]
                acc[r, halves(i, HD), cols] = before[2][0, r, halves(i, HD), :]

    def update(masked):
        keys = k_ref[...]
        turned = v_ref[...].astype(F32).T.astype(BF16)
        if masked:
            allowed = allowed_keys(owner_ref[0], key_rows, columns, place_ref)
        for r in range(GROUP):
            queries = masked_pair(q_ref[:, r * LANES : (r + 1) * LANES])
            scores = lax.dot_general(keys, queries, NT, preferred_element_type=F32)
            if masked:
                scores = jnp.where(allowed, scores, NEGATIVE)
            old = top[r]
            now = jnp.maximum(old, jnp.max(scores, axis=0, keepdims=True))
            shrinking = jnp.exp(old - now)
            terms = jnp.exp(scores - now)
            top[r] = now
            total[r] = total[r] * shrinking + jnp.sum(terms, axis=0, keepdims=True)
            acc[r] = acc[r] * shrinking + jnp.dot(
                turned, terms.astype(BF16), preferred_element_type=F32
            )

    @pl.when(flag_ref[sub] == 1)
    def _():
        update(True)

    @pl.when(flag_ref[sub] == 2)
    def _():
        update(False)

    for r in range(GROUP):
        mixed = acc[r] / total[r] if final else acc[r]
        both = jnp.concatenate([mixed[:HD, :rows], mixed[HD:, rows:]], axis=0)
        if final:
            lse = top[r] + jnp.log(total[r])
        for i in range(2):
            head = slice(2 * r + i, 2 * r + i + 1)
            if final:
                outs[1][0, head, :] = lse[:, halves(i, rows)]
            else:
                outs[0][0, head, :] = top[r, :, halves(i, rows)]
                outs[1][0, head, :] = total[r, :, halves(i, rows)]
        outs[2][0, r] = both
        if final:
            outs[0][:, r * LANES : (r + 1) * LANES] = both.T.astype(BF16)


def head_specs(rows, sub_rows):
    line = pl.BlockSpec((1, 2 * GROUP, sub_rows), lambda p, s, *_: (p, 0, s))
    turned = pl.BlockSpec((1, GROUP, LANES, sub_rows), lambda p, s, *_: (p, 0, 0, s))
    wide = pl.BlockSpec((sub_rows, GROUP * LANES), lambda p, s, *_: (s, p))
    line_shape = jax.ShapeDtypeStruct((PAIRS, 2 * GROUP, rows), F32)
    turned_shape = jax.ShapeDtypeStruct((PAIRS, GROUP, LANES, rows), F32)
    wide_shape = jax.ShapeDtypeStruct((rows, HEADS * HD), BF16)
    return (line, turned, wide, line_shape, turned_shape, wide_shape)


def attend_forward(place, owner, q, piece, before, final):
    rows = q.shape[0]
    sub_rows = min(256, rows)
    columns = 2 * sub_rows
    line, turned, wide, line_shape, turned_shape, wide_shape = head_specs(rows, sub_rows)
    return pl.pallas_call(
        functools.partial(attend_kernel, not before, final),
        grid_spec=pltpu.PrefetchScalarGridSpec(
            num_scalar_prefetch=2,
            grid=(PAIRS, rows // sub_rows),
            in_specs=[
                pl.BlockSpec((2, sub_rows), lambda p, s, *_: (0, s)),
                wide,
                pl.BlockSpec((rows, LANES), lambda p, s, *_: (0, p)),
                pl.BlockSpec((rows, LANES), lambda p, s, *_: (0, p)),
                *([line, line, turned] if before else []),
            ],
            out_specs=[wide, line, turned] if final else [line, line, turned],
            scratch_shapes=[
                pltpu.VMEM((GROUP, 1, columns), F32),
                pltpu.VMEM((GROUP, 1, columns), F32),
                pltpu.VMEM((GROUP, LANES, columns), F32),
            ],
        ),
        out_shape=[wide_shape if final else line_shape, line_shape, turned_shape],
        compiler_params=pltpu.CompilerParams(vmem_limit_bytes=40 * 1024 * 1024),
        cost_estimate=pl.CostEstimate(
            flops=40 * rows * rows * D, bytes_accessed=8 * rows * D, transcendentals=0
        ),
    )(chunk_flags(place, owner, sub_rows), owner[None], place, q, *piece, *before)


def delta_kernel(do_ref, ot_ref, delta_ref):
    for r in range(GROUP):
        product = do_ref[:, r * LANES : (r + 1) * LANES].astype(F32).T * ot_ref[0, r]
        for i in range(2):
            delta_ref[0, 2 * r + i : 2 * r + i + 1, :] = jnp.sum(
                product[halves(i, HD)], axis=0, keepdims=True
            )


def row_deltas(do, ot):
    rows = do.shape[0]
    line, turned, wide, line_shape, _, _ = head_specs(rows, rows)
    return pl.pallas_call(
        delta_kernel,
        grid=(PAIRS, 1),
        in_specs=[wide, turned],
        out_specs=line,
        out_shape=line_shape,
        cost_estimate=pl.CostEstimate(
            flops=2 * rows * D, bytes_accessed=6 * rows * D, transcendentals=0
        ),
    )(do, ot)


def attend_back_kernel(
    first,
    final,
    flag_ref,
    owner_ref,
    place_ref,
    q_ref,
    do_ref,
    lse_ref,
    delta_ref,
    k_ref,
    v_ref,
    cos_ref,
    sin_ref,
    own_cos_ref,
    own_sin_ref,
    *refs,
):
    sub = pl.program_id(1)
    rows = q_ref.shape[0]
    key_rows = k_ref.shape[0]
    columns = 2 * rows
    if not first:
        before = refs[0]
    grad_ref, pair_ref, acc, dk, dv = refs[len(refs) - 5 :]

    @pl.when(sub == 0)
    def _():
        dk[...] = jnp.zeros(dk.shape, F32)
        dv[...] = jnp.zeros(dv.shape, F32)

    acc[...] = jnp.zeros(acc.shape, F32)
    if not first:
        for r in range(GROUP):
            for i in range(2):
                acc[r, halves(i, HD), halves(i, rows)] = before[0, r, halves(i, HD), :]

    def update(masked):
        keys = k_ref[...]
        values = v_ref[...]
        turned = keys.astype(F32).T.astype(BF16)
        key_grad = dk[...]
        value_grad = dv[...]
        if masked:
            allowed = allowed_keys(owner_ref[0], key_rows, columns, place_ref)
        for r in range(GROUP):
            lanes = slice(r * LANES, (r + 1) * LANES)
            queries = masked_pair(q_ref[:, lanes])
            grads = masked_pair(do_ref[:, lanes])
            heads = [slice(2 * r + i, 2 * r + i + 1) for i in range(2)]
            lse = jnp.concatenate([lse_ref[0, head, :] for head in heads], axis=1)
            delta = jnp.concatenate([delta_ref[0, head, :] for head in heads], axis=1)
            scores = lax.dot_general(keys, queries, NT, preferred_element_type=F32)
            probs = jnp.exp(scores - lse)
            if masked:
                probs = jnp.where(allowed, probs, 0.0)
            value_grad += jnp.dot(probs.astype(BF16), grads, preferred_element_type=F32)
            prob_grad = lax.dot_general(values, grads, NT, preferred_element_type=F32)
            score_grad = (probs * (prob_grad - delta)).astype(BF16)
            key_grad += jnp.dot(score_grad, queries, preferred_element_type=F32)
            acc[r] += jnp.dot(turned, score_grad, preferred_element_type=F32)
        dk[...] = key_grad
        dv[...] = value_grad

    @pl.when(flag_ref[sub] == 1)
    def _():
        update(True)

    @pl.when(flag_ref[sub] == 2)
    def _():
        update(False)

    for r in range(GROUP):
        both = jnp.concatenate([acc[r, :HD, :rows], acc[r, HD:, rows:]], axis=0)
        if final:
            grad = both.T * SCALE
            grad = grad * own_cos_ref[...] - swap_halves(grad) * own_sin_ref[...]
            grad_ref[:, r * LANES : (r + 1) * LANES] = grad.astype(BF16)
        else:
            grad_ref[0, r] = both

    @pl.when(sub == pl.num_programs(1) - 1)
    def _():
        pair_ref[0] = (dk[...] * cos_ref[...] - swap_halves(dk[...]) * sin_ref[...]).astype(BF16)
        pair_ref[1] = dv[...].astype(BF16)


def attend_backward(
    place, owner, q, do, lse, delta, piece, tables, own_tables, before, final, tie
):
    rows = q.shape[0]
    sub_rows = min(256, rows)
    columns = 2 * sub_rows
    line, turned, wide, _, turned_shape, wide_shape = head_specs(rows, sub_rows)
    far = pl.BlockSpec((rows, LANES), lambda p, s, flags, own: (jnp.maximum(own[0], 0), 0))
    near = pl.BlockSpec((sub_rows, LANES), lambda p, s, *_: (s, 0))
    return pl.pallas_call(
        functools.partial(attend_back_kernel, not before, final),
        grid_spec=pltpu.PrefetchScalarGridSpec(
            num_scalar_prefetch=2,
            grid=(PAIRS, rows // sub_rows),
            in_specs=[
                pl.BlockSpec((2, sub_rows), lambda p, s, *_: (0, s)),
                wide,
                wide,
                line,
                line,
                pl.BlockSpec((rows, LANES), lambda p, s, *_: (0, p)),
                pl.BlockSpec((rows, LANES), lambda p, s, *_: (0, p)),
                far,
                far,
                near,
                near,
                *([turned] if before else []),
                *([pl.BlockSpec(memory_space=pl.ANY)] * len(tie)),
            ],
            out_specs=[
                wide if final else turned,
                pl.BlockSpec((2, rows, LANES), lambda p, s, *_: (0, 0, p)),
            ],
            scratch_shapes=[
                pltpu.VMEM((GROUP, LANES, columns), F32),
                pltpu.VMEM((rows, LANES), F32),
                pltpu.VMEM((rows, LANES), F32),
            ],
        ),
        out_shape=[
            wide_shape if final else turned_shape,
            jax.ShapeDtypeStruct((2, rows, KVH * HD), BF16),
        ],
        compiler_params=pltpu.CompilerParams(vmem_limit_bytes=40 * 1024 * 1024),
        cost_estimate=pl.CostEstimate(
            flops=60 * rows * rows * D, bytes_accessed=8 * rows * D, transcendentals=0
        ),
    )(
        chunk_flags(place, owner, sub_rows),
        owner[None],
        place,
        q,
        do,
        lse,
        delta,
        *piece,
        *tables,
        *own_tables,
        *before,
        *tie,
    )


def slot_codes(route_ids, priority_row, experts, capacity):
    rows, top_count = route_ids.shape
    ranks = priority_row.reshape(rows, top_count)
    routed = route_ids[:, :, None] == jnp.arange(experts, dtype=jnp.int32)[None, None, :]
    unused = rows * top_count
    rank = jnp.min(jnp.where(routed, ranks[:, :, None], unused), axis=1).T
    earlier = jnp.sum((rank[:, None, :] < rank[:, :, None]).astype(jnp.int32), axis=2)
    return jnp.where(rank < unused, jnp.where(earlier < capacity, 2, 1), 0).T


def pack_experts(expand, shrink):
    parts = [expand[:, :, :FF], expand[:, :, FF:]]
    parts += [shrink[:, :, j * FF : (j + 1) * FF] for j in range(D // FF)]
    return jnp.concatenate(parts, axis=1)


def after(value, *others):
    return lax.optimization_barrier((value, *others))[0]


def split_devices():
    return (lax.axis_size("dp"), lax.axis_size("ctx"), lax.axis_size("exp")) == (2, 4, 4)


def greet(partners):
    barrier = pltpu.get_barrier_semaphore()
    for partner in partners:
        pl.semaphore_signal(
            barrier, inc=1, device_id=partner, device_id_type=pl.DeviceIdType.MESH
        )
    pl.semaphore_wait(barrier, len(partners))


def neighbours():
    x = lax.axis_index("dp")
    z = lax.axis_index("ctx")
    spot = lax.axis_index("exp")
    y = spot // 2
    core = spot % 2
    other_core = {"exp": 2 * y + 1 - core}
    other_x = {"dp": 1 - x}
    other_y = {"exp": 2 * (1 - y) + core}
    along = [{"ctx": lax.rem(z + d, 4)} for d in range(1, 4)]
    return (x, y, z, core, other_core, other_x, other_y, along)


def send_to(source, target, sems, number, device):
    copy = pltpu.make_async_remote_copy(
        src_ref=source,
        dst_ref=target,
        send_sem=sems[0].at[number],
        recv_sem=sems[1].at[number],
        device_id=device,
        device_id_type=pl.DeviceIdType.MESH,
    )
    copy.start()
    return copy


def dense_gather_kernel(first_ref, second_ref, all_first, all_second, local_sem, *sems):
    x, y, z, core, other_core, other_x, other_y, along = neighbours()
    greet([other_core, other_x, other_y] + along)
    spread = [
        (
            send_to(first_ref, all_first.at[x, z, y, core], sems, 2 * d, along[d]),
            send_to(second_ref, all_second.at[x, z, y, core], sems, 2 * d + 1, along[d]),
        )
        for d in range(3)
    ]
    local = [
        pltpu.make_async_copy(first_ref, all_first.at[x, z, y, core], local_sem.at[0]),
        pltpu.make_async_copy(second_ref, all_second.at[x, z, y, core], local_sem.at[1]),
    ]
    for copy in local:
        copy.start()
    steps = [[], [], []]

    def send_near(index):
        if index == 0:
            for copy in local:
                copy.wait()
        else:
            for copy in spread[index - 1]:
                copy.wait_recv()
        spot = lax.rem(z - index + 4, 4)
        base = 6 + 6 * index
        block = all_first.at[x, spot, y, core]
        other = all_second.at[x, spot, y, core]
        steps[0].append(
            (
                send_to(block, block, sems, base, other_y),
                send_to(other, other, sems, base + 1, other_x),
            )
        )

    def send_far(index):
        for copy in steps[0][index]:
            copy.wait_recv()
        spot = lax.rem(z - index + 4, 4)
        base = 6 + 6 * index
        block = all_first.at[x, spot, :, core]
        other = all_second.at[:, spot, y, core]
        steps[1].append(
            (
                send_to(block, block, sems, base + 2, other_x),
                send_to(other, other, sems, base + 3, other_y),
            )
        )

    def send_core(index):
        for copy in steps[1][index]:
            copy.wait_recv()
        spot = lax.rem(z - index + 4, 4)
        base = 6 + 6 * index
        block = all_first.at[:, spot, :, core]
        other = all_second.at[:, spot, :, core]
        steps[2].append(
            (
                send_to(block, block, sems, base + 4, other_core),
                send_to(other, other, sems, base + 5, other_core),
            )
        )

    send_near(0)
    send_far(0)
    send_near(1)
    send_core(0)
    send_far(1)
    send_near(2)
    send_core(1)
    send_far(2)
    send_near(3)
    send_core(2)
    send_far(3)
    send_core(3)
    for pair in steps[2]:
        for copy in pair:
            copy.wait_recv()
    for pair in spread + steps[0] + steps[1] + steps[2]:
        for copy in pair:
            copy.wait_send()


def dense_gather(first, second):
    if not split_devices():
        every = ("dp", "ctx", "exp")
        return tuple(
            lax.all_gather(part, every, axis=0, tiled=True) for part in (first, second)
        )
    shapes = [(2, 4, 2, 2) + part.shape for part in (first, second)]
    gathered = pl.pallas_call(
        dense_gather_kernel,
        in_specs=[pl.BlockSpec(memory_space=pl.ANY)] * 2,
        out_specs=[pl.BlockSpec(memory_space=pl.ANY)] * 2,
        out_shape=[jax.ShapeDtypeStruct(shape, BF16) for shape in shapes],
        scratch_shapes=[
            pltpu.SemaphoreType.DMA((2,)),
            pltpu.SemaphoreType.DMA((30,)),
            pltpu.SemaphoreType.DMA((30,)),
        ],
        compiler_params=pltpu.CompilerParams(collective_id=2, has_side_effects=True),
        cost_estimate=pl.CostEstimate(
            flops=0, bytes_accessed=64 * (first.size + second.size), transcendentals=0
        ),
    )(first, second)
    return tuple(part.reshape(-1, part.shape[-1]) for part in gathered)


def dense_sum_kernel(starts, *refs):
    count = len(starts)
    parts = refs[:count]
    (
        out_ref,
        own,
        got_core,
        got_x,
        got_y,
        late_x,
        late_y,
        got_z,
        load_sem,
        send_sem,
        recv_sem,
    ) = refs[count:]
    x, y, z, core, other_core, other_x, other_y, along = neighbours()
    half = got_x.shape[-1]
    greet([other_core, other_x, other_y] + along)
    sems = (send_sem, recv_sem)
    first = []
    loads = []
    for index in range(count):
        columns = slice(starts[index], starts[index] + parts[index].shape[-1])
        first.append(
            send_to(
                parts[index].at[:, :, :, 1 - core],
                got_core.at[:, :, :, :, columns],
                sems,
                7 + index,
                other_core,
            )
        )
        loads.append(
            pltpu.make_async_copy(
                parts[index].at[:, :, :, core], own.at[:, :, :, :, columns], load_sem.at[index]
            )
        )
    for copy in loads:
        copy.start()
    for copy in loads + first:
        copy.wait()

    def add_core(index, carry):
        i = index // 8
        j = (index // 2) % 4
        k = index % 2
        own[i, j, k] = (own[i, j, k].astype(F32) + got_core[i, j, k].astype(F32)).astype(BF16)
        return carry

    lax.fori_loop(0, 16, add_core, 0)
    by_x = send_to(own.at[1 - x, :, :, :, :half], got_x, sems, 0, other_x)
    by_y = send_to(own.at[:, :, 1 - y, :, half:], got_y, sems, 1, other_y)
    by_x.wait()

    def add_x(index, carry):
        j = index // 2
        k = index % 2
        own[x, j, k, :, :half] = (
            own[x, j, k, :, :half].astype(F32) + got_x[j, k].astype(F32)
        ).astype(BF16)
        return carry

    lax.fori_loop(0, 8, add_x, 0)
    next_y = send_to(own.at[x, :, 1 - y, :, :half], late_y, sems, 2, other_y)
    by_y.wait()

    def add_y(index, carry):
        i = index // 4
        j = index % 4
        own[i, j, y, :, half:] = (
            own[i, j, y, :, half:].astype(F32) + got_y[i, j].astype(F32)
        ).astype(BF16)
        return carry

    lax.fori_loop(0, 8, add_y, 0)
    next_x = send_to(own.at[1 - x, :, y, :, half:], late_x, sems, 3, other_x)
    next_y.wait()
    next_x.wait()

    def add_late(j, carry):
        own[x, j, y, :, :half] = (
            own[x, j, y, :, :half].astype(F32) + late_y[j].astype(F32)
        ).astype(BF16)
        own[x, j, y, :, half:] = (
            own[x, j, y, :, half:].astype(F32) + late_x[j].astype(F32)
        ).astype(BF16)
        return carry

    lax.fori_loop(0, 4, add_late, 0)
    last = [
        send_to(own.at[x, lax.rem(z + d + 1, 4), y], got_z.at[d], sems, 4 + d, along[d])
        for d in range(3)
    ]
    for copy in last:
        copy.wait()
    total = own[x, z, y].astype(F32)
    for d in range(3):
        total += got_z[d].astype(F32)
    out_ref[...] = total


def dense_sum(*parts):
    if not split_devices():
        every = ("dp", "ctx", "exp")
        sums = [lax.psum_scatter(part, every, scatter_dimension=0, tiled=True) for part in parts]
        return jnp.concatenate(sums, axis=1).astype(F32)
    rows = parts[0].shape[0] // 32
    starts = []
    columns = 0
    for part in parts:
        starts.append(columns)
        columns += part.shape[1]
    half = columns // 2 // LANES * LANES
    rest = columns - half
    return pl.pallas_call(
        functools.partial(dense_sum_kernel, tuple(starts)),
        in_specs=[pl.BlockSpec(memory_space=pl.ANY)] * len(parts),
        out_specs=pl.BlockSpec(memory_space=pltpu.VMEM),
        out_shape=jax.ShapeDtypeStruct((rows, columns), F32),
        scratch_shapes=[
            pltpu.VMEM((2, 4, 2, rows, columns), BF16),
            pltpu.VMEM((2, 4, 2, rows, columns), BF16),
            pltpu.VMEM((4, 2, rows, half), BF16),
            pltpu.VMEM((2, 4, rows, rest), BF16),
            pltpu.VMEM((4, rows, rest), BF16),
            pltpu.VMEM((4, rows, half), BF16),
            pltpu.VMEM((3, rows, columns), BF16),
            pltpu.SemaphoreType.DMA((len(parts),)),
            pltpu.SemaphoreType.DMA((7 + len(parts),)),
            pltpu.SemaphoreType.DMA((7 + len(parts),)),
        ],
        compiler_params=pltpu.CompilerParams(
            collective_id=1, has_side_effects=True, vmem_limit_bytes=48 * 1024 * 1024
        ),
        cost_estimate=pl.CostEstimate(
            flops=0, bytes_accessed=64 * 1536 * columns, transcendentals=0
        ),
    )(*[part.reshape(2, 4, 2, 2, rows, part.shape[1]) for part in parts])


def experts_kernel(has_before, first_ref, h_ref, do_ref, code_ref, router_ref, weights, *refs):
    if has_before:
        back_before, tail_before, mix_before = refs[:3]
        refs = refs[3:]
    refs = refs[len(refs) - 7 :]
    gh_ref, dgu_ref, back_ref, mix_ref, table, back_acc, mix_acc = refs
    expert = pl.program_id(0)
    chunk = pl.program_id(1)
    tokens = h_ref.shape[0]
    owners = weights.shape[0]
    rows = D // owners
    thin = FF // owners
    own = pl.ds(pl.multiple_of(chunk * tokens, tokens), tokens)
    lane = lax.broadcasted_iota(jnp.int32, (tokens, LANES), 1)
    codes = code_ref[...].astype(F32)

    @pl.when(expert == 0)
    def _():
        logits = jnp.dot(h_ref[...], router_ref[...], preferred_element_type=F32)
        routed = codes > 0.5
        top = jnp.max(jnp.where(routed, logits, NEGATIVE), axis=1, keepdims=True)
        terms = jnp.where(routed, jnp.exp(jnp.where(routed, logits - top, 0.0)), 0.0)
        shares = terms / jnp.sum(terms, axis=1, keepdims=True)
        table[own, :] = jnp.where(codes > 1.5, shares, 0.0)
        if has_before:
            back_acc[own, :] = back_before[...].astype(F32)
            mix_acc[own, :] = mix_before[...].astype(F32)
        else:
            back_acc[own, :] = jnp.zeros((tokens, D), F32)
            mix_acc[own, :] = jnp.zeros((tokens, D), F32)

    mine = lane == first_ref[0] + expert
    kept = jnp.sum(jnp.where(mine, codes, 0.0), axis=1, keepdims=True) > 1.5
    gate = jnp.sum(jnp.where(mine, table[own, :], 0.0), axis=1, keepdims=True)
    gate_w = weights[:, 0, :rows].reshape(D, FF)
    up_w = weights[:, 0, rows : 2 * rows].reshape(D, FF)
    thirds = [
        weights[:, 0, 2 * rows + j * thin : 2 * rows + (j + 1) * thin].reshape(FF, FF)
        for j in range(D // FF)
    ]
    hidden_rows = h_ref[...]
    gated = jnp.dot(hidden_rows, gate_w, preferred_element_type=F32)
    upper = jnp.dot(hidden_rows, up_w, preferred_element_type=F32)
    grad_hidden = jnp.zeros((tokens, FF), F32)
    for j in range(D // FF):
        grad_hidden += lax.dot_general(
            do_ref[:, j * FF : (j + 1) * FF], thirds[j], NT, preferred_element_type=F32
        )
    sigma = 1.0 / (1.0 + jnp.exp(-gated))
    silu = gated * sigma
    hidden = silu * upper
    gated_hidden = (gate * hidden).astype(BF16)
    grad_gate = jnp.sum(grad_hidden * hidden, axis=1, keepdims=True)
    spot = lane == first_ref[0] + expert + LANES // 2
    table[own, :] += jnp.where(spot, jnp.where(kept, grad_gate, 0.0), 0.0)
    grad_hidden = gate * grad_hidden
    dg = (grad_hidden * upper * (sigma * (1.0 + gated * (1.0 - sigma)))).astype(BF16)
    du = (grad_hidden * silu).astype(BF16)
    gh_ref[...] = gated_hidden
    dgu_ref[:, :FF] = dg
    dgu_ref[:, FF:] = du
    for j in range(D // FF):
        cols = slice(j * FF, (j + 1) * FF)
        mix_acc[own, cols] += jnp.dot(gated_hidden, thirds[j], preferred_element_type=F32)
        back_acc[own, cols] += lax.dot_general(
            dg, gate_w[cols], NT, preferred_element_type=F32
        ) + lax.dot_general(du, up_w[cols], NT, preferred_element_type=F32)

    @pl.when(expert == pl.num_programs(0) - 1)
    def _():
        total = jnp.where(lane < LANES // 2, pltpu.roll(table[own, :], LANES // 2, 1), 0.0)
        coarse = total.astype(BF16)
        fine = total - coarse.astype(F32)
        grad_gates = coarse.astype(F32) + pltpu.roll(fine, LANES // 2, 1)
        if has_before:
            grad_gates += tail_before[...].astype(F32)
        mix_ref[...] = mix_acc[own, :].astype(BF16)
        back_ref[:, :D] = back_acc[own, :].astype(BF16)
        back_ref[:, D:] = grad_gates.astype(BF16)


def run_experts(first, part, parts, second, known, first_w, weights, block, before, kept, tie):
    tokens = second.shape[0]
    chunk = tokens // 2
    owners, experts, depth, _ = weights.shape
    last = experts - 1
    once = pl.Buffered(1)

    def final(e, c, *_):
        return (jnp.where(e == last, c, 0), 0)

    def initial(e, c, *_):
        return (jnp.where(e == 0, c, 1), 0)

    in_specs = [
        pl.BlockSpec((chunk, D), lambda e, c, *_: (c, 0)),
        pl.BlockSpec((chunk, D), lambda e, c, *_: (c, 0)),
        pl.BlockSpec((chunk, LANES), lambda e, c, *_: (c, D // LANES)),
        pl.BlockSpec((D, LANES), lambda e, c, *_: (0, block), pipeline_mode=once),
    ]
    in_specs.append(pl.BlockSpec((owners, 1, depth, FF), lambda e, c, *_: (0, e, 0, 0)))
    operands = [first, second, known, known, first_w, weights]
    if before:
        in_specs += [
            pl.BlockSpec((chunk, D), initial),
            pl.BlockSpec((chunk, LANES), lambda e, c, *_: (c, D // LANES)),
            pl.BlockSpec((chunk, D), initial),
        ]
        operands += [before[0], before[0], before[1]]
    in_specs += [pl.BlockSpec(memory_space=pl.ANY)] * len(tie)
    operands += list(tie)
    aliases = {}
    if kept:
        in_specs += [pl.BlockSpec(memory_space=pl.ANY)] * 2
        aliases = {len(operands): 0, len(operands) + 1: 1}
        operands += list(kept)
    return pl.pallas_call(
        functools.partial(experts_kernel, bool(before)),
        grid_spec=pltpu.PrefetchScalarGridSpec(
            num_scalar_prefetch=1,
            grid=(experts, 2),
            in_specs=in_specs,
            out_specs=[
                pl.BlockSpec((chunk, FF), lambda e, c, *_: (2 * part + c, e)),
                pl.BlockSpec((chunk, 2 * FF), lambda e, c, *_: (2 * part + c, e)),
                pl.BlockSpec((chunk, D + LANES), final),
                pl.BlockSpec((chunk, D), final),
            ],
            scratch_shapes=[
                pltpu.VMEM((tokens, LANES), F32),
                pltpu.VMEM((tokens, D), F32),
                pltpu.VMEM((tokens, D), F32),
            ],
        ),
        out_shape=[
            jax.ShapeDtypeStruct((parts * tokens, experts * FF), BF16),
            jax.ShapeDtypeStruct((parts * tokens, experts * 2 * FF), BF16),
            jax.ShapeDtypeStruct((tokens, D + LANES), BF16),
            jax.ShapeDtypeStruct((tokens, D), BF16),
        ],
        input_output_aliases=aliases,
        compiler_params=pltpu.CompilerParams(vmem_limit_bytes=58 * 1024 * 1024),
        cost_estimate=pl.CostEstimate(
            flops=18 * tokens * D * FF * experts,
            bytes_accessed=tokens * D * 16,
            transcendentals=0,
        ),
    )(*operands)


def swap_core(block):
    return lax.ppermute(block, "exp", [(i, i ^ 1) for i in range(lax.axis_size("exp"))])


def swap_far(block):
    return lax.ppermute(block, "exp", [(i, i ^ 2) for i in range(lax.axis_size("exp"))])


def body(
    tokens,
    cotangent,
    doc_starts,
    routes,
    priority,
    attend_master,
    attend_mean,
    attend_square,
    outward_master,
    outward_mean,
    outward_square,
    router_master,
    router_mean,
    router_square,
    gains_master,
    gains_mean,
    gains_square,
    expand_master,
    expand_mean,
    expand_square,
    shrink_master,
    shrink_mean,
    shrink_square,
):
    local_low = tokens[0, 0]
    local_rows = local_low.astype(F32)
    rows_dev, width = local_rows.shape
    ctx_count = lax.axis_size("ctx")
    ctx_place = lax.axis_index("ctx")
    exp_count = lax.axis_size("exp")
    exp_place = lax.axis_index("exp")
    stream_len = rows_dev * ctx_count
    experts = router_master.shape[1]
    local_experts = experts // exp_count
    top_count = routes.shape[-1]
    capacity = rows_dev * top_count * 9 // (8 * experts)
    query_end = HEADS * HD
    qkv = (HEADS + 2 * KVH) * HD
    shard = attend_master.shape[0]

    attend_own = jnp.concatenate(
        [pair_heads(attend_master[:, :query_end], 1), attend_master[:, query_end:]], axis=1
    )
    rest = LANES - experts - 2
    first_own = jnp.concatenate(
        [attend_own, router_master, gains_master.T, jnp.zeros((shard, rest), F32)], axis=1
    ).astype(BF16)
    half = local_experts // 2
    packed = [
        pack_experts(
            expand_master[i : i + half].astype(BF16), shrink_master[i : i + half].astype(BF16)
        )
        for i in (0, half)
    ]
    front = lax.all_gather(packed[0], ("dp", "ctx"), axis=0, tiled=False)
    first_w, outward_w = dense_gather(first_own, pair_heads(outward_master, 0).T.astype(BF16))
    attend_w = first_w[:, :qkv]
    router_w = first_w[:, qkv : qkv + experts]
    gains_f = first_w[:, qkv + experts : qkv + experts + 2].T.astype(F32)

    codes = slot_codes(routes[0, 0], priority[0, 0, 0], experts, capacity)
    known = jnp.concatenate(
        [cotangent[0, 0], codes.astype(BF16), jnp.zeros((rows_dev, LANES - experts), BF16)], axis=1
    )
    known = after(known, first_w)
    known_core = swap_core(known)
    known_far = swap_far(known)
    known_last = swap_core(known_far)
    known_near = jnp.concatenate([known, known_core], axis=0)
    known_far = jnp.concatenate([known_far, known_last], axis=0)
    grad_out_all = jnp.concatenate([known_near[:, :width], known_far[:, :width]], axis=0)

    positions = ctx_place * rows_dev + jnp.arange(rows_dev, dtype=jnp.int32)
    all_positions = jnp.arange(stream_len, dtype=jnp.int32)
    starts = doc_starts[0, 0]
    first_pos = jnp.max(jnp.where(starts[None, :] <= positions[:, None], starts[None, :], 0), axis=1)
    place = jnp.stack([positions, first_pos], axis=0)
    tables = turn_tables(all_positions)
    own_tables = tuple(
        lax.dynamic_slice_in_dim(table, ctx_place * rows_dev, rows_dev, 0) for table in tables
    )
    queries, pairs, first_low = project(local_low, gains_f[0:1], first_w, *own_tables)
    key_pieces = [(pairs[:, : KVH * HD], pairs[:, KVH * HD :])]
    for step in range(ctx_count - 1):
        route = [(i, i + 1) for i in range(step, ctx_count - 1)]
        key_pieces.append(tuple(lax.ppermute(part, "ctx", route) for part in key_pieces[-1]))
    rear = lax.all_gather(after(packed[1], *key_pieces[-1]), ("dp", "ctx"), axis=0, tiled=False)
    state = ()
    for step in range(ctx_count):
        state = attend_forward(
            place, ctx_place - step, queries, key_pieces[step], state, step == ctx_count - 1
        )
        if step == ctx_count - 2:
            *state, known_near, known_far, grad_out_all = lax.optimization_barrier(
                (*state, known_near, known_far, grad_out_all)
            )
    mixed_low, log_total, mixed_turned = state
    branch = lax.dot_general(mixed_low, outward_w, NT, preferred_element_type=F32)
    middle = local_rows + branch
    second_norm, second_unit, second_scale = rms_forward(middle, gains_f[1])
    second_low = second_norm.astype(BF16)

    first_expert = jnp.reshape(exp_place * local_experts, (1,)).astype(jnp.int32)
    second_core = swap_core(second_low)
    second_far = swap_far(second_low)
    second_near = jnp.concatenate([second_low, second_core], axis=0)
    router_block = qkv // LANES

    def group(index, part, second, known, weights, before, kept, *tie):
        first = first_expert + index * half
        return run_experts(
            first, part, 2, second, known, first_w, weights, router_block, before, kept, tie
        )

    contract = (((0,), (0,)), ((), ()))

    def wide_grad_of(grad, *others):
        grad = after(grad, *others)
        wide = lax.dot_general(second_all, grad, contract, preferred_element_type=F32)
        return wide.astype(BF16)

    def thin_grad_of(hidden, *others):
        hidden = after(hidden, *others)
        thin = lax.dot_general(hidden, grad_out_all, contract, preferred_element_type=F32)
        return thin.astype(BF16).reshape(half, FF, width)

    owners = lax.axis_size("dp") * ctx_count

    def owner_rows(wide, thin):
        thin = jnp.swapaxes(thin.reshape(half, owners, FF // owners, width), 0, 1)
        thin = thin.reshape(owners, width // owners, half * FF)
        both = jnp.concatenate([wide.reshape(owners, width // owners, -1), thin], axis=2)
        return both.reshape(width, -1)

    def scatter(both):
        return lax.psum_scatter(both, ("dp", "ctx"), scatter_dimension=0, tiled=True)

    def update_experts(total, first, expand_kept, shrink_kept):
        rows = total.shape[0]
        tiles = 2 if rows % 32 == 0 else 1
        expand = adam_group(
            (expand_master, expand_mean, expand_square),
            total,
            pl.BlockSpec((rows // tiles, 2 * FF), lambda i, j: (j, i)),
            first,
            tiles,
            D ** (-0.5),
            DECAY,
            expand_kept,
        )
        thin = total[:, half * 2 * FF :].reshape(half, FF // owners, width)
        shrink = adam_group(
            (shrink_master, shrink_mean, shrink_square),
            thin,
            pl.BlockSpec((1, FF // owners, width), lambda i, j: (i, j, 0)),
            first,
            1,
            (FF // 32) ** (-0.5),
            DECAY,
            shrink_kept,
        )
        return (expand, shrink)

    *kept, back_near, mix_near = group(0, 0, second_near, known_near, front, (), ())
    second_far = after(second_far, back_near)
    second_last = swap_core(second_far)
    second_far = jnp.concatenate([second_far, second_last], axis=0)
    second_all = jnp.concatenate([second_near, second_far], axis=0)
    hidden, grad, back_far, mix_far = group(0, 1, second_far, known_far, front, (), kept)
    front_grads = (wide_grad_of(grad, back_far), thin_grad_of(hidden, back_far))
    front_rows = owner_rows(*front_grads)
    front_sum = scatter(front_rows)
    *kept, back_far, mix_far = group(
        1, 1, second_far, known_far, rear, (back_far, mix_far), (), front_rows
    )
    across = back_far[:rows_dev].astype(F32) + swap_core(back_far[rows_dev:]).astype(F32)
    across = across.astype(BF16)
    second_near = after(second_near, across)
    across = swap_far(across)
    hidden, grad, back_near, mix_near = group(
        1, 0, second_near, known_near, rear, (back_near, mix_near), kept
    )
    back_near, across = lax.optimization_barrier((back_near, across))
    row_grads = (
        back_near[:rows_dev].astype(F32)
        + swap_core(back_near[rows_dev:]).astype(F32)
        + across.astype(F32)
    )
    grad_gates = (
        row_grads[:, width : width + experts]
        + row_grads[:, width + LANES // 2 : width + LANES // 2 + experts]
    )
    mix_near, mix_far, row_grads = lax.optimization_barrier((mix_near, mix_far, row_grads))
    mix_core = swap_core(mix_near[rows_dev:])
    mixture = mix_far[:rows_dev].astype(F32) + swap_core(mix_far[rows_dev:]).astype(F32)
    mixture = swap_far(mixture.astype(BF16))
    row_grads = row_grads[:, :width]

    logits = jnp.dot(second_low, router_w, preferred_element_type=F32)
    gates = jax.nn.softmax(jnp.where(codes > 0, logits, NEGATIVE), axis=-1)
    gates = jnp.where(codes > 0, gates, 0.0)
    mean_term = jnp.sum(gates * grad_gates, axis=-1, keepdims=True)
    grad_logits = (gates * (grad_gates - mean_term)).astype(BF16)
    router_grad = jnp.einsum("td,te->de", second_low, grad_logits, preferred_element_type=F32)
    grad_second = row_grads + jnp.einsum(
        "te,de->td", grad_logits, router_w, preferred_element_type=F32
    )
    grad_middle_norm, gain_two_grad = rms_backward(
        grad_second, second_unit, second_scale, gains_f[1]
    )
    grad_middle = cotangent[0, 0].astype(F32) + grad_middle_norm
    grad_branch = grad_middle.astype(BF16)

    grad_mixed = jnp.dot(grad_branch, outward_w, preferred_element_type=F32).astype(BF16)
    deltas = row_deltas(grad_mixed, mixed_turned)
    grad_query = ()
    got = None
    expand_new, shrink_new = update_experts(front_sum, 0, (), ())
    early = (expand_new[0], shrink_new[0])
    for step in range(1, ctx_count + 1):
        back = ctx_count - step
        *grad_query, grad_pairs = attend_backward(
            place,
            ctx_place - back,
            queries,
            grad_mixed,
            log_total,
            deltas,
            key_pieces[back],
            tables,
            own_tables,
            grad_query,
            back == 0,
            (front_sum,) if step == 3 else early if back == 0 else (),
        )
        key_sum = grad_pairs.astype(F32)
        if step > 1:
            key_sum += got.astype(F32)
        key_sum = key_sum.astype(BF16)
        if back > 0:
            pairs_back = [(i, i - 1) for i in range(back, ctx_count)]
            got = jnp.stack([lax.ppermute(key_sum[i], "ctx", pairs_back) for i in range(2)])
        if step == 1:
            thin = thin_grad_of(hidden, grad_pairs)
        if step == 2:
            wide = wide_grad_of(grad, grad_pairs)
    (grad_query,) = grad_query
    rear_sum = scatter(owner_rows(wide, thin))
    mixture, mix_core = lax.optimization_barrier((mixture, mix_core, key_sum))[:2]
    mixture = mixture.astype(F32) + mix_core.astype(F32) + mix_near[:rows_dev].astype(F32)
    output = (middle + mixture).astype(BF16)
    outward_grad = jnp.einsum("td,tc->dc", grad_branch, mixed_low, preferred_element_type=F32)
    grad_project = jnp.concatenate([grad_query, key_sum[0], key_sum[1]], axis=1)
    attend_grad = jnp.einsum("tc,tp->cp", first_low, grad_project, preferred_element_type=F32)
    grad_first = lax.dot_general(grad_project, attend_w, NT, preferred_element_type=F32)
    first_norm, first_unit, first_scale = rms_forward(local_rows, gains_f[0])
    grad_input_norm, gain_one_grad = rms_backward(grad_first, first_unit, first_scale, gains_f[0])
    input_grad = grad_middle + grad_input_norm
    thin_grad = jnp.concatenate(
        [
            router_grad.astype(BF16),
            jnp.stack([gain_one_grad, gain_two_grad], axis=1).astype(BF16),
            jnp.zeros((width, rest), BF16),
        ],
        axis=1,
    )
    first_sum = dense_sum(attend_grad.astype(BF16), thin_grad, outward_grad.astype(BF16))
    rear_sum, first_sum = lax.optimization_barrier((rear_sum, first_sum))
    expand_new, shrink_new = update_experts(rear_sum, half, expand_new, shrink_new)
    rates = ((D ** (-0.5), DECAY), (4.0 * D ** (-0.5), DECAY), (0.5 * D ** (-0.5), DECAY), (0.6, 0.0))
    if split_devices():
        attend_new, outward_new, router_new, gains_new = dense_adam(
            first_sum,
            (
                (attend_master, attend_mean, attend_square),
                (outward_master.T, outward_mean.T, outward_square.T),
                (router_master, router_mean, router_square),
                (gains_master, gains_mean, gains_square),
            ),
            rates,
        )
        outward_new = [new.T for new in outward_new]
    else:
        outward_sum = first_sum[:, qkv + LANES :]
        attend_sum = jnp.concatenate(
            [unpair_heads(first_sum[:, :query_end], 1), first_sum[:, query_end:qkv]], axis=1
        )
        router_sum = first_sum[:, qkv : qkv + experts]
        gains_sum = first_sum[:, qkv + experts : qkv + experts + 2].T
        outward_sum = unpair_heads(outward_sum.T, 0)
        attend_new = adam_update(
            attend_master, attend_mean, attend_square, attend_sum, D ** (-0.5), DECAY
        )
        outward_new = adam_update(
            outward_master, outward_mean, outward_square, outward_sum, 4.0 * D ** (-0.5), DECAY
        )
        router_new = adam_update(
            router_master, router_mean, router_square, router_sum, 0.5 * D ** (-0.5), DECAY
        )
        gains_new = adam_update(gains_master, gains_mean, gains_square, gains_sum, 0.6, 0.0)
    return (
        output[None, None],
        input_grad[None, None],
        attend_new[0],
        attend_new[1],
        attend_new[2],
        attend_new[3],
        outward_new[0],
        outward_new[1],
        outward_new[2],
        outward_new[3],
        router_new[0],
        router_new[1],
        router_new[2],
        router_new[3],
        gains_new[0],
        gains_new[1],
        gains_new[2],
        gains_new[3],
        expand_new[0],
        expand_new[1],
        expand_new[2],
        expand_new[3],
        shrink_new[0],
        shrink_new[1],
        shrink_new[2],
        shrink_new[3],
    )


def solution(mesh):
    in_specs = (
        P("dp", "exp", "ctx", None),
        P("dp", "exp", "ctx", None),
        P("dp", "exp", None),
        P("dp", "exp", "ctx", None),
        P("dp", "exp", "ctx", None),
        P(("dp", "ctx", "exp"), None),
        P(("dp", "ctx", "exp"), None),
        P(("dp", "ctx", "exp"), None),
        P(None, ("dp", "ctx", "exp")),
        P(None, ("dp", "ctx", "exp")),
        P(None, ("dp", "ctx", "exp")),
        P(("dp", "ctx", "exp"), None),
        P(("dp", "ctx", "exp"), None),
        P(("dp", "ctx", "exp"), None),
        P(None, ("dp", "ctx", "exp")),
        P(None, ("dp", "ctx", "exp")),
        P(None, ("dp", "ctx", "exp")),
        P("exp", ("dp", "ctx"), None),
        P("exp", ("dp", "ctx"), None),
        P("exp", ("dp", "ctx"), None),
        P("exp", ("dp", "ctx"), None),
        P("exp", ("dp", "ctx"), None),
        P("exp", ("dp", "ctx"), None),
    )
    out_specs = (
        P("dp", "exp", "ctx", None),
        P("dp", "exp", "ctx", None),
        P(("dp", "ctx", "exp"), None),
        P(("dp", "ctx", "exp"), None),
        P(("dp", "ctx", "exp"), None),
        P(("dp", "ctx", "exp"), None),
        P(None, ("dp", "ctx", "exp")),
        P(None, ("dp", "ctx", "exp")),
        P(None, ("dp", "ctx", "exp")),
        P(None, ("dp", "ctx", "exp")),
        P(("dp", "ctx", "exp"), None),
        P(("dp", "ctx", "exp"), None),
        P(("dp", "ctx", "exp"), None),
        P(("dp", "ctx", "exp"), None),
        P(None, ("dp", "ctx", "exp")),
        P(None, ("dp", "ctx", "exp")),
        P(None, ("dp", "ctx", "exp")),
        P(None, ("dp", "ctx", "exp")),
        P("exp", ("dp", "ctx"), None),
        P("exp", ("dp", "ctx"), None),
        P("exp", ("dp", "ctx"), None),
        P("exp", ("dp", "ctx"), None),
        P("exp", ("dp", "ctx"), None),
        P("exp", ("dp", "ctx"), None),
        P("exp", ("dp", "ctx"), None),
        P("exp", ("dp", "ctx"), None),
    )
    return jax.shard_map(body, mesh=mesh, in_specs=in_specs, out_specs=out_specs, check_vma=False)
```

```python
import functools
import math

import jax
import jax.numpy as jnp
from jax import lax
from jax.experimental import pallas as pl
from jax.experimental.pallas import tpu as pltpu
from jax.sharding import PartitionSpec as P

D = 1536
HEADS = 24
KVH = 8
HD = 64
FF = 512
STEP = 10
GROUP = HEADS // KVH
PAIRS = KVH // 2
LANES = 2 * HD
SCALE = HD**-0.5


EPSILON = 1e-05
THETA = 10000.0
BETA_ONE = 0.9
BETA_TWO = 0.95
ADAM_EPSILON = 1e-08
DECAY = 0.1
NEGATIVE = -1e30
BF16 = jnp.bfloat16
F32 = jnp.float32
NT = (((1,), (1,)), ((), ()))


def rms_forward(values, gain_vec):
    scale_row = lax.rsqrt(jnp.mean(values * values, axis=-1, keepdims=True) + EPSILON)
    unit_rows = values * scale_row
    return (unit_rows * gain_vec, unit_rows, scale_row)


def rms_backward(grad_rows, unit_rows, scale_row, gain_vec):
    inner = grad_rows * gain_vec
    grad_values = scale_row * (
        inner - unit_rows * jnp.mean(inner * unit_rows, axis=-1, keepdims=True)
    )
    return (grad_values, jnp.sum(grad_rows * unit_rows, axis=0))


def adam_update(master, first_mom, second_mom, grad, rate, decay):
    first_new = BETA_ONE * first_mom + (1.0 - BETA_ONE) * grad
    second_new = BETA_TWO * second_mom + (1.0 - BETA_TWO) * grad * grad
    first_hat = first_new / (1.0 - BETA_ONE**STEP)
    second_hat = second_new / (1.0 - BETA_TWO**STEP)
    master_new = master - rate * (
        first_hat / (jnp.sqrt(second_hat) + ADAM_EPSILON) + decay * master
    )
    return (first_new, second_new, master_new, master_new.astype(jnp.bfloat16))


def adam_kernel(rate, decay, master_ref, mean_ref, square_ref, grad_ref, *refs):
    outs = refs[len(refs) - 4 :]
    grad = grad_ref[...].reshape(master_ref.shape).astype(F32)
    news = adam_update(master_ref[...], mean_ref[...], square_ref[...], grad, rate, decay)
    for out, new in zip(outs, news):
        out[...] = new


def dense_adam_kernel(experts, rates, sum_ref, *refs):
    groups = [refs[3 * i : 3 * i + 3] for i in range(4)]
    results = [refs[12 + 4 * i : 16 + 4 * i] for i in range(4)]
    rows = sum_ref.shape[0]
    lane = lax.broadcasted_iota(jnp.int32, (rows, LANES), 1)
    qkv = (HEADS + 2 * KVH) * HD

    def update(index, cut, grad):
        rate, decay = rates[index]
        news = adam_update(*(ref[cut] for ref in groups[index]), grad, rate, decay)
        for out, new in zip(results[index], news):
            out[cut] = new

    def columns(start):
        return (slice(None), slice(start, start + LANES))

    def place(head):
        group, member = head // GROUP, head % GROUP
        return (GROUP * (group // 2) + member, group % 2)

    for index, begin in ((0, 0), (1, qkv + LANES)):
        for pair in range(HEADS // 2):
            parts = []
            for side in range(2):
                spot, part = place(2 * pair + side)
                block = sum_ref[columns(begin + spot * LANES)]
                parts.append(block if part == side else pltpu.roll(block, HD, 1))
            update(index, columns(pair * LANES), jnp.where(lane < HD, parts[0], parts[1]))
    for start in range(HEADS * HD, qkv, LANES):
        update(0, columns(start), sum_ref[columns(start)])
    thin = sum_ref[columns(qkv)]
    whole = (slice(None), slice(None))
    update(2, whole, thin[:, :experts])
    update(3, whole, thin.T[experts : experts + 2])


def dense_adam(total, arrays, rates):
    shapes = []
    for master, _, _ in arrays:
        shapes += [jax.ShapeDtypeStruct(master.shape, F32)] * 3
        shapes.append(jax.ShapeDtypeStruct(master.shape, BF16))
    outs = pl.pallas_call(
        functools.partial(dense_adam_kernel, arrays[2][0].shape[1], rates),
        in_specs=[pl.BlockSpec(memory_space=pltpu.VMEM)] * 13,
        out_specs=[pl.BlockSpec(memory_space=pltpu.VMEM)] * 16,
        out_shape=shapes,
        compiler_params=pltpu.CompilerParams(vmem_limit_bytes=48 * 1024 * 1024),
        cost_estimate=pl.CostEstimate(
            flops=20 * total.size, bytes_accessed=40 * total.size, transcendentals=0
        ),
    )(total, *(array for group in arrays for array in group))
    return [outs[4 * i : 4 * i + 4] for i in range(4)]


def adam_group(arrays, grad, grad_spec, first, tiles, rate, decay, kept):
    shape = arrays[0].shape
    rows = shape[1] // tiles
    own = pl.BlockSpec((1, rows, shape[2]), lambda i, j: (first + i, j, 0))
    count = shape[0] // 2
    whole = [pl.BlockSpec(memory_space=pl.ANY)] * len(kept)
    return pl.pallas_call(
        functools.partial(adam_kernel, rate, decay),
        grid=(count, tiles),
        in_specs=[own, own, own, grad_spec, *whole],
        out_specs=[own] * 4,
        out_shape=[jax.ShapeDtypeStruct(shape, F32)] * 3 + [jax.ShapeDtypeStruct(shape, BF16)],
        input_output_aliases={4 + i: i for i in range(len(kept))},
        compiler_params=pltpu.CompilerParams(vmem_limit_bytes=40 * 1024 * 1024),
        cost_estimate=pl.CostEstimate(
            flops=10 * arrays[0].size, bytes_accessed=14 * arrays[0].size, transcendentals=0
        ),
    )(*arrays, grad, *kept)


def pair_heads(block, axis):
    shape = block.shape
    split = shape[:axis] + (PAIRS, 2, GROUP, HD) + shape[axis + 1 :]
    return jnp.swapaxes(block.reshape(split), axis + 1, axis + 2).reshape(shape)


def unpair_heads(block, axis):
    shape = block.shape
    split = shape[:axis] + (PAIRS, GROUP, 2, HD) + shape[axis + 1 :]
    return jnp.swapaxes(block.reshape(split), axis + 1, axis + 2).reshape(shape)


def turn_tables(positions):
    half = HD // 2
    frequency = THETA ** (-jnp.arange(half, dtype=F32) / half)
    angles = positions.astype(F32)[:, None] * frequency[None, :]
    cosine = jnp.cos(angles)
    sine = jnp.sin(angles)
    return (
        jnp.concatenate([cosine] * 4, axis=1),
        jnp.concatenate([-sine, sine, -sine, sine], axis=1),
    )


def swap_halves(block):
    half = HD // 2
    lane = lax.broadcasted_iota(jnp.int32, block.shape, 1)
    ahead = pltpu.roll(block, LANES - half, 1)
    behind = pltpu.roll(block, half, 1)
    return jnp.where(lane % HD < half, ahead, behind)


def project_kernel(x_ref, gain_ref, w_ref, cos_ref, sin_ref, q_ref, kv_ref, h_ref):
    step = pl.program_id(0)
    query_tiles = HEADS * HD // 256
    key_tiles = KVH * HD // 256

    @pl.when(step == 0)
    def _():
        rows = x_ref[...].astype(F32)
        scale_row = lax.rsqrt(jnp.mean(rows * rows, axis=-1, keepdims=True) + EPSILON)
        h_ref[...] = (rows * scale_row * gain_ref[...]).astype(BF16)

    acc = jnp.dot(h_ref[...], w_ref[...], preferred_element_type=F32)

    def turned(half):
        part = acc[:, half * LANES : (half + 1) * LANES]
        return part * cos_ref[...] + swap_halves(part) * sin_ref[...]

    @pl.when(step < query_tiles)
    def _():
        for half in range(2):
            q_ref[:, half * LANES : (half + 1) * LANES] = (turned(half) * SCALE).astype(BF16)

    @pl.when((step >= query_tiles) & (step < query_tiles + key_tiles))
    def _():
        for half in range(2):
            kv_ref[:, half * LANES : (half + 1) * LANES] = turned(half).astype(BF16)

    @pl.when(step >= query_tiles + key_tiles)
    def _():
        kv_ref[...] = acc.astype(BF16)


def project(x, gain, weights, cosine, sine):
    rows = x.shape[0]
    query_tiles = HEADS * HD // 256
    tiles = (HEADS + 2 * KVH) * HD // 256
    return pl.pallas_call(
        project_kernel,
        grid=(tiles,),
        in_specs=[
            pl.BlockSpec((rows, D), lambda j: (0, 0)),
            pl.BlockSpec((1, D), lambda j: (0, 0)),
            pl.BlockSpec((D, 256), lambda j: (0, j)),
            pl.BlockSpec((rows, LANES), lambda j: (0, 0)),
            pl.BlockSpec((rows, LANES), lambda j: (0, 0)),
        ],
        out_specs=[
            pl.BlockSpec((rows, 256), lambda j: (0, jnp.minimum(j, query_tiles - 1))),
            pl.BlockSpec((rows, 256), lambda j: (0, jnp.maximum(j - query_tiles, 0))),
            pl.BlockSpec((rows, D), lambda j: (0, 0)),
        ],
        out_shape=[
            jax.ShapeDtypeStruct((rows, HEADS * HD), BF16),
            jax.ShapeDtypeStruct((rows, 2 * KVH * HD), BF16),
            jax.ShapeDtypeStruct((rows, D), BF16),
        ],
        compiler_params=pltpu.CompilerParams(vmem_limit_bytes=40 * 1024 * 1024),
        cost_estimate=pl.CostEstimate(
            flops=2 * rows * D * tiles * 256, bytes_accessed=D * tiles * 512, transcendentals=0
        ),
    )(x, gain, weights, cosine, sine)


def masked_pair(block):
    lane = lax.broadcasted_iota(jnp.int32, block.shape, 1)
    zero = jnp.zeros_like(block)
    return jnp.concatenate(
        [jnp.where(lane < HD, block, zero), jnp.where(lane >= HD, block, zero)], axis=0
    )


def chunk_flags(place, owner, sub_rows):
    rows = place.shape[1]
    start = owner * rows
    end = start + rows - 1
    first = place[:, ::sub_rows]
    last = place[:, sub_rows - 1 :: sub_rows]
    seen = (owner >= 0) & (start <= last[0]) & (end >= first[1])
    whole = (last[1] <= start) & (end <= first[0])
    return jnp.where(seen, jnp.where(whole, 2, 1), 0).astype(jnp.int32)


def allowed_keys(owner, key_rows, columns, place_ref):
    key_pos = owner * key_rows + lax.broadcasted_iota(jnp.int32, (key_rows, columns), 0)
    query_pos = jnp.concatenate([place_ref[0:1, :]] * 2, axis=1)
    first_pos = jnp.concatenate([place_ref[1:2, :]] * 2, axis=1)
    return (key_pos <= query_pos) & (key_pos >= first_pos)


def halves(index, rows):
    return slice(index * rows, (index + 1) * rows)


def attend_kernel(first, final, flag_ref, owner_ref, place_ref, q_ref, k_ref, v_ref, *refs):
    sub = pl.program_id(1)
    rows = q_ref.shape[0]
    key_rows = k_ref.shape[0]
    columns = 2 * rows
    if first:
        before = None
    else:
        before, refs = refs[:3], refs[3:]
    outs, (top, total, acc) = refs[:3], refs[3:]
    for r in range(GROUP):
        if first:
            top[r] = jnp.full((1, columns), NEGATIVE, F32)
            total[r] = jnp.zeros((1, columns), F32)
            acc[r] = jnp.zeros((LANES, columns), F32)
        else:
            acc[r] = jnp.zeros((LANES, columns), F32)
            for i in range(2):
                cols = halves(i, rows)
                head = slice(2 * r + i, 2 * r + i + 1)
                top[r, :, cols] = before[0][0, head, :]
                total[r, :, cols] = before[1][0, head, :]
                acc[r, halves(i, HD), cols] = before[2][0, r, halves(i, HD), :]

    def update(masked):
        keys = k_ref[...]
        turned = v_ref[...].astype(F32).T.astype(BF16)
        if masked:
            allowed = allowed_keys(owner_ref[0], key_rows, columns, place_ref)
        for r in range(GROUP):
            queries = masked_pair(q_ref[:, r * LANES : (r + 1) * LANES])
            scores = lax.dot_general(keys, queries, NT, preferred_element_type=F32)
            if masked:
                scores = jnp.where(allowed, scores, NEGATIVE)
            old = top[r]
            now = jnp.maximum(old, jnp.max(scores, axis=0, keepdims=True))
            shrinking = jnp.exp(old - now)
            terms = jnp.exp(scores - now)
            top[r] = now
            total[r] = total[r] * shrinking + jnp.sum(terms, axis=0, keepdims=True)
            acc[r] = acc[r] * shrinking + jnp.dot(
                turned, terms.astype(BF16), preferred_element_type=F32
            )

    @pl.when(flag_ref[sub] == 1)
    def _():
        update(True)

    @pl.when(flag_ref[sub] == 2)
    def _():
        update(False)

    for r in range(GROUP):
        mixed = acc[r] / total[r] if final else acc[r]
        both = jnp.concatenate([mixed[:HD, :rows], mixed[HD:, rows:]], axis=0)
        if final:
            lse = top[r] + jnp.log(total[r])
        for i in range(2):
            head = slice(2 * r + i, 2 * r + i + 1)
            if final:
                outs[1][0, head, :] = lse[:, halves(i, rows)]
            else:
                outs[0][0, head, :] = top[r, :, halves(i, rows)]
                outs[1][0, head, :] = total[r, :, halves(i, rows)]
        outs[2][0, r] = both
        if final:
            outs[0][:, r * LANES : (r + 1) * LANES] = both.T.astype(BF16)


def head_specs(rows, sub_rows):
    line = pl.BlockSpec((1, 2 * GROUP, sub_rows), lambda p, s, *_: (p, 0, s))
    turned = pl.BlockSpec((1, GROUP, LANES, sub_rows), lambda p, s, *_: (p, 0, 0, s))
    wide = pl.BlockSpec((sub_rows, GROUP * LANES), lambda p, s, *_: (s, p))
    line_shape = jax.ShapeDtypeStruct((PAIRS, 2 * GROUP, rows), F32)
    turned_shape = jax.ShapeDtypeStruct((PAIRS, GROUP, LANES, rows), F32)
    wide_shape = jax.ShapeDtypeStruct((rows, HEADS * HD), BF16)
    return (line, turned, wide, line_shape, turned_shape, wide_shape)


def attend_forward(place, owner, q, piece, before, final):
    rows = q.shape[0]
    sub_rows = min(256, rows)
    columns = 2 * sub_rows
    line, turned, wide, line_shape, turned_shape, wide_shape = head_specs(rows, sub_rows)
    return pl.pallas_call(
        functools.partial(attend_kernel, not before, final),
        grid_spec=pltpu.PrefetchScalarGridSpec(
            num_scalar_prefetch=2,
            grid=(PAIRS, rows // sub_rows),
            in_specs=[
                pl.BlockSpec((2, sub_rows), lambda p, s, *_: (0, s)),
                wide,
                pl.BlockSpec((rows, LANES), lambda p, s, *_: (0, p)),
                pl.BlockSpec((rows, LANES), lambda p, s, *_: (0, p)),
                *([line, line, turned] if before else []),
            ],
            out_specs=[wide, line, turned] if final else [line, line, turned],
            scratch_shapes=[
                pltpu.VMEM((GROUP, 1, columns), F32),
                pltpu.VMEM((GROUP, 1, columns), F32),
                pltpu.VMEM((GROUP, LANES, columns), F32),
            ],
        ),
        out_shape=[wide_shape if final else line_shape, line_shape, turned_shape],
        compiler_params=pltpu.CompilerParams(vmem_limit_bytes=40 * 1024 * 1024),
        cost_estimate=pl.CostEstimate(
            flops=40 * rows * rows * D, bytes_accessed=8 * rows * D, transcendentals=0
        ),
    )(chunk_flags(place, owner, sub_rows), owner[None], place, q, *piece, *before)


def delta_kernel(do_ref, ot_ref, delta_ref):
    for r in range(GROUP):
        product = do_ref[:, r * LANES : (r + 1) * LANES].astype(F32).T * ot_ref[0, r]
        for i in range(2):
            delta_ref[0, 2 * r + i : 2 * r + i + 1, :] = jnp.sum(
                product[halves(i, HD)], axis=0, keepdims=True
            )


def row_deltas(do, ot):
    rows = do.shape[0]
    line, turned, wide, line_shape, _, _ = head_specs(rows, rows)
    return pl.pallas_call(
        delta_kernel,
        grid=(PAIRS, 1),
        in_specs=[wide, turned],
        out_specs=line,
        out_shape=line_shape,
        cost_estimate=pl.CostEstimate(
            flops=2 * rows * D, bytes_accessed=6 * rows * D, transcendentals=0
        ),
    )(do, ot)


def attend_back_kernel(
    first,
    final,
    flag_ref,
    owner_ref,
    place_ref,
    q_ref,
    do_ref,
    lse_ref,
    delta_ref,
    k_ref,
    v_ref,
    cos_ref,
    sin_ref,
    own_cos_ref,
    own_sin_ref,
    *refs,
):
    sub = pl.program_id(1)
    rows = q_ref.shape[0]
    key_rows = k_ref.shape[0]
    columns = 2 * rows
    if not first:
        before = refs[0]
    grad_ref, pair_ref, acc, dk, dv = refs[len(refs) - 5 :]

    @pl.when(sub == 0)
    def _():
        dk[...] = jnp.zeros(dk.shape, F32)
        dv[...] = jnp.zeros(dv.shape, F32)

    acc[...] = jnp.zeros(acc.shape, F32)
    if not first:
        for r in range(GROUP):
            for i in range(2):
                acc[r, halves(i, HD), halves(i, rows)] = before[0, r, halves(i, HD), :]

    def update(masked):
        keys = k_ref[...]
        values = v_ref[...]
        turned = keys.astype(F32).T.astype(BF16)
        key_grad = dk[...]
        value_grad = dv[...]
        if masked:
            allowed = allowed_keys(owner_ref[0], key_rows, columns, place_ref)
        for r in range(GROUP):
            lanes = slice(r * LANES, (r + 1) * LANES)
            queries = masked_pair(q_ref[:, lanes])
            grads = masked_pair(do_ref[:, lanes])
            heads = [slice(2 * r + i, 2 * r + i + 1) for i in range(2)]
            lse = jnp.concatenate([lse_ref[0, head, :] for head in heads], axis=1)
            delta = jnp.concatenate([delta_ref[0, head, :] for head in heads], axis=1)
            scores = lax.dot_general(keys, queries, NT, preferred_element_type=F32)
            probs = jnp.exp(scores - lse)
            if masked:
                probs = jnp.where(allowed, probs, 0.0)
            value_grad += jnp.dot(probs.astype(BF16), grads, preferred_element_type=F32)
            prob_grad = lax.dot_general(values, grads, NT, preferred_element_type=F32)
            score_grad = (probs * (prob_grad - delta)).astype(BF16)
            key_grad += jnp.dot(score_grad, queries, preferred_element_type=F32)
            acc[r] += jnp.dot(turned, score_grad, preferred_element_type=F32)
        dk[...] = key_grad
        dv[...] = value_grad

    @pl.when(flag_ref[sub] == 1)
    def _():
        update(True)

    @pl.when(flag_ref[sub] == 2)
    def _():
        update(False)

    for r in range(GROUP):
        both = jnp.concatenate([acc[r, :HD, :rows], acc[r, HD:, rows:]], axis=0)
        if final:
            grad = both.T * SCALE
            grad = grad * own_cos_ref[...] - swap_halves(grad) * own_sin_ref[...]
            grad_ref[:, r * LANES : (r + 1) * LANES] = grad.astype(BF16)
        else:
            grad_ref[0, r] = both

    @pl.when(sub == pl.num_programs(1) - 1)
    def _():
        pair_ref[0] = (dk[...] * cos_ref[...] - swap_halves(dk[...]) * sin_ref[...]).astype(BF16)
        pair_ref[1] = dv[...].astype(BF16)


def attend_backward(
    place, owner, q, do, lse, delta, piece, tables, own_tables, before, final, tie
):
    rows = q.shape[0]
    sub_rows = min(256, rows)
    columns = 2 * sub_rows
    line, turned, wide, _, turned_shape, wide_shape = head_specs(rows, sub_rows)
    far = pl.BlockSpec((rows, LANES), lambda p, s, flags, own: (jnp.maximum(own[0], 0), 0))
    near = pl.BlockSpec((sub_rows, LANES), lambda p, s, *_: (s, 0))
    return pl.pallas_call(
        functools.partial(attend_back_kernel, not before, final),
        grid_spec=pltpu.PrefetchScalarGridSpec(
            num_scalar_prefetch=2,
            grid=(PAIRS, rows // sub_rows),
            in_specs=[
                pl.BlockSpec((2, sub_rows), lambda p, s, *_: (0, s)),
                wide,
                wide,
                line,
                line,
                pl.BlockSpec((rows, LANES), lambda p, s, *_: (0, p)),
                pl.BlockSpec((rows, LANES), lambda p, s, *_: (0, p)),
                far,
                far,
                near,
                near,
                *([turned] if before else []),
                *([pl.BlockSpec(memory_space=pl.ANY)] * len(tie)),
            ],
            out_specs=[
                wide if final else turned,
                pl.BlockSpec((2, rows, LANES), lambda p, s, *_: (0, 0, p)),
            ],
            scratch_shapes=[
                pltpu.VMEM((GROUP, LANES, columns), F32),
                pltpu.VMEM((rows, LANES), F32),
                pltpu.VMEM((rows, LANES), F32),
            ],
        ),
        out_shape=[
            wide_shape if final else turned_shape,
            jax.ShapeDtypeStruct((2, rows, KVH * HD), BF16),
        ],
        compiler_params=pltpu.CompilerParams(vmem_limit_bytes=40 * 1024 * 1024),
        cost_estimate=pl.CostEstimate(
            flops=60 * rows * rows * D, bytes_accessed=8 * rows * D, transcendentals=0
        ),
    )(
        chunk_flags(place, owner, sub_rows),
        owner[None],
        place,
        q,
        do,
        lse,
        delta,
        *piece,
        *tables,
        *own_tables,
        *before,
        *tie,
    )


def slot_codes(route_ids, priority_row, experts, capacity):
    rows, top_count = route_ids.shape
    ranks = priority_row.reshape(rows, top_count)
    routed = route_ids[:, :, None] == jnp.arange(experts, dtype=jnp.int32)[None, None, :]
    unused = rows * top_count
    rank = jnp.min(jnp.where(routed, ranks[:, :, None], unused), axis=1).T
    earlier = jnp.sum((rank[:, None, :] < rank[:, :, None]).astype(jnp.int32), axis=2)
    return jnp.where(rank < unused, jnp.where(earlier < capacity, 2, 1), 0).T


def pack_experts(expand, shrink):
    parts = [expand[:, :, :FF], expand[:, :, FF:]]
    parts += [shrink[:, :, j * FF : (j + 1) * FF] for j in range(D // FF)]
    return jnp.concatenate(parts, axis=1)


def after(value, *others):
    return lax.optimization_barrier((value, *others))[0]


def split_devices():
    return (lax.axis_size("dp"), lax.axis_size("ctx"), lax.axis_size("exp")) == (2, 4, 4)


def greet(partners):
    barrier = pltpu.get_barrier_semaphore()
    for partner in partners:
        pl.semaphore_signal(
            barrier, inc=1, device_id=partner, device_id_type=pl.DeviceIdType.MESH
        )
    pl.semaphore_wait(barrier, len(partners))


def neighbours():
    x = lax.axis_index("dp")
    z = lax.axis_index("ctx")
    spot = lax.axis_index("exp")
    y = spot // 2
    core = spot % 2
    other_core = {"exp": 2 * y + 1 - core}
    other_x = {"dp": 1 - x}
    other_y = {"exp": 2 * (1 - y) + core}
    along = [{"ctx": lax.rem(z + d, 4)} for d in range(1, 4)]
    return (x, y, z, core, other_core, other_x, other_y, along)


def send_to(source, target, sems, number, device):
    copy = pltpu.make_async_remote_copy(
        src_ref=source,
        dst_ref=target,
        send_sem=sems[0].at[number],
        recv_sem=sems[1].at[number],
        device_id=device,
        device_id_type=pl.DeviceIdType.MESH,
    )
    copy.start()
    return copy


def dense_gather_kernel(first_ref, second_ref, all_first, all_second, local_sem, *sems):
    x, y, z, core, other_core, other_x, other_y, along = neighbours()
    greet([other_core, other_x, other_y] + along)
    spread = [
        (
            send_to(first_ref, all_first.at[x, z, y, core], sems, 2 * d, along[d]),
            send_to(second_ref, all_second.at[x, z, y, core], sems, 2 * d + 1, along[d]),
        )
        for d in range(3)
    ]
    local = [
        pltpu.make_async_copy(first_ref, all_first.at[x, z, y, core], local_sem.at[0]),
        pltpu.make_async_copy(second_ref, all_second.at[x, z, y, core], local_sem.at[1]),
    ]
    for copy in local:
        copy.start()
    steps = [[], [], []]

    def send_near(index):
        if index == 0:
            for copy in local:
                copy.wait()
        else:
            for copy in spread[index - 1]:
                copy.wait_recv()
        spot = lax.rem(z - index + 4, 4)
        base = 6 + 6 * index
        block = all_first.at[x, spot, y, core]
        other = all_second.at[x, spot, y, core]
        steps[0].append(
            (
                send_to(block, block, sems, base, other_y),
                send_to(other, other, sems, base + 1, other_x),
            )
        )

    def send_far(index):
        for copy in steps[0][index]:
            copy.wait_recv()
        spot = lax.rem(z - index + 4, 4)
        base = 6 + 6 * index
        block = all_first.at[x, spot, :, core]
        other = all_second.at[:, spot, y, core]
        steps[1].append(
            (
                send_to(block, block, sems, base + 2, other_x),
                send_to(other, other, sems, base + 3, other_y),
            )
        )

    def send_core(index):
        for copy in steps[1][index]:
            copy.wait_recv()
        spot = lax.rem(z - index + 4, 4)
        base = 6 + 6 * index
        block = all_first.at[:, spot, :, core]
        other = all_second.at[:, spot, :, core]
        steps[2].append(
            (
                send_to(block, block, sems, base + 4, other_core),
                send_to(other, other, sems, base + 5, other_core),
            )
        )

    send_near(0)
    send_far(0)
    send_near(1)
    send_core(0)
    send_far(1)
    send_near(2)
    send_core(1)
    send_far(2)
    send_near(3)
    send_core(2)
    send_far(3)
    send_core(3)
    for pair in steps[2]:
        for copy in pair:
            copy.wait_recv()
    for pair in spread + steps[0] + steps[1] + steps[2]:
        for copy in pair:
            copy.wait_send()


def dense_gather(first, second):
    if not split_devices():
        every = ("dp", "ctx", "exp")
        return tuple(
            lax.all_gather(part, every, axis=0, tiled=True) for part in (first, second)
        )
    shapes = [(2, 4, 2, 2) + part.shape for part in (first, second)]
    gathered = pl.pallas_call(
        dense_gather_kernel,
        in_specs=[pl.BlockSpec(memory_space=pl.ANY)] * 2,
        out_specs=[pl.BlockSpec(memory_space=pl.ANY)] * 2,
        out_shape=[jax.ShapeDtypeStruct(shape, BF16) for shape in shapes],
        scratch_shapes=[
            pltpu.SemaphoreType.DMA((2,)),
            pltpu.SemaphoreType.DMA((30,)),
            pltpu.SemaphoreType.DMA((30,)),
        ],
        compiler_params=pltpu.CompilerParams(collective_id=2, has_side_effects=True),
        cost_estimate=pl.CostEstimate(
            flops=0, bytes_accessed=64 * (first.size + second.size), transcendentals=0
        ),
    )(first, second)
    return tuple(part.reshape(-1, part.shape[-1]) for part in gathered)


def dense_sum_kernel(starts, *refs):
    count = len(starts)
    parts = refs[:count]
    (
        out_ref,
        own,
        got_core,
        got_x,
        got_y,
        late_x,
        late_y,
        got_z,
        load_sem,
        send_sem,
        recv_sem,
    ) = refs[count:]
    x, y, z, core, other_core, other_x, other_y, along = neighbours()
    half = got_x.shape[-1]
    greet([other_core, other_x, other_y] + along)
    sems = (send_sem, recv_sem)
    first = []
    loads = []
    for index in range(count):
        columns = slice(starts[index], starts[index] + parts[index].shape[-1])
        first.append(
            send_to(
                parts[index].at[:, :, :, 1 - core],
                got_core.at[:, :, :, :, columns],
                sems,
                7 + index,
                other_core,
            )
        )
        loads.append(
            pltpu.make_async_copy(
                parts[index].at[:, :, :, core], own.at[:, :, :, :, columns], load_sem.at[index]
            )
        )
    for copy in loads:
        copy.start()
    for copy in loads + first:
        copy.wait()

    def add_core(index, carry):
        i = index // 8
        j = (index // 2) % 4
        k = index % 2
        own[i, j, k] = (own[i, j, k].astype(F32) + got_core[i, j, k].astype(F32)).astype(BF16)
        return carry

    lax.fori_loop(0, 16, add_core, 0)
    by_x = send_to(own.at[1 - x, :, :, :, :half], got_x, sems, 0, other_x)
    by_y = send_to(own.at[:, :, 1 - y, :, half:], got_y, sems, 1, other_y)
    by_x.wait()

    def add_x(index, carry):
        j = index // 2
        k = index % 2
        own[x, j, k, :, :half] = (
            own[x, j, k, :, :half].astype(F32) + got_x[j, k].astype(F32)
        ).astype(BF16)
        return carry

    lax.fori_loop(0, 8, add_x, 0)
    next_y = send_to(own.at[x, :, 1 - y, :, :half], late_y, sems, 2, other_y)
    by_y.wait()

    def add_y(index, carry):
        i = index // 4
        j = index % 4
        own[i, j, y, :, half:] = (
            own[i, j, y, :, half:].astype(F32) + got_y[i, j].astype(F32)
        ).astype(BF16)
        return carry

    lax.fori_loop(0, 8, add_y, 0)
    next_x = send_to(own.at[1 - x, :, y, :, half:], late_x, sems, 3, other_x)
    next_y.wait()
    next_x.wait()

    def add_late(j, carry):
        own[x, j, y, :, :half] = (
            own[x, j, y, :, :half].astype(F32) + late_y[j].astype(F32)
        ).astype(BF16)
        own[x, j, y, :, half:] = (
            own[x, j, y, :, half:].astype(F32) + late_x[j].astype(F32)
        ).astype(BF16)
        return carry

    lax.fori_loop(0, 4, add_late, 0)
    last = [
        send_to(own.at[x, lax.rem(z + d + 1, 4), y], got_z.at[d], sems, 4 + d, along[d])
        for d in range(3)
    ]
    for copy in last:
        copy.wait()
    total = own[x, z, y].astype(F32)
    for d in range(3):
        total += got_z[d].astype(F32)
    out_ref[...] = total


def dense_sum(*parts):
    if not split_devices():
        every = ("dp", "ctx", "exp")
        sums = [lax.psum_scatter(part, every, scatter_dimension=0, tiled=True) for part in parts]
        return jnp.concatenate(sums, axis=1).astype(F32)
    rows = parts[0].shape[0] // 32
    starts = []
    columns = 0
    for part in parts:
        starts.append(columns)
        columns += part.shape[1]
    half = columns // 2 // LANES * LANES
    rest = columns - half
    return pl.pallas_call(
        functools.partial(dense_sum_kernel, tuple(starts)),
        in_specs=[pl.BlockSpec(memory_space=pl.ANY)] * len(parts),
        out_specs=pl.BlockSpec(memory_space=pltpu.VMEM),
        out_shape=jax.ShapeDtypeStruct((rows, columns), F32),
        scratch_shapes=[
            pltpu.VMEM((2, 4, 2, rows, columns), BF16),
            pltpu.VMEM((2, 4, 2, rows, columns), BF16),
            pltpu.VMEM((4, 2, rows, half), BF16),
            pltpu.VMEM((2, 4, rows, rest), BF16),
            pltpu.VMEM((4, rows, rest), BF16),
            pltpu.VMEM((4, rows, half), BF16),
            pltpu.VMEM((3, rows, columns), BF16),
            pltpu.SemaphoreType.DMA((len(parts),)),
            pltpu.SemaphoreType.DMA((7 + len(parts),)),
            pltpu.SemaphoreType.DMA((7 + len(parts),)),
        ],
        compiler_params=pltpu.CompilerParams(
            collective_id=1, has_side_effects=True, vmem_limit_bytes=48 * 1024 * 1024
        ),
        cost_estimate=pl.CostEstimate(
            flops=0, bytes_accessed=64 * 1536 * columns, transcendentals=0
        ),
    )(*[part.reshape(2, 4, 2, 2, rows, part.shape[1]) for part in parts])


def experts_kernel(has_before, first_ref, h_ref, do_ref, code_ref, router_ref, weights, *refs):
    if has_before:
        back_before, tail_before, mix_before = refs[:3]
        refs = refs[3:]
    refs = refs[len(refs) - 7 :]
    gh_ref, dgu_ref, back_ref, mix_ref, table, back_acc, mix_acc = refs
    expert = pl.program_id(0)
    chunk = pl.program_id(1)
    tokens = h_ref.shape[0]
    owners = weights.shape[0]
    rows = D // owners
    thin = FF // owners
    own = pl.ds(pl.multiple_of(chunk * tokens, tokens), tokens)
    lane = lax.broadcasted_iota(jnp.int32, (tokens, LANES), 1)
    codes = code_ref[...].astype(F32)

    @pl.when(expert == 0)
    def _():
        logits = jnp.dot(h_ref[...], router_ref[...], preferred_element_type=F32)
        routed = codes > 0.5
        top = jnp.max(jnp.where(routed, logits, NEGATIVE), axis=1, keepdims=True)
        terms = jnp.where(routed, jnp.exp(jnp.where(routed, logits - top, 0.0)), 0.0)
        shares = terms / jnp.sum(terms, axis=1, keepdims=True)
        table[own, :] = jnp.where(codes > 1.5, shares, 0.0)
        if has_before:
            back_acc[own, :] = back_before[...].astype(F32)
            mix_acc[own, :] = mix_before[...].astype(F32)
        else:
            back_acc[own, :] = jnp.zeros((tokens, D), F32)
            mix_acc[own, :] = jnp.zeros((tokens, D), F32)

    mine = lane == first_ref[0] + expert
    kept = jnp.sum(jnp.where(mine, codes, 0.0), axis=1, keepdims=True) > 1.5
    gate = jnp.sum(jnp.where(mine, table[own, :], 0.0), axis=1, keepdims=True)
    gate_w = weights[:, 0, :rows].reshape(D, FF)
    up_w = weights[:, 0, rows : 2 * rows].reshape(D, FF)
    thirds = [
        weights[:, 0, 2 * rows + j * thin : 2 * rows + (j + 1) * thin].reshape(FF, FF)
        for j in range(D // FF)
    ]
    hidden_rows = h_ref[...]
    gated = jnp.dot(hidden_rows, gate_w, preferred_element_type=F32)
    upper = jnp.dot(hidden_rows, up_w, preferred_element_type=F32)
    grad_hidden = jnp.zeros((tokens, FF), F32)
    for j in range(D // FF):
        grad_hidden += lax.dot_general(
            do_ref[:, j * FF : (j + 1) * FF], thirds[j], NT, preferred_element_type=F32
        )
    sigma = 1.0 / (1.0 + jnp.exp(-gated))
    silu = gated * sigma
    hidden = silu * upper
    gated_hidden = (gate * hidden).astype(BF16)
    grad_gate = jnp.sum(grad_hidden * hidden, axis=1, keepdims=True)
    spot = lane == first_ref[0] + expert + LANES // 2
    table[own, :] += jnp.where(spot, jnp.where(kept, grad_gate, 0.0), 0.0)
    grad_hidden = gate * grad_hidden
    dg = (grad_hidden * upper * (sigma * (1.0 + gated * (1.0 - sigma)))).astype(BF16)
    du = (grad_hidden * silu).astype(BF16)
    gh_ref[...] = gated_hidden
    dgu_ref[:, :FF] = dg
    dgu_ref[:, FF:] = du
    for j in range(D // FF):
        cols = slice(j * FF, (j + 1) * FF)
        mix_acc[own, cols] += jnp.dot(gated_hidden, thirds[j], preferred_element_type=F32)
        back_acc[own, cols] += lax.dot_general(
            dg, gate_w[cols], NT, preferred_element_type=F32
        ) + lax.dot_general(du, up_w[cols], NT, preferred_element_type=F32)

    @pl.when(expert == pl.num_programs(0) - 1)
    def _():
        total = jnp.where(lane < LANES // 2, pltpu.roll(table[own, :], LANES // 2, 1), 0.0)
        coarse = total.astype(BF16)
        fine = total - coarse.astype(F32)
        grad_gates = coarse.astype(F32) + pltpu.roll(fine, LANES // 2, 1)
        if has_before:
            grad_gates += tail_before[...].astype(F32)
        mix_ref[...] = mix_acc[own, :].astype(BF16)
        back_ref[:, :D] = back_acc[own, :].astype(BF16)
        back_ref[:, D:] = grad_gates.astype(BF16)


def run_experts(first, part, parts, second, known, first_w, weights, block, before, kept, tie):
    tokens = second.shape[0]
    chunk = tokens // 2
    owners, experts, depth, _ = weights.shape
    last = experts - 1
    once = pl.Buffered(1)

    def final(e, c, *_):
        return (jnp.where(e == last, c, 0), 0)

    def initial(e, c, *_):
        return (jnp.where(e == 0, c, 1), 0)

    in_specs = [
        pl.BlockSpec((chunk, D), lambda e, c, *_: (c, 0)),
        pl.BlockSpec((chunk, D), lambda e, c, *_: (c, 0)),
        pl.BlockSpec((chunk, LANES), lambda e, c, *_: (c, D // LANES)),
        pl.BlockSpec((D, LANES), lambda e, c, *_: (0, block), pipeline_mode=once),
    ]
    in_specs.append(pl.BlockSpec((owners, 1, depth, FF), lambda e, c, *_: (0, e, 0, 0)))
    operands = [first, second, known, known, first_w, weights]
    if before:
        in_specs += [
            pl.BlockSpec((chunk, D), initial),
            pl.BlockSpec((chunk, LANES), lambda e, c, *_: (c, D // LANES)),
            pl.BlockSpec((chunk, D), initial),
        ]
        operands += [before[0], before[0], before[1]]
    in_specs += [pl.BlockSpec(memory_space=pl.ANY)] * len(tie)
    operands += list(tie)
    aliases = {}
    if kept:
        in_specs += [pl.BlockSpec(memory_space=pl.ANY)] * 2
        aliases = {len(operands): 0, len(operands) + 1: 1}
        operands += list(kept)
    return pl.pallas_call(
        functools.partial(experts_kernel, bool(before)),
        grid_spec=pltpu.PrefetchScalarGridSpec(
            num_scalar_prefetch=1,
            grid=(experts, 2),
            in_specs=in_specs,
            out_specs=[
                pl.BlockSpec((chunk, FF), lambda e, c, *_: (2 * part + c, e)),
                pl.BlockSpec((chunk, 2 * FF), lambda e, c, *_: (2 * part + c, e)),
                pl.BlockSpec((chunk, D + LANES), final),
                pl.BlockSpec((chunk, D), final),
            ],
            scratch_shapes=[
                pltpu.VMEM((tokens, LANES), F32),
                pltpu.VMEM((tokens, D), F32),
                pltpu.VMEM((tokens, D), F32),
            ],
        ),
        out_shape=[
            jax.ShapeDtypeStruct((parts * tokens, experts * FF), BF16),
            jax.ShapeDtypeStruct((parts * tokens, experts * 2 * FF), BF16),
            jax.ShapeDtypeStruct((tokens, D + LANES), BF16),
            jax.ShapeDtypeStruct((tokens, D), BF16),
        ],
        input_output_aliases=aliases,
        compiler_params=pltpu.CompilerParams(vmem_limit_bytes=58 * 1024 * 1024),
        cost_estimate=pl.CostEstimate(
            flops=18 * tokens * D * FF * experts,
            bytes_accessed=tokens * D * 16,
            transcendentals=0,
        ),
    )(*operands)


def swap_core(block):
    return lax.ppermute(block, "exp", [(i, i ^ 1) for i in range(lax.axis_size("exp"))])


def swap_far(block):
    return lax.ppermute(block, "exp", [(i, i ^ 2) for i in range(lax.axis_size("exp"))])


def body(
    tokens,
    cotangent,
    doc_starts,
    routes,
    priority,
    attend_master,
    attend_mean,
    attend_square,
    outward_master,
    outward_mean,
    outward_square,
    router_master,
    router_mean,
    router_square,
    gains_master,
    gains_mean,
    gains_square,
    expand_master,
    expand_mean,
    expand_square,
    shrink_master,
    shrink_mean,
    shrink_square,
):
    local_low = tokens[0, 0]
    local_rows = local_low.astype(F32)
    rows_dev, width = local_rows.shape
    ctx_count = lax.axis_size("ctx")
    ctx_place = lax.axis_index("ctx")
    exp_count = lax.axis_size("exp")
    exp_place = lax.axis_index("exp")
    stream_len = rows_dev * ctx_count
    experts = router_master.shape[1]
    local_experts = experts // exp_count
    top_count = routes.shape[-1]
    capacity = rows_dev * top_count * 9 // (8 * experts)
    query_end = HEADS * HD
    qkv = (HEADS + 2 * KVH) * HD
    shard = attend_master.shape[0]

    attend_own = jnp.concatenate(
        [pair_heads(attend_master[:, :query_end], 1), attend_master[:, query_end:]], axis=1
    )
    rest = LANES - experts - 2
    first_own = jnp.concatenate(
        [attend_own, router_master, gains_master.T, jnp.zeros((shard, rest), F32)], axis=1
    ).astype(BF16)
    half = local_experts // 2
    packed = [
        pack_experts(
            expand_master[i : i + half].astype(BF16), shrink_master[i : i + half].astype(BF16)
        )
        for i in (0, half)
    ]
    front = lax.all_gather(packed[0], ("dp", "ctx"), axis=0, tiled=False)
    first_w, outward_w = dense_gather(first_own, pair_heads(outward_master, 0).T.astype(BF16))
    attend_w = first_w[:, :qkv]
    router_w = first_w[:, qkv : qkv + experts]
    gains_f = first_w[:, qkv + experts : qkv + experts + 2].T.astype(F32)

    codes = slot_codes(routes[0, 0], priority[0, 0, 0], experts, capacity)
    known = jnp.concatenate(
        [cotangent[0, 0], codes.astype(BF16), jnp.zeros((rows_dev, LANES - experts), BF16)], axis=1
    )
    known = after(known, first_w)
    known_core = swap_core(known)
    known_far = swap_far(known)
    known_last = swap_core(known_far)
    known_near = jnp.concatenate([known, known_core], axis=0)
    known_far = jnp.concatenate([known_far, known_last], axis=0)
    grad_out_all = jnp.concatenate([known_near[:, :width], known_far[:, :width]], axis=0)

    positions = ctx_place * rows_dev + jnp.arange(rows_dev, dtype=jnp.int32)
    all_positions = jnp.arange(stream_len, dtype=jnp.int32)
    starts = doc_starts[0, 0]
    first_pos = jnp.max(jnp.where(starts[None, :] <= positions[:, None], starts[None, :], 0), axis=1)
    place = jnp.stack([positions, first_pos], axis=0)
    tables = turn_tables(all_positions)
    own_tables = tuple(
        lax.dynamic_slice_in_dim(table, ctx_place * rows_dev, rows_dev, 0) for table in tables
    )
    queries, pairs, first_low = project(local_low, gains_f[0:1], first_w, *own_tables)
    key_pieces = [(pairs[:, : KVH * HD], pairs[:, KVH * HD :])]
    for step in range(ctx_count - 1):
        route = [(i, i + 1) for i in range(step, ctx_count - 1)]
        key_pieces.append(tuple(lax.ppermute(part, "ctx", route) for part in key_pieces[-1]))
    rear = lax.all_gather(after(packed[1], *key_pieces[-1]), ("dp", "ctx"), axis=0, tiled=False)
    state = ()
    for step in range(ctx_count):
        state = attend_forward(
            place, ctx_place - step, queries, key_pieces[step], state, step == ctx_count - 1
        )
        if step == ctx_count - 2:
            *state, known_near, known_far, grad_out_all = lax.optimization_barrier(
                (*state, known_near, known_far, grad_out_all)
            )
    mixed_low, log_total, mixed_turned = state
    branch = lax.dot_general(mixed_low, outward_w, NT, preferred_element_type=F32)
    middle = local_rows + branch
    second_norm, second_unit, second_scale = rms_forward(middle, gains_f[1])
    second_low = second_norm.astype(BF16)

    first_expert = jnp.reshape(exp_place * local_experts, (1,)).astype(jnp.int32)
    second_core = swap_core(second_low)
    second_far = swap_far(second_low)
    second_near = jnp.concatenate([second_low, second_core], axis=0)
    router_block = qkv // LANES

    def group(index, part, second, known, weights, before, kept, *tie):
        first = first_expert + index * half
        return run_experts(
            first, part, 2, second, known, first_w, weights, router_block, before, kept, tie
        )

    contract = (((0,), (0,)), ((), ()))

    def wide_grad_of(grad, *others):
        grad = after(grad, *others)
        wide = lax.dot_general(second_all, grad, contract, preferred_element_type=F32)
        return wide.astype(BF16)

    def thin_grad_of(hidden, *others):
        hidden = after(hidden, *others)
        thin = lax.dot_general(hidden, grad_out_all, contract, preferred_element_type=F32)
        return thin.astype(BF16).reshape(half, FF, width)

    owners = lax.axis_size("dp") * ctx_count

    def owner_rows(wide, thin):
        thin = jnp.swapaxes(thin.reshape(half, owners, FF // owners, width), 0, 1)
        thin = thin.reshape(owners, width // owners, half * FF)
        both = jnp.concatenate([wide.reshape(owners, width // owners, -1), thin], axis=2)
        return both.reshape(width, -1)

    def scatter(both):
        return lax.psum_scatter(both, ("dp", "ctx"), scatter_dimension=0, tiled=True)

    def update_experts(total, first, expand_kept, shrink_kept):
        rows = total.shape[0]
        tiles = 2 if rows % 32 == 0 else 1
        expand = adam_group(
            (expand_master, expand_mean, expand_square),
            total,
            pl.BlockSpec((rows // tiles, 2 * FF), lambda i, j: (j, i)),
            first,
            tiles,
            D ** (-0.5),
            DECAY,
            expand_kept,
        )
        thin = total[:, half * 2 * FF :].reshape(half, FF // owners, width)
        shrink = adam_group(
            (shrink_master, shrink_mean, shrink_square),
            thin,
            pl.BlockSpec((1, FF // owners, width), lambda i, j: (i, j, 0)),
            first,
            1,
            (FF // 32) ** (-0.5),
            DECAY,
            shrink_kept,
        )
        return (expand, shrink)

    *kept, back_near, mix_near = group(0, 0, second_near, known_near, front, (), ())
    second_far = after(second_far, back_near)
    second_last = swap_core(second_far)
    second_far = jnp.concatenate([second_far, second_last], axis=0)
    second_all = jnp.concatenate([second_near, second_far], axis=0)
    hidden, grad, back_far, mix_far = group(0, 1, second_far, known_far, front, (), kept)
    front_grads = (wide_grad_of(grad, back_far), thin_grad_of(hidden, back_far))
    front_rows = owner_rows(*front_grads)
    front_sum = scatter(front_rows)
    *kept, back_far, mix_far = group(
        1, 1, second_far, known_far, rear, (back_far, mix_far), (), front_rows
    )
    across = back_far[:rows_dev].astype(F32) + swap_core(back_far[rows_dev:]).astype(F32)
    across = across.astype(BF16)
    second_near = after(second_near, across)
    across = swap_far(across)
    hidden, grad, back_near, mix_near = group(
        1, 0, second_near, known_near, rear, (back_near, mix_near), kept
    )
    back_near, across = lax.optimization_barrier((back_near, across))
    row_grads = (
        back_near[:rows_dev].astype(F32)
        + swap_core(back_near[rows_dev:]).astype(F32)
        + across.astype(F32)
    )
    grad_gates = (
        row_grads[:, width : width + experts]
        + row_grads[:, width + LANES // 2 : width + LANES // 2 + experts]
    )
    mix_near, mix_far, row_grads = lax.optimization_barrier((mix_near, mix_far, row_grads))
    mix_core = swap_core(mix_near[rows_dev:])
    mixture = mix_far[:rows_dev].astype(F32) + swap_core(mix_far[rows_dev:]).astype(F32)
    mixture = swap_far(mixture.astype(BF16))
    row_grads = row_grads[:, :width]

    logits = jnp.dot(second_low, router_w, preferred_element_type=F32)
    gates = jax.nn.softmax(jnp.where(codes > 0, logits, NEGATIVE), axis=-1)
    gates = jnp.where(codes > 0, gates, 0.0)
    mean_term = jnp.sum(gates * grad_gates, axis=-1, keepdims=True)
    grad_logits = (gates * (grad_gates - mean_term)).astype(BF16)
    router_grad = jnp.einsum("td,te->de", second_low, grad_logits, preferred_element_type=F32)
    grad_second = row_grads + jnp.einsum(
        "te,de->td", grad_logits, router_w, preferred_element_type=F32
    )
    grad_middle_norm, gain_two_grad = rms_backward(
        grad_second, second_unit, second_scale, gains_f[1]
    )
    grad_middle = cotangent[0, 0].astype(F32) + grad_middle_norm
    grad_branch = grad_middle.astype(BF16)

    grad_mixed = jnp.dot(grad_branch, outward_w, preferred_element_type=F32).astype(BF16)
    deltas = row_deltas(grad_mixed, mixed_turned)
    grad_query = ()
    got = None
    expand_new, shrink_new = update_experts(front_sum, 0, (), ())
    early = (expand_new[0], shrink_new[0])
    for step in range(1, ctx_count + 1):
        back = ctx_count - step
        *grad_query, grad_pairs = attend_backward(
            place,
            ctx_place - back,
            queries,
            grad_mixed,
            log_total,
            deltas,
            key_pieces[back],
            tables,
            own_tables,
            grad_query,
            back == 0,
            hops if step == 2 else (front_sum,) if step == 3 else early if back == 0 else (),
        )
        key_sum = grad_pairs.astype(F32)
        if step > 1:
            key_sum += got.astype(F32)
        key_sum = key_sum.astype(BF16)
        if back > 0:
            pairs_back = [(i, i - 1) for i in range(back, ctx_count)]
            hops = tuple(lax.ppermute(key_sum[i], "ctx", pairs_back) for i in range(2))
            got = jnp.stack(hops)
        if step == 1:
            thin = thin_grad_of(hidden, grad_pairs)
            wide = wide_grad_of(grad, grad_pairs)
    (grad_query,) = grad_query
    rear_sum = scatter(owner_rows(wide, thin))
    mixture, mix_core = lax.optimization_barrier((mixture, mix_core, key_sum))[:2]
    mixture = mixture.astype(F32) + mix_core.astype(F32) + mix_near[:rows_dev].astype(F32)
    output = (middle + mixture).astype(BF16)
    outward_grad = jnp.einsum("td,tc->dc", grad_branch, mixed_low, preferred_element_type=F32)
    grad_project = jnp.concatenate([grad_query, key_sum[0], key_sum[1]], axis=1)
    attend_grad = jnp.einsum("tc,tp->cp", first_low, grad_project, preferred_element_type=F32)
    grad_first = lax.dot_general(grad_project, attend_w, NT, preferred_element_type=F32)
    first_norm, first_unit, first_scale = rms_forward(local_rows, gains_f[0])
    grad_input_norm, gain_one_grad = rms_backward(grad_first, first_unit, first_scale, gains_f[0])
    input_grad = grad_middle + grad_input_norm
    thin_grad = jnp.concatenate(
        [
            router_grad.astype(BF16),
            jnp.stack([gain_one_grad, gain_two_grad], axis=1).astype(BF16),
            jnp.zeros((width, rest), BF16),
        ],
        axis=1,
    )
    first_sum = dense_sum(attend_grad.astype(BF16), thin_grad, outward_grad.astype(BF16))
    rear_sum, first_sum = lax.optimization_barrier((rear_sum, first_sum))
    expand_new, shrink_new = update_experts(rear_sum, half, expand_new, shrink_new)
    rates = ((D ** (-0.5), DECAY), (4.0 * D ** (-0.5), DECAY), (0.5 * D ** (-0.5), DECAY), (0.6, 0.0))
    if split_devices():
        attend_new, outward_new, router_new, gains_new = dense_adam(
            first_sum,
            (
                (attend_master, attend_mean, attend_square),
                (outward_master.T, outward_mean.T, outward_square.T),
                (router_master, router_mean, router_square),
                (gains_master, gains_mean, gains_square),
            ),
            rates,
        )
        outward_new = [new.T for new in outward_new]
    else:
        outward_sum = first_sum[:, qkv + LANES :]
        attend_sum = jnp.concatenate(
            [unpair_heads(first_sum[:, :query_end], 1), first_sum[:, query_end:qkv]], axis=1
        )
        router_sum = first_sum[:, qkv : qkv + experts]
        gains_sum = first_sum[:, qkv + experts : qkv + experts + 2].T
        outward_sum = unpair_heads(outward_sum.T, 0)
        attend_new = adam_update(
            attend_master, attend_mean, attend_square, attend_sum, D ** (-0.5), DECAY
        )
        outward_new = adam_update(
            outward_master, outward_mean, outward_square, outward_sum, 4.0 * D ** (-0.5), DECAY
        )
        router_new = adam_update(
            router_master, router_mean, router_square, router_sum, 0.5 * D ** (-0.5), DECAY
        )
        gains_new = adam_update(gains_master, gains_mean, gains_square, gains_sum, 0.6, 0.0)
    return (
        output[None, None],
        input_grad[None, None],
        attend_new[0],
        attend_new[1],
        attend_new[2],
        attend_new[3],
        outward_new[0],
        outward_new[1],
        outward_new[2],
        outward_new[3],
        router_new[0],
        router_new[1],
        router_new[2],
        router_new[3],
        gains_new[0],
        gains_new[1],
        gains_new[2],
        gains_new[3],
        expand_new[0],
        expand_new[1],
        expand_new[2],
        expand_new[3],
        shrink_new[0],
        shrink_new[1],
        shrink_new[2],
        shrink_new[3],
    )


def solution(mesh):
    in_specs = (
        P("dp", "exp", "ctx", None),
        P("dp", "exp", "ctx", None),
        P("dp", "exp", None),
        P("dp", "exp", "ctx", None),
        P("dp", "exp", "ctx", None),
        P(("dp", "ctx", "exp"), None),
        P(("dp", "ctx", "exp"), None),
        P(("dp", "ctx", "exp"), None),
        P(None, ("dp", "ctx", "exp")),
        P(None, ("dp", "ctx", "exp")),
        P(None, ("dp", "ctx", "exp")),
        P(("dp", "ctx", "exp"), None),
        P(("dp", "ctx", "exp"), None),
        P(("dp", "ctx", "exp"), None),
        P(None, ("dp", "ctx", "exp")),
        P(None, ("dp", "ctx", "exp")),
        P(None, ("dp", "ctx", "exp")),
        P("exp", ("dp", "ctx"), None),
        P("exp", ("dp", "ctx"), None),
        P("exp", ("dp", "ctx"), None),
        P("exp", ("dp", "ctx"), None),
        P("exp", ("dp", "ctx"), None),
        P("exp", ("dp", "ctx"), None),
    )
    out_specs = (
        P("dp", "exp", "ctx", None),
        P("dp", "exp", "ctx", None),
        P(("dp", "ctx", "exp"), None),
        P(("dp", "ctx", "exp"), None),
        P(("dp", "ctx", "exp"), None),
        P(("dp", "ctx", "exp"), None),
        P(None, ("dp", "ctx", "exp")),
        P(None, ("dp", "ctx", "exp")),
        P(None, ("dp", "ctx", "exp")),
        P(None, ("dp", "ctx", "exp")),
        P(("dp", "ctx", "exp"), None),
        P(("dp", "ctx", "exp"), None),
        P(("dp", "ctx", "exp"), None),
        P(("dp", "ctx", "exp"), None),
        P(None, ("dp", "ctx", "exp")),
        P(None, ("dp", "ctx", "exp")),
        P(None, ("dp", "ctx", "exp")),
        P(None, ("dp", "ctx", "exp")),
        P("exp", ("dp", "ctx"), None),
        P("exp", ("dp", "ctx"), None),
        P("exp", ("dp", "ctx"), None),
        P("exp", ("dp", "ctx"), None),
        P("exp", ("dp", "ctx"), None),
        P("exp", ("dp", "ctx"), None),
        P("exp", ("dp", "ctx"), None),
        P("exp", ("dp", "ctx"), None),
    )
    return jax.shard_map(body, mesh=mesh, in_specs=in_specs, out_specs=out_specs, check_vma=False)
```
